256 devices in a mesh: grp: 8 (over z_hi, core), fsdp: 32 (over y, x, z_lo).
Axes of the slice: x: 4, y: 4, z: 8 (z_hi: 4, z_lo: 2; z = z_hi * 2 + z_lo), core: 2. Of those that a mesh axis runs over, the one named last changes fastest.
Arguments:
- queries: bfloat16 [32, 1024, 4096], P('fsdp', 'grp')
- out_grad: bfloat16 [32, 1024, 4096], P('fsdp', 'grp'), may hold values from -6 to 6
- resp_in: bfloat16 [32, 1024, 5120], P('fsdp', 'grp'), may hold values from -6 to 6
- prompt_in: bfloat16 [32, 512, 5120], P('fsdp', 'grp'), may hold values from -6 to 6
- key_matrix: bfloat16 [5120, 512], P('fsdp'), may hold values from -0.078125 to 0.078125
- value_matrix: bfloat16 [5120, 512], P('fsdp'), may hold values from -0.078125 to 0.078125
- key_gain: float32 [128], replicated, may hold values from 0.1 to 1.9
- seg_prompt: int32 [32, 16], P('fsdp', 'grp'), may hold values from 0 to 7, as said below
- seg_start: int32 [32, 16], P('fsdp', 'grp'), may hold values from 0 to 112, as said below
- seg_len: int32 [32, 16], P('fsdp', 'grp'), may hold values from 1 to 112, as said below
- owner: int32 [32, 8], P('fsdp'), may hold values from 0 to 7, as said below
Outputs:
- query_grad: bfloat16 [32, 1024, 4096], P('fsdp', 'grp')
- resp_grad: bfloat16 [32, 1024, 5120], P('fsdp', 'grp')
- prompt_grad: bfloat16 [32, 512, 5120], P('fsdp', 'grp')
- key_weight_grad: bfloat16 [5120, 512], P('fsdp')
- value_weight_grad: bfloat16 [5120, 512], P('fsdp')
The draws below stay inside these ranges and needn't reach their ends.
Inputs may be any that keep to these rules, and one draw needn't show every extreme that they name: `owner`: each row of the grp devices of one group is a permutation of 0 to 7. `seg_prompt`: within one group every prompt is named exactly 2 times. `seg_start`: on each device the starts rise, the first is 0, all are multiples of 16, and each response ends no later than the next one starts (the last one within the device's slots). `seg_len`: each response ends within the 16 slots before the next start (or the device's end).
All inputs are finite; a program needn't handle non-finite values.
Results may differ from the reference program's by a relative error of at most 0.04.
The reference program's roundings to bfloat16 on the way count: a program that leaves them out, or rounds other values in their place, can miss the bound.
Values may be sent and summed in bfloat16 or wider, within the bound.
A program may use at most 128 MiB of HBM per device.

```python
import math
import jax
import jax.numpy as jnp
from jax import lax

MODEL_WIDTH = 5120
QUERY_HEADS = 32
KEY_VALUE_HEADS = 4
HEAD_SIZE = 128
TOK_DEV = 128
PROMPT_DEV = 64
SEGS = 2
BLK = 16
N_GRP = 8
N_FSDP = 32


def segment_blocks(key):
    nblocks = TOK_DEV // BLK

    def one_device(row_key, marked):
        shuffled = jax.random.permutation(row_key, nblocks - 1) + 1
        cut_points = jnp.sort(shuffled[:SEGS - 1].astype(jnp.int32))
        tail_cuts = jnp.arange(nblocks - SEGS + 1, nblocks, dtype=jnp.int32)
        cut_points = jnp.where(marked, tail_cuts, cut_points)
        block_edges = jnp.concatenate([jnp.zeros((1,), jnp.int32), cut_points, jnp.full((1,), nblocks, jnp.int32)])
        blocks = block_edges[1:] - block_edges[:-1]
        tail_sizes = jax.random.randint(jax.random.fold_in(row_key, 1), (SEGS,), 1, BLK + 1).astype(jnp.int32)
        forced = jnp.concatenate([jnp.full((1,), BLK, jnp.int32), tail_sizes[1:SEGS - 1], jnp.ones((1,), jnp.int32)])
        tail_sizes = jnp.where(marked, forced, tail_sizes)
        return (block_edges[:-1] * BLK, (blocks - 1) * BLK + tail_sizes)
    device_keys = jax.random.split(key, N_FSDP * N_GRP)
    marks = jnp.arange(N_FSDP * N_GRP, dtype=jnp.int32) == 0
    seg_begin, seg_size = jax.vmap(one_device)(device_keys, marks)
    return (seg_begin.reshape(N_FSDP, N_GRP * SEGS), seg_size.reshape(N_FSDP, N_GRP * SEGS))


def draw_seg_start(key, part):
    seg_begin, seg_size = segment_blocks(key)
    return seg_begin


def draw_seg_len(key, part):
    seg_begin, seg_size = segment_blocks(key)
    return seg_size


def draw_owner(key, part):
    key = jax.random.fold_in(key, 3)
    group_keys = jax.random.split(key, N_FSDP)
    return jax.vmap(lambda one_key: jax.random.permutation(one_key, N_GRP).astype(jnp.int32))(group_keys)


def draw_seg_prompt(key, part):
    key = jax.random.fold_in(key, 5)
    repeated = jnp.repeat(jnp.arange(N_GRP, dtype=jnp.int32), SEGS)
    group_keys = jax.random.split(key, N_FSDP)
    return jax.vmap(lambda one_key: jax.random.permutation(one_key, repeated))(group_keys)


def draw_queries(key, part):
    key = jax.random.fold_in(key, 7)
    shape = (N_FSDP, N_GRP * TOK_DEV, QUERY_HEADS * HEAD_SIZE)
    value_tensor = jax.random.normal(key, shape, jnp.float32)
    return value_tensor.astype(jnp.bfloat16)


def block_levels(own_key, extent, cuts, low, top_value):
    def one(dim, parts):
        heights = jax.random.uniform(jax.random.fold_in(jax.random.fold_in(own_key, 6), dim), (parts,), jnp.float32, low / len(cuts), top_value / len(cuts))
        return jnp.repeat(jnp.exp(heights), extent[dim] // parts).reshape((-1,) + (1,) * (len(extent) - dim - 1))

    level = one(*cuts[0])
    for cut in cuts[1:]:
        level = level * one(*cut)
    return level


def gaussian(rng, dims, spread, bound, pieces=(), kind=jnp.bfloat16):
    entries = spread * jax.random.normal(rng, dims, jnp.float32)
    if pieces:
        entries = entries * block_levels(rng, dims, pieces, -0.22, 0.18)
    return jnp.clip(entries, -bound, bound).astype(kind)


def setup_inputs(seed: int = 0) -> dict:
    key_of = jax.random.split(jax.random.key(seed), 12)
    queries = draw_queries(jax.random.fold_in(key_of[11], 71), 0)
    out_grad = gaussian(key_of[1], (N_FSDP, N_GRP * TOK_DEV, QUERY_HEADS * HEAD_SIZE), 1.0, 6.0, ((0, 32), (1, 8)))
    resp_in = gaussian(key_of[2], (N_FSDP, N_GRP * TOK_DEV, MODEL_WIDTH), 1.0, 6.0, ((0, 32), (1, 8)))
    prompt_in = gaussian(key_of[3], (N_FSDP, N_GRP * PROMPT_DEV, MODEL_WIDTH), 1.0, 6.0, ((0, 32), (1, 8)))
    key_matrix = gaussian(key_of[4], (MODEL_WIDTH, KEY_VALUE_HEADS * HEAD_SIZE), MODEL_WIDTH ** -0.5, 0.078125, ((0, 32),))
    value_matrix = gaussian(key_of[5], (MODEL_WIDTH, KEY_VALUE_HEADS * HEAD_SIZE), MODEL_WIDTH ** -0.5, 0.078125, ((0, 32),))
    key_gain = jnp.clip(1.0 + 0.18 * jax.random.normal(key_of[6], (HEAD_SIZE,), jnp.float32), 0.1, 1.9)
    seg_prompt = draw_seg_prompt(jax.random.fold_in(key_of[11], 71), 0)
    seg_start = draw_seg_start(jax.random.fold_in(key_of[11], 71), 0)
    seg_len = draw_seg_len(jax.random.fold_in(key_of[11], 71), 0)
    owner = draw_owner(jax.random.fold_in(key_of[11], 71), 0)
    return dict(queries=queries, out_grad=out_grad, resp_in=resp_in, prompt_in=prompt_in, key_matrix=key_matrix, value_matrix=value_matrix, key_gain=key_gain, seg_prompt=seg_prompt, seg_start=seg_start, seg_len=seg_len, owner=owner)


rope_base = 1000000.0

def layout(starts, lengths, count_of_rows):
    index_row = jnp.arange(count_of_rows, dtype=jnp.int32)
    segment = lax.optimization_barrier(jnp.sum((index_row[:, None] >= starts[None, :]).astype(jnp.int32), 1)) - 1
    onehot = segment[:, None] == jnp.arange(starts.shape[0], dtype=jnp.int32)[None, :]
    seg_begin = lax.optimization_barrier(jnp.sum(jnp.where(onehot, starts[None, :], 0), 1))
    seg_size = lax.optimization_barrier(jnp.sum(jnp.where(onehot, lengths[None, :], 0), 1))
    offset = index_row - seg_begin
    return (segment, offset, offset < seg_size)

def norm_rope(raw, gain, positions):
    how_many = raw.shape[0]
    heads = raw.reshape(how_many, -1, HEAD_SIZE)
    square_mean = lax.optimization_barrier(jnp.mean(heads * heads, axis=-1, keepdims=True))
    normed = heads * lax.rsqrt(square_mean + 1e-06) * gain
    half_dim = HEAD_SIZE // 2
    frequency = rope_base ** (-jnp.arange(half_dim, dtype=jnp.float32) / half_dim)
    angles = positions.astype(jnp.float32)[:, None] * frequency[None, :]
    cosine = jnp.cos(angles)[:, None, :]
    sines = jnp.sin(angles)[:, None, :]
    lower_half = normed[..., :half_dim]
    upper_half = normed[..., half_dim:]
    turned = jnp.concatenate([lower_half * cosine - upper_half * sines, upper_half * cosine + lower_half * sines], -1)
    return turned.reshape(how_many, -1)

def attend(queries, key_tensor, value_tensor, allowed):
    count_of_rows = queries.shape[0]
    heads_per_group = QUERY_HEADS // KEY_VALUE_HEADS
    query_head_count = queries.astype(jnp.float32).reshape(count_of_rows, KEY_VALUE_HEADS, heads_per_group, HEAD_SIZE)
    key_head_count = key_tensor.astype(jnp.float32).reshape(-1, KEY_VALUE_HEADS, HEAD_SIZE)
    value_head_count = value_tensor.astype(jnp.float32).reshape(-1, KEY_VALUE_HEADS, HEAD_SIZE)
    scores = jnp.einsum('rkgd,mkd->kgrm', query_head_count, key_head_count) / math.sqrt(HEAD_SIZE)
    scores = jnp.where(allowed[None, None], scores, -1e+30)
    row_max = lax.stop_gradient(lax.optimization_barrier(jnp.max(scores, axis=-1, keepdims=True)))
    weights = jnp.exp(scores - row_max)
    probabilities = (weights / lax.optimization_barrier(jnp.sum(weights, axis=-1, keepdims=True))).astype(jnp.bfloat16)
    attended = jnp.einsum('kgrm,mkd->rkgd', probabilities.astype(jnp.float32), value_head_count)
    return attended.reshape(count_of_rows, QUERY_HEADS * HEAD_SIZE)

def device_attention(my_queries, my_cotangent, own_keys, own_values, segment, offset, usable, slot_rows, prompt_keys_all, prompt_values_all):
    index_row = jnp.arange(TOK_DEV, dtype=jnp.int32)
    resp_ok = (segment[:, None] == segment[None, :]) & (index_row[None, :] <= index_row[:, None]) & usable[None, :]
    slot_of_key = jnp.arange(N_GRP * PROMPT_DEV, dtype=jnp.int32) // PROMPT_DEV
    prompt_ok = slot_rows[:, None] == slot_of_key[None, :]
    allowed = jnp.concatenate([prompt_ok, resp_ok], 1)
    key_tensor = jnp.concatenate([prompt_keys_all, own_keys], 0)
    value_tensor = jnp.concatenate([prompt_values_all, own_values], 0)
    _, backward = jax.vjp(lambda qarg, karg, varg: attend(qarg, karg, varg, allowed), my_queries, key_tensor, value_tensor)
    cotangent = my_cotangent.astype(jnp.float32) * usable[:, None].astype(jnp.float32)
    query_grad, key_grad, value_grad = backward(cotangent)
    split_at = N_GRP * PROMPT_DEV
    return (query_grad, key_grad[:split_at], key_grad[split_at:], value_grad[:split_at], value_grad[split_at:])

def reference(queries, out_grad, resp_in, prompt_in, key_matrix, value_matrix, key_gain, seg_prompt, seg_start, seg_len, owner):
    key_value_width = KEY_VALUE_HEADS * HEAD_SIZE
    both = jnp.concatenate([key_matrix, value_matrix], 1)

    def per_group(total, inputs):
        my_queries, my_cotangent, resp_rows, prompt_rows, prompt_ids, starts, lengths, owners = inputs
        starts = starts.reshape(N_GRP, SEGS)
        lengths = lengths.reshape(N_GRP, SEGS)
        prompt_ids = prompt_ids.reshape(N_GRP, SEGS)
        segment, offset, usable = jax.vmap(lambda first, second: layout(first, second, TOK_DEV))(starts, lengths)
        proj_resp = jnp.dot(resp_rows, both, preferred_element_type=jnp.float32)
        proj_prompt = jnp.dot(prompt_rows, both, preferred_element_type=jnp.float32)
        resp_pos = (PROMPT_DEV + offset).reshape(-1)
        prompt_pos = jnp.tile(jnp.arange(PROMPT_DEV, dtype=jnp.int32), N_GRP)
        positions = jnp.concatenate([resp_pos, prompt_pos], 0)
        raw_keys = jnp.concatenate([proj_resp[:, :key_value_width], proj_prompt[:, :key_value_width]], 0)
        keys_all = norm_rope(raw_keys, key_gain, positions).astype(jnp.bfloat16)
        resp_keys = keys_all[:N_GRP * TOK_DEV].reshape(N_GRP, TOK_DEV, key_value_width)
        prompt_keys_all = keys_all[N_GRP * TOK_DEV:]
        resp_values = proj_resp[:, key_value_width:].astype(jnp.bfloat16).reshape(N_GRP, TOK_DEV, key_value_width)
        prompt_values_all = proj_prompt[:, key_value_width:].astype(jnp.bfloat16)
        seg_slot = owners[prompt_ids]
        slot_rows = jnp.take_along_axis(seg_slot, segment, axis=1)
        results = lax.map(lambda item: device_attention(*item, prompt_keys_all, prompt_values_all), (my_queries.reshape(N_GRP, TOK_DEV, -1), my_cotangent.reshape(N_GRP, TOK_DEV, -1), resp_keys, resp_values, segment, offset, usable, slot_rows))
        query_grad, prompt_kparts, resp_kgrad, prompt_vparts, resp_vgrad = results
        prompt_kgrad = lax.optimization_barrier(jnp.sum(prompt_kparts.astype(jnp.float32), 0))
        prompt_vgrad = lax.optimization_barrier(jnp.sum(prompt_vparts.astype(jnp.float32), 0)).astype(jnp.bfloat16)
        _, key_back = jax.vjp(lambda raw: norm_rope(raw, key_gain, positions), raw_keys)
        key_cot = jnp.concatenate([resp_kgrad.reshape(-1, key_value_width).astype(jnp.float32), prompt_kgrad], 0)
        raw_kgrad = key_back(key_cot)[0].astype(jnp.bfloat16)
        value_all = jnp.concatenate([resp_vgrad.reshape(-1, key_value_width), prompt_vgrad], 0)
        grads_all = jnp.concatenate([raw_kgrad, value_all], 1)
        input_grad = jnp.dot(grads_all, both.T, preferred_element_type=jnp.float32).astype(jnp.bfloat16)
        resp_grads = grads_all[:N_GRP * TOK_DEV].reshape(N_GRP, TOK_DEV, 2 * key_value_width)
        prompt_grads = grads_all[N_GRP * TOK_DEV:].reshape(N_GRP, PROMPT_DEV, 2 * key_value_width)
        resp_x = resp_rows.reshape(N_GRP, TOK_DEV, MODEL_WIDTH)
        prompt_x = prompt_rows.reshape(N_GRP, PROMPT_DEV, MODEL_WIDTH)

        def add_term(running, item):
            rows_x = jnp.concatenate([item[0], item[1]], 0)
            rows_g = jnp.concatenate([item[2], item[3]], 0)
            term = jnp.dot(rows_x.T, rows_g, preferred_element_type=jnp.float32).astype(jnp.bfloat16)
            return (running + term.astype(jnp.float32), 0)
        total, _ = lax.scan(add_term, total, (resp_x, prompt_x, resp_grads, prompt_grads))
        outputs = (query_grad.reshape(N_GRP * TOK_DEV, -1), input_grad[:N_GRP * TOK_DEV], input_grad[N_GRP * TOK_DEV:])
        return (total, outputs)
    start_total = jnp.zeros((MODEL_WIDTH, 2 * key_value_width), jnp.float32)
    total, outputs = lax.scan(per_group, start_total, (queries, out_grad, resp_in, prompt_in, seg_prompt, seg_start, seg_len, owner))
    query_grad, resp_grad, prompt_grad = outputs
    return (query_grad, resp_grad, prompt_grad, total[:, :key_value_width].astype(jnp.bfloat16), total[:, key_value_width:].astype(jnp.bfloat16))
```

```python
import functools
import math

import jax
import jax.numpy as jnp
import numpy as np
from jax import lax
from jax.experimental import pallas as pl
from jax.experimental.pallas import tpu as pltpu
from jax.sharding import PartitionSpec as P

MESH = pl.DeviceIdType.MESH
ANY = pl.BlockSpec(memory_space=pl.ANY)
SMEM = pl.BlockSpec(memory_space=pltpu.SMEM)
VMEM = pl.BlockSpec(memory_space=pltpu.VMEM)
VMEM_LIMIT = 52 * 1024 * 1024

WIDTH = 5120
HEAD = 128
ROWS = 160
HALF = 80
TOK = 128
PRO = 64
DEV = TOK + PRO
SCALE = 1.0 / math.sqrt(HEAD)
BASE = 1000000.0
bf16 = jnp.bfloat16
f32 = jnp.float32


def rotary_tables():
    frequency = np.float32(BASE) ** (-np.arange(64, dtype=np.float32) / np.float32(64))
    angles = np.arange(-128, 192, dtype=np.float32)[:, None] * frequency[None, :].astype(np.float32)
    angles = angles.astype(np.float32).astype(np.float64)
    cos, sin = np.cos(angles), np.sin(angles)
    return (
        np.concatenate([cos, cos], 1).astype(np.float32),
        np.concatenate([-sin, sin], 1).astype(np.float32),
    )


class Place:
    def __init__(self):
        g, f = lax.axis_index("grp"), lax.axis_index("fsdp")
        self.core, self.zh = lax.rem(g, 2), lax.div(g, 2)
        self.zl = lax.rem(f, 2)
        self.x = lax.rem(lax.div(f, 2), 4)
        self.y = lax.div(f, 8)
        self.z = self.zh * 2 + self.zl

    def at(self, y=None, x=None, z=None, core=None):
        y = self.y if y is None else y
        x = self.x if x is None else x
        z = self.z if z is None else z
        core = self.core if core is None else core
        return {"grp": lax.div(z, 2) * 2 + core, "fsdp": (y * 4 + x) * 2 + lax.rem(z, 2)}

    def ring_x(self):
        return self.x, self.at(x=lax.rem(self.x + 3, 4)), self.at(x=lax.rem(self.x + 1, 4))

    def ring_y(self):
        return self.y, self.at(y=lax.rem(self.y + 3, 4)), self.at(y=lax.rem(self.y + 1, 4))

    def ring_zh(self):
        return self.zh, self.at(z=lax.rem(self.z + 6, 8)), self.at(z=lax.rem(self.z + 2, 8))

    def near_z(self):
        return self.at(z=lax.rem(self.z + 7, 8)), self.at(z=lax.rem(self.z + 1, 8))

    def partner(self):
        return self.at(core=1 - self.core)


def greet(devices):
    barrier = pltpu.get_barrier_semaphore()
    for device in devices:
        pl.semaphore_signal(barrier, inc=1, device_id=device, device_id_type=MESH)
    pl.semaphore_wait(barrier, len(devices))


class Links:
    def __init__(self, send, recv):
        self.send, self.recv, self.used, self.sent = send, recv, 0, []

    def take(self):
        self.used += 1
        return self.used - 1

    def copy(self, number, src, dst, device):
        return pltpu.make_async_remote_copy(
            src_ref=src,
            dst_ref=dst,
            send_sem=self.send.at[number],
            recv_sem=self.recv.at[number],
            device_id=device,
            device_id_type=MESH,
        )

    def start(self, number, src, dst, device):
        made = self.copy(number, src, dst, device)
        made.start()
        self.sent.append(made)

    def arrived(self, number, dst, device):
        self.copy(number, dst, dst, device).wait_recv()

    def drain(self):
        for made in self.sent:
            made.wait_send()
        self.sent = []


class Gather4:
    def __init__(self, links, ring, view, half, own=None):
        self.links, self.view, self.half = links, view, half
        self.me, self.minus, self.plus = ring
        self.own = view(self.me) if own is None else own
        self.n = [links.take() for _ in range(4)]

    def begin(self):
        self.links.start(self.n[0], self.own, self.view(self.me), self.plus)
        self.links.start(self.n[1], self.own, self.view(self.me), self.minus)

    def forward(self):
        left, right = lax.rem(self.me + 3, 4), lax.rem(self.me + 1, 4)
        self.links.arrived(self.n[0], self.view(left), self.plus)
        self.links.start(self.n[2], self.half(left, 0), self.half(left, 0), self.plus)
        self.links.arrived(self.n[1], self.view(right), self.minus)
        self.links.start(self.n[3], self.half(right, 1), self.half(right, 1), self.minus)

    def finish(self):
        across = lax.rem(self.me + 2, 4)
        self.links.arrived(self.n[2], self.half(across, 0), self.plus)
        self.links.arrived(self.n[3], self.half(across, 1), self.minus)


class Reduce4:
    def __init__(self, links, ring, part, slot, add):
        self.links, self.part, self.slot, self.add = links, part, slot, add
        self.me, self.minus, self.plus = ring
        self.n = [links.take() for _ in range(6)]

    def begin(self):
        across = lax.rem(self.me + 2, 4)
        left, right = lax.rem(self.me + 3, 4), lax.rem(self.me + 1, 4)
        part, slot, n = self.part, self.slot, self.n
        self.links.start(n[0], part(across, 0), slot(0), self.plus)
        self.links.start(n[1], part(across, 1), slot(1), self.minus)
        self.links.start(n[2], part(right, 1), slot(2), self.plus)
        self.links.start(n[3], part(left, 0), slot(3), self.minus)

    def mid(self):
        left, right = lax.rem(self.me + 3, 4), lax.rem(self.me + 1, 4)
        part, slot, n = self.part, self.slot, self.n
        self.links.arrived(n[0], slot(0), self.plus)
        self.add(slot(0), [slot(0), part(right, 0)])
        self.links.start(n[4], slot(0), slot(4), self.plus)
        self.links.arrived(n[1], slot(1), self.minus)
        self.add(slot(1), [slot(1), part(left, 1)])
        self.links.start(n[5], slot(1), slot(5), self.minus)

    def finish(self, out):
        part, slot, n = self.part, self.slot, self.n
        self.links.arrived(n[3], slot(3), self.minus)
        self.links.arrived(n[4], slot(4), self.plus)
        self.add(out(0), [part(self.me, 0), slot(3), slot(4)])
        self.links.arrived(n[2], slot(2), self.plus)
        self.links.arrived(n[5], slot(5), self.minus)
        self.add(out(1), [part(self.me, 1), slot(2), slot(5)])


def add_block(dst, terms):
    total = terms[0][...].astype(f32)
    for term in terms[1:]:
        total = total + term[...].astype(f32)
    dst[...] = total.astype(dst.dtype)


def add_blocks(dst, terms):
    def body(i, carry):
        total = terms[0][i].astype(f32)
        for term in terms[1:]:
            total = total + term[i].astype(f32)
        dst[i] = total.astype(dst.dtype)
        return carry

    lax.fori_loop(0, dst.shape[0], body, 0)


def remote_params(number):
    return pltpu.CompilerParams(
        collective_id=number, has_side_effects=True, vmem_limit_bytes=VMEM_LIMIT
    )


LOCAL = pltpu.CompilerParams(vmem_limit_bytes=VMEM_LIMIT)


GATHER_COPIES = 64


def gather_kernel(kw, vw, resp, prompt, q, og, info, W, X, Q, OG, INFO, send, recv, local):
    me = Place()
    core, partner = me.core, me.partner()
    near_minus, near_plus = me.near_z()
    _, xm, xp = me.ring_x()
    _, ym, yp = me.ring_y()
    greet([xm, xp, ym, yp, near_minus, near_plus, partner])
    links = Links(send, recv)

    def columns(matrix, j):
        return matrix.at[:, pl.ds(pl.multiple_of((core * 2 + j) * HEAD, HEAD), HEAD)]

    own = [columns(kw, 0), columns(kw, 1), columns(vw, 0), columns(vw, 1)]
    x, y, zl = me.x, me.y, me.zl
    rows = lambda h: pl.ds(h * HALF, HALF)

    ax = Gather4(links, me.ring_x(), lambda c: W.at[0, y, c, zl], lambda c, h: W.at[0, y, c, zl, rows(h)], own[0])
    ay = Gather4(links, me.ring_y(), lambda c: W.at[0, c, :, zl], lambda c, h: W.at[0, c, :, zl, rows(h)])
    by = Gather4(links, me.ring_y(), lambda c: W.at[1, c, x, zl], lambda c, h: W.at[1, c, x, zl, rows(h)], own[1])
    bx = Gather4(links, me.ring_x(), lambda c: W.at[1, :, c, zl], lambda c, h: W.at[1, :, c, zl, rows(h)])
    cx = Gather4(links, me.ring_x(), lambda c: W.at[2, y, c], lambda c, h: W.at[2, y, c, h])
    cy = Gather4(links, me.ring_y(), lambda c: W.at[2, c], lambda c, h: W.at[2, c, :, h])
    dy = Gather4(links, me.ring_y(), lambda c: W.at[3, c, x], lambda c, h: W.at[3, c, x, h])
    dx = Gather4(links, me.ring_x(), lambda c: W.at[3, :, c], lambda c, h: W.at[3, :, c, h])
    zn = [(links.take(), links.take()) for _ in range(4)]

    def z_begin(t, src):
        links.start(zn[t][0], src(0), z_view(t, zl, 0), near_plus)
        links.start(zn[t][1], src(1), z_view(t, zl, 1), near_minus)

    def z_finish(t):
        links.arrived(zn[t][0], z_view(t, 1 - zl, 0), near_plus)
        links.arrived(zn[t][1], z_view(t, 1 - zl, 1), near_minus)

    def z_view(t, which, h):
        if t < 2:
            return W.at[t, :, :, which, rows(h)]
        return W.at[t, y, x, which, rows(h)]

    ax.begin()
    by.begin()
    for t in (2, 3):
        matrix_half = lambda h, t=t: vw.at[rows(h), pl.ds(pl.multiple_of((core * 2 + t - 2) * HEAD, HEAD), HEAD)]
        z_begin(t, matrix_half)

    locals_ = []

    def here(src, dst):
        made = pltpu.make_async_copy(src, dst, local.at[len(locals_)])
        made.start()
        locals_.append(made)

    for t in range(4):
        here(own[t], W.at[t, y, x, zl])
    swaps = []

    def swap(src, dst_mine, dst_theirs):
        number = links.take()
        links.start(number, src, dst_mine, partner)
        swaps.append((number, dst_theirs))

    mine = pl.ds(pl.multiple_of(core * 2048, 2048), 2048)
    theirs = pl.ds(pl.multiple_of((1 - core) * 2048, 2048), 2048)
    swap(info, INFO.at[core], INFO.at[1 - core])
    swap(resp.at[0], X.at[core, pl.ds(0, TOK)], X.at[1 - core, pl.ds(0, TOK)])
    swap(prompt.at[0], X.at[core, pl.ds(TOK, PRO)], X.at[1 - core, pl.ds(TOK, PRO)])
    swap(q.at[0, :, theirs], Q.at[core], Q.at[1 - core])
    swap(og.at[0, :, theirs], OG.at[core], OG.at[1 - core])
    here(info, INFO.at[core])
    here(resp.at[0], X.at[core, pl.ds(0, TOK)])
    here(prompt.at[0], X.at[core, pl.ds(TOK, PRO)])
    here(q.at[0, :, mine], Q.at[core])
    here(og.at[0, :, mine], OG.at[core])

    ax.forward()
    by.forward()
    for made in locals_[:4]:
        made.wait()
    z_finish(2)
    cx.begin()
    z_finish(3)
    dy.begin()
    ax.finish()
    ay.begin()
    by.finish()
    bx.begin()
    cx.forward()
    dy.forward()
    cx.finish()
    cy.begin()
    dy.finish()
    dx.begin()
    ay.forward()
    bx.forward()
    ay.finish()
    z_begin(0, lambda h: z_view(0, zl, h))
    bx.finish()
    z_begin(1, lambda h: z_view(1, zl, h))
    cy.forward()
    dx.forward()
    cy.finish()
    dx.finish()
    z_finish(0)
    z_finish(1)
    for number, landing in swaps:
        links.arrived(number, landing, partner)
    for made in locals_[4:]:
        made.wait()
    links.drain()
    assert links.used <= GATHER_COPIES


def gather(kw, vw, resp, prompt, q, og, info):
    return pl.pallas_call(
        gather_kernel,
        out_shape=(
            jax.ShapeDtypeStruct((4, 4, 4, 2, ROWS, HEAD), bf16),
            jax.ShapeDtypeStruct((2, DEV, WIDTH), bf16),
            jax.ShapeDtypeStruct((2, TOK, 2048), bf16),
            jax.ShapeDtypeStruct((2, TOK, 2048), bf16),
            jax.ShapeDtypeStruct((2, 8, 128), jnp.int32),
        ),
        in_specs=[ANY] * 7,
        out_specs=(ANY,) * 5,
        scratch_shapes=[
            pltpu.SemaphoreType.DMA((GATHER_COPIES,)),
            pltpu.SemaphoreType.DMA((GATHER_COPIES,)),
            pltpu.SemaphoreType.DMA((16,)),
        ],
        compiler_params=remote_params(1),
        name="gather",
    )(kw, vw, resp, prompt, q, og, info)


K_STEP = 1024


def swap_halves(a):
    return pltpu.roll(a, 64, 1)


def tables_of(info, d, cos, sin):
    start = info[d, 0, 3]
    late = pl.multiple_of(192 - start, 16)
    row = lax.broadcasted_iota(jnp.int32, (TOK, HEAD), 0)
    out = []
    for table in (cos, sin):
        first = table[pl.ds(192, TOK), :]
        second = table[pl.ds(late, TOK), :]
        out.append(jnp.concatenate([jnp.where(row < start, first, second), table[pl.ds(128, PRO), :]], 0))
    return out


def project_kernel(info, X, W, cos, sin, gain, raw, keys, vals, pkv, acc):
    step = pl.program_id(0)
    left = jnp.concatenate([X[0], X[1]], 0)
    right = jnp.concatenate([W[t] for t in range(4)], 1)
    part = jnp.dot(left, right, preferred_element_type=f32)

    @pl.when(step == 0)
    def _():
        acc[...] = part

    @pl.when(step > 0)
    def _():
        acc[...] += part

    @pl.when(step == pl.num_programs(0) - 1)
    def _():
        for d in range(2):
            c, s = tables_of(info, d, cos, sin)
            for j in range(2):
                k = acc[pl.ds(d * DEV, DEV), pl.ds(j * HEAD, HEAD)]
                raw[j, d] = k
                square = jnp.mean(k * k, axis=1, keepdims=True)
                normed = k * lax.rsqrt(square + 1e-06) * gain[...]
                turned = (normed * c + swap_halves(normed) * s).astype(bf16)
                keys[j, d] = turned
                pkv[j, d] = turned[TOK:]
                v = acc[pl.ds(d * DEV, DEV), pl.ds((2 + j) * HEAD, HEAD)].astype(bf16)
                vals[j, d] = v
                pkv[2 + j, d] = v[TOK:]


def project(info, X, W, cos, sin, gain):
    return pl.pallas_call(
        project_kernel,
        out_shape=(
            jax.ShapeDtypeStruct((2, 2, DEV, HEAD), f32),
            jax.ShapeDtypeStruct((2, 2, DEV, HEAD), bf16),
            jax.ShapeDtypeStruct((2, 2, DEV, HEAD), bf16),
            jax.ShapeDtypeStruct((4, 2, PRO, HEAD), bf16),
        ),
        grid=(WIDTH // K_STEP,),
        in_specs=[
            SMEM,
            pl.BlockSpec((2, DEV, K_STEP), lambda i: (0, 0, i)),
            pl.BlockSpec((4, K_STEP, HEAD), lambda i: (0, i, 0)),
            VMEM,
            VMEM,
            VMEM,
        ],
        out_specs=(VMEM,) * 4,
        scratch_shapes=[pltpu.VMEM((2 * DEV, 512), f32)],
        compiler_params=LOCAL,
        name="project",
    )(info, X, W, cos, sin, gain)


SHARE_COPIES = 8


def share_kernel(pkv, W, everyone, W2, send, recv, local):
    me = Place()
    ring, partner = me.ring_zh(), me.partner()
    greet([ring[1], ring[2], partner])
    links = Links(send, recv)
    own = pltpu.make_async_copy(pkv, everyone.at[me.zh], local)
    own.start()
    going = Gather4(
        links, ring, lambda c: everyone.at[c], lambda c, h: everyone.at[c, pl.ds(2 * h, 2)], pkv
    )
    going.begin()
    weights = links.take()
    links.start(weights, W, W2, partner)
    going.forward()
    going.finish()
    own.wait()
    links.arrived(weights, W2, partner)
    links.drain()


def share(pkv, W):
    return pl.pallas_call(
        share_kernel,
        out_shape=(
            jax.ShapeDtypeStruct((4, 4, 2, PRO, HEAD), bf16),
            jax.ShapeDtypeStruct((4, 4, 4, 2, ROWS, HEAD), bf16),
        ),
        in_specs=[ANY, ANY],
        out_specs=(ANY, ANY),
        scratch_shapes=[
            pltpu.SemaphoreType.DMA((SHARE_COPIES,)),
            pltpu.SemaphoreType.DMA((SHARE_COPIES,)),
            pltpu.SemaphoreType.DMA,
        ],
        compiler_params=remote_params(2),
        name="share",
    )(pkv, W)


def attention_kernel(info, everyone, keys, vals, Q, OG, QG, RG, PP, probs, slopes, queries, cots, parts):
    d, j = pl.program_id(0), pl.program_id(1)

    @pl.when((d == 0) & (j == 0))
    def _():
        parts[...] = jnp.zeros_like(parts)

    slots = [info[d, 0, 0], info[d, 0, 1]]
    start, lens = info[d, 0, 3], [info[d, 0, 4], info[d, 0, 5]]
    places = [(lax.div(s, 2), lax.rem(s, 2)) for s in slots]
    K = jnp.concatenate([everyone[zh, j, c] for zh, c in places] + [keys[0, 0, :TOK]], 0)
    V = jnp.concatenate([everyone[zh, 2 + j, c] for zh, c in places] + [vals[0, 0, :TOK]], 0)

    key = lax.broadcasted_iota(jnp.int32, (2 * TOK, TOK), 0)
    row = lax.broadcasted_iota(jnp.int32, (2 * TOK, TOK), 1)
    late = row >= start
    first = jnp.where(late, start, 0)
    end = jnp.where(late, start + lens[1], lens[0])
    from_key = jnp.where(key < TOK, jnp.where(late, PRO, 0), first + TOK)
    to_key = jnp.where(key < TOK, jnp.where(late, TOK, PRO), jnp.minimum(end, row + 1) + TOK)
    allowed = (key >= from_key) & (key < to_key)
    line = lax.broadcasted_iota(jnp.int32, (TOK, HEAD), 0)
    used = line < jnp.where(line >= start, start + lens[1], lens[0])

    for h in range(8):
        lanes = pl.ds(h * HEAD, HEAD)
        block = pl.ds(h * TOK, TOK)
        q = Q[0, :, lanes]
        cot = jnp.where(used, OG[0, :, lanes].astype(f32), 0.0).astype(bf16)
        queries[block, :] = q
        cots[block, :] = cot
        scores = lax.dot_general(K, q, (((1,), (1,)), ((), ())), preferred_element_type=f32)
        scores = jnp.where(allowed, scores * SCALE, -1e30)
        top = jnp.max(scores, axis=0, keepdims=True)
        weights = jnp.exp(scores - top)
        prob = weights / jnp.sum(weights, axis=0, keepdims=True)
        probs[:, block] = prob.astype(bf16)
        slope = lax.dot_general(V, cot, (((1,), (1,)), ((), ())), preferred_element_type=f32)
        slope = slope.astype(bf16).astype(f32)
        inner = jnp.sum(slope * prob, axis=0, keepdims=True)
        back = (prob * (slope - inner) * SCALE).astype(bf16)
        slopes[:, block] = back
        QG[0, :, lanes] = lax.dot_general(
            back, K, (((0,), (0,)), ((), ())), preferred_element_type=f32
        ).astype(bf16)
    dv = jnp.dot(probs[...], cots[...], preferred_element_type=f32)
    dk = jnp.dot(slopes[...], queries[...], preferred_element_type=f32)
    RG[0, 0, 0] = dk[TOK:].astype(bf16)
    RG[0, 0, 1] = dv[TOK:].astype(bf16)
    for s, (zh, c) in enumerate(places):
        parts[zh, j, c] += dk[s * PRO : (s + 1) * PRO]
        parts[zh, 2 + j, c] += dv[s * PRO : (s + 1) * PRO]

    @pl.when((d == 1) & (j == 1))
    def _():
        PP[...] = parts[...].astype(bf16)


def attention(info, everyone, keys, vals, Q, OG):
    return pl.pallas_call(
        attention_kernel,
        out_shape=(
            jax.ShapeDtypeStruct((2, TOK, 2048), bf16),
            jax.ShapeDtypeStruct((2, 2, 2, TOK, HEAD), bf16),
            jax.ShapeDtypeStruct((4, 4, 2, PRO, HEAD), bf16),
        ),
        grid=(2, 2),
        in_specs=[
            SMEM,
            VMEM,
            pl.BlockSpec((1, 1, DEV, HEAD), lambda d, j: (j, d, 0, 0)),
            pl.BlockSpec((1, 1, DEV, HEAD), lambda d, j: (j, d, 0, 0)),
            pl.BlockSpec((1, TOK, 1024), lambda d, j: (d, 0, j)),
            pl.BlockSpec((1, TOK, 1024), lambda d, j: (d, 0, j)),
        ],
        out_specs=(
            pl.BlockSpec((1, TOK, 1024), lambda d, j: (d, 0, j)),
            pl.BlockSpec((1, 1, 2, TOK, HEAD), lambda d, j: (j, d, 0, 0, 0)),
            VMEM,
        ),
        scratch_shapes=[
            pltpu.VMEM((256, 1024), bf16),
            pltpu.VMEM((256, 1024), bf16),
            pltpu.VMEM((1024, HEAD), bf16),
            pltpu.VMEM((1024, HEAD), bf16),
            pltpu.VMEM((4, 4, 2, PRO, HEAD), f32),
        ],
        compiler_params=LOCAL,
        name="attention",
    )(info, everyone, keys, vals, Q, OG)


RETURN_COPIES = 8


def return_kernel(PP, QG, PS, QP, land, send, recv):
    me = Place()
    ring, partner = me.ring_zh(), me.partner()
    greet([ring[1], ring[2], partner])
    links = Links(send, recv)

    def add(dst, terms):
        for i in range(2):
            for d in range(2):
                total = terms[0][i, d].astype(f32)
                for term in terms[1:]:
                    total = total + term[i, d].astype(f32)
                dst[i, d] = total.astype(dst.dtype)

    going = Reduce4(
        links, ring, lambda c, h: PP.at[c, pl.ds(2 * h, 2)], lambda i: land.at[i], add
    )
    going.begin()
    queries = links.take()
    links.start(queries, QG.at[1 - me.core], QP, partner)
    going.mid()
    going.finish(lambda h: PS.at[pl.ds(2 * h, 2)])
    links.arrived(queries, QP, partner)
    links.drain()


def give_back(PP, QG):
    return pl.pallas_call(
        return_kernel,
        out_shape=(
            jax.ShapeDtypeStruct((4, 2, PRO, HEAD), f32),
            jax.ShapeDtypeStruct((TOK, 2048), bf16),
        ),
        in_specs=[VMEM, ANY],
        out_specs=(VMEM, ANY),
        scratch_shapes=[
            pltpu.VMEM((6, 2, 2, PRO, HEAD), bf16),
            pltpu.SemaphoreType.DMA((RETURN_COPIES,)),
            pltpu.SemaphoreType.DMA((RETURN_COPIES,)),
        ],
        compiler_params=remote_params(3),
        name="give_back",
    )(PP, QG)


W_STEP = 640


def weight_kernel(info, raw, RG, PS, cos, sin, gain, X, D, G, grads):
    step = pl.program_id(0)

    @pl.when(step == 0)
    def _():
        for d in range(2):
            c, s = tables_of(info, d, cos, sin)
            for j in range(2):
                cot = jnp.concatenate([RG[j, d, 0].astype(f32), PS[j, d]], 0)
                turned = (cot * c + swap_halves(cot * s)) * gain[...]
                k = raw[j, d]
                inverse = lax.rsqrt(jnp.mean(k * k, axis=1, keepdims=True) + 1e-06)
                along = jnp.mean(k * turned, axis=1, keepdims=True)
                back = inverse * turned - k * (inverse * inverse * inverse * along)
                grads[pl.ds(d * DEV, DEV), pl.ds(j * HEAD, HEAD)] = back.astype(bf16)
                values = jnp.concatenate([RG[j, d, 1], PS[2 + j, d].astype(bf16)], 0)
                grads[pl.ds(d * DEV, DEV), pl.ds((2 + j) * HEAD, HEAD)] = values
        G[0] = grads[:DEV]
        G[1] = grads[DEV:]

    rows = jnp.concatenate([X[0], X[1]], 0)
    term = lax.dot_general(
        rows, grads[...], (((0,), (0,)), ((), ())), preferred_element_type=f32
    ).astype(bf16)
    for t in range(4):
        D[t] = term[:, t * HEAD : (t + 1) * HEAD]


def weight_terms(info, raw, RG, PS, cos, sin, gain, X):
    return pl.pallas_call(
        weight_kernel,
        out_shape=(
            jax.ShapeDtypeStruct((4, WIDTH, HEAD), bf16),
            jax.ShapeDtypeStruct((2, DEV, 512), bf16),
        ),
        grid=(WIDTH // W_STEP,),
        in_specs=[SMEM] + [VMEM] * 6 + [pl.BlockSpec((2, DEV, W_STEP), lambda i: (0, 0, i))],
        out_specs=(pl.BlockSpec((4, W_STEP, HEAD), lambda i: (0, i, 0)), VMEM),
        scratch_shapes=[pltpu.VMEM((2 * DEV, 512), bf16)],
        compiler_params=LOCAL,
        name="weight_terms",
    )(info, raw, RG, PS, cos, sin, gain, X)


SUM_COPIES = 64


def sum_kernel(D, G, WG, GO, one, acc1, two, acc2, near, acc3, three, wg, send, recv):
    me = Place()
    partner = me.partner()
    near_minus, near_plus = me.near_z()
    ring_x, ring_y, ring_zh = me.ring_x(), me.ring_y(), me.ring_zh()
    greet([*ring_x[1:], *ring_y[1:], *ring_zh[1:], near_minus, near_plus, partner])
    links = Links(send, recv)
    core, zl = me.core, me.zl

    first, second = [], []
    for t in range(4):
        if t < 2:
            part = lambda c, h, t=t: D.at[t, :, c, h]
        else:
            part = lambda c, h, t=t: D.at[t, c, :, h]
        ring = ring_x if t < 2 else ring_y
        other = ring_y if t < 2 else ring_x
        first.append(Reduce4(links, ring, part, lambda i, t=t: one.at[t, i], add_blocks))
        second.append(
            Reduce4(
                links,
                other,
                lambda c, h, t=t: acc1.at[t, c, h],
                lambda i, t=t: two.at[t, i],
                add_block,
            )
        )
    order = (0, 2, 1, 3)
    for t in order:
        first[t].begin()
    grads = links.take()
    links.start(grads, G.at[1 - core], GO, partner)
    for t in order:
        first[t].mid()
    for t in order:
        first[t].finish(lambda h, t=t: acc1.at[t, :, h])
        second[t].begin()
    for t in order:
        second[t].mid()
    for t in order:
        second[t].finish(lambda h, t=t: acc2.at[t, h])

    up, down = links.take(), links.take()
    links.start(up, acc2.at[:, 1 - zl, pl.ds(0, HALF)], near.at[0], near_plus)
    links.start(down, acc2.at[:, 1 - zl, pl.ds(HALF, HALF)], near.at[1], near_minus)
    links.arrived(up, near.at[0], near_plus)
    add_blocks(acc3.at[:, 0], [acc2.at[:, zl, pl.ds(0, HALF)], near.at[0]])
    links.arrived(down, near.at[1], near_minus)
    add_blocks(acc3.at[:, 1], [acc2.at[:, zl, pl.ds(HALF, HALF)], near.at[1]])

    third = Reduce4(links, ring_zh, lambda c, h: acc3.at[c, h], lambda i: three.at[i], add_block)
    third.begin()
    third.mid()
    third.finish(lambda h: wg.at[core, me.zh, h])
    last = Gather4(links, ring_zh, lambda c: wg.at[core, c], lambda c, h: wg.at[core, c, h])
    last.begin()
    last.forward()
    last.finish()
    across = links.take()
    links.start(across, wg.at[core], wg.at[core], partner)
    links.arrived(across, wg.at[1 - core], partner)
    links.arrived(grads, GO, partner)
    WG[...] = wg[...]
    links.drain()
    assert links.used <= SUM_COPIES


def sum_terms(D, G):
    return pl.pallas_call(
        sum_kernel,
        out_shape=(
            jax.ShapeDtypeStruct((2, 4, 2, HALF, HEAD), bf16),
            jax.ShapeDtypeStruct((DEV, 512), bf16),
        ),
        in_specs=[VMEM, ANY],
        out_specs=(VMEM, ANY),
        scratch_shapes=[
            pltpu.VMEM((4, 6, 4, ROWS, HEAD), bf16),
            pltpu.VMEM((4, 4, 2, ROWS, HEAD), bf16),
            pltpu.VMEM((4, 6, ROWS, HEAD), bf16),
            pltpu.VMEM((4, 2, ROWS, HEAD), bf16),
            pltpu.VMEM((2, 4, HALF, HEAD), bf16),
            pltpu.VMEM((4, 2, HALF, HEAD), bf16),
            pltpu.VMEM((6, HALF, HEAD), bf16),
            pltpu.VMEM((2, 4, 2, HALF, HEAD), bf16),
            pltpu.SemaphoreType.DMA((SUM_COPIES,)),
            pltpu.SemaphoreType.DMA((SUM_COPIES,)),
        ],
        compiler_params=remote_params(4),
        name="sum_terms",
    )(D, G)


I_STEP = 640


def input_kernel(info, G, GO, W, W2, WG, QG, QP, resp, prompt, qgrad, kout, vout, sems):
    step = pl.program_id(0)
    core = info[0, 1, 0]
    mine = pl.ds(pl.multiple_of(core * 2048, 2048), 2048)
    theirs = pl.ds(pl.multiple_of((1 - core) * 2048, 2048), 2048)
    copies = (
        pltpu.make_async_copy(QG.at[core], qgrad.at[0, :, mine], sems.at[0]),
        pltpu.make_async_copy(QP, qgrad.at[0, :, theirs], sems.at[1]),
    )

    @pl.when(step == 0)
    def _():
        for made in copies:
            made.start()
        for c in range(2):
            for j in range(2):
                lanes = pl.ds((2 * c + j) * HEAD, HEAD)
                kout[:, lanes] = WG[c, j]
                vout[:, lanes] = WG[c, 2 + j]

    total = 0.0
    for grads, weights in ((G[core], W), (GO[...], W2)):
        both = jnp.concatenate([weights[t] for t in range(4)], 1)
        total = total + lax.dot_general(
            grads, both, (((1,), (1,)), ((), ())), preferred_element_type=f32
        )
    total = total.astype(bf16)
    resp[0] = total[:TOK]
    prompt[0] = total[TOK:]

    @pl.when(step == pl.num_programs(0) - 1)
    def _():
        for made in copies:
            made.wait()


def input_grads(info, G, GO, W, W2, WG, QG, QP):
    return pl.pallas_call(
        input_kernel,
        out_shape=(
            jax.ShapeDtypeStruct((1, TOK, WIDTH), bf16),
            jax.ShapeDtypeStruct((1, PRO, WIDTH), bf16),
            jax.ShapeDtypeStruct((1, TOK, 4096), bf16),
            jax.ShapeDtypeStruct((ROWS, 512), bf16),
            jax.ShapeDtypeStruct((ROWS, 512), bf16),
        ),
        grid=(WIDTH // I_STEP,),
        in_specs=[
            SMEM,
            VMEM,
            VMEM,
            pl.BlockSpec((4, I_STEP, HEAD), lambda i: (0, i, 0)),
            pl.BlockSpec((4, I_STEP, HEAD), lambda i: (0, i, 0)),
            VMEM,
            ANY,
            ANY,
        ],
        out_specs=(
            pl.BlockSpec((1, TOK, I_STEP), lambda i: (0, 0, i)),
            pl.BlockSpec((1, PRO, I_STEP), lambda i: (0, 0, i)),
            ANY,
            VMEM,
            VMEM,
        ),
        scratch_shapes=[pltpu.SemaphoreType.DMA((2,))],
        compiler_params=LOCAL,
        name="input_grads",
    )(info, G, GO, W, W2, WG, QG, QP)


def local(
    queries, out_grad, resp_in, prompt_in, key_matrix, value_matrix, key_gain, seg_prompt, seg_start, seg_len, owner
):
    cos, sin = rotary_tables()
    gain = key_gain.reshape(1, HEAD)
    match = seg_prompt[0][:, None] == jnp.arange(8, dtype=jnp.int32)[None, :]
    slots = jnp.sum(jnp.where(match, owner[0][None, :], 0), 1)
    line = jnp.concatenate([slots, seg_start[0], seg_len[0], jnp.zeros((122,), jnp.int32)])
    core = lax.rem(lax.axis_index("grp"), 2).astype(jnp.int32)
    info = jnp.concatenate([line[None], jnp.broadcast_to(core, (7, 128))], 0)

    W, X, Q, OG, both = gather(key_matrix, value_matrix, resp_in, prompt_in, queries, out_grad, info)
    flat = W.reshape(4, WIDTH, HEAD)
    raw, keys, vals, pkv = project(both, X, flat, cos, sin, gain)
    everyone, W2 = share(pkv, W)
    QG, RG, PP = attention(both, everyone, keys, vals, Q, OG)
    PS, QP = give_back(PP, QG)
    D, G = weight_terms(both, raw, RG, PS, cos, sin, gain, X)
    WG, GO = sum_terms(D.reshape(4, 4, 4, 2, ROWS, HEAD), G)
    WG = WG.reshape(2, 4, ROWS, HEAD)
    resp, prompt, qgrad, kout, vout = input_grads(
        info.reshape(1, 8, 128), G, GO, flat, W2.reshape(4, WIDTH, HEAD), WG, QG, QP
    )
    return qgrad, resp, prompt, kout, vout


def solution(mesh):
    in_specs = (
        P("fsdp", "grp", None),
        P("fsdp", "grp", None),
        P("fsdp", "grp", None),
        P("fsdp", "grp", None),
        P("fsdp", None),
        P("fsdp", None),
        P(),
        P("fsdp", "grp"),
        P("fsdp", "grp"),
        P("fsdp", "grp"),
        P("fsdp", None),
    )
    out_specs = (
        P("fsdp", "grp", None),
        P("fsdp", "grp", None),
        P("fsdp", "grp", None),
        P("fsdp", None),
        P("fsdp", None),
    )
    return jax.shard_map(local, mesh=mesh, in_specs=in_specs, out_specs=out_specs, check_vma=False)
```

```python
import functools
import math

import jax
import jax.numpy as jnp
import numpy as np
from jax import lax
from jax.experimental import pallas as pl
from jax.experimental.pallas import tpu as pltpu
from jax.sharding import PartitionSpec as P

MESH = pl.DeviceIdType.MESH
HBM = pl.BlockSpec(memory_space=pltpu.HBM)
SMEM = pl.BlockSpec(memory_space=pltpu.SMEM)
VMEM = pl.BlockSpec(memory_space=pltpu.VMEM)
VMEM_LIMIT = 52 * 1024 * 1024

WIDTH = 5120
HEAD = 128
ROWS = 160
HALF = 80
TOK = 128
PRO = 64
DEV = TOK + PRO
SCALE = 1.0 / math.sqrt(HEAD)
BASE = 1000000.0
bf16 = jnp.bfloat16
f32 = jnp.float32


def rotary_tables():
    frequency = np.float32(BASE) ** (-np.arange(64, dtype=np.float32) / np.float32(64))
    angles = np.arange(-128, 192, dtype=np.float32)[:, None] * frequency[None, :].astype(np.float32)
    angles = angles.astype(np.float32).astype(np.float64)
    cos, sin = np.cos(angles), np.sin(angles)
    return (
        np.concatenate([cos, cos], 1).astype(np.float32),
        np.concatenate([-sin, sin], 1).astype(np.float32),
    )


class Place:
    def __init__(self):
        g, f = lax.axis_index("grp"), lax.axis_index("fsdp")
        self.core, self.zh = lax.rem(g, 2), lax.div(g, 2)
        self.zl = lax.rem(f, 2)
        self.x = lax.rem(lax.div(f, 2), 4)
        self.y = lax.div(f, 8)
        self.z = self.zh * 2 + self.zl

    def at(self, y=None, x=None, z=None, core=None):
        y = self.y if y is None else y
        x = self.x if x is None else x
        z = self.z if z is None else z
        core = self.core if core is None else core
        return {"grp": lax.div(z, 2) * 2 + core, "fsdp": (y * 4 + x) * 2 + lax.rem(z, 2)}

    def ring_x(self):
        return self.x, self.at(x=lax.rem(self.x + 3, 4)), self.at(x=lax.rem(self.x + 1, 4))

    def ring_y(self):
        return self.y, self.at(y=lax.rem(self.y + 3, 4)), self.at(y=lax.rem(self.y + 1, 4))

    def ring_zh(self):
        return self.zh, self.at(z=lax.rem(self.z + 6, 8)), self.at(z=lax.rem(self.z + 2, 8))

    def near_z(self):
        return self.at(z=lax.rem(self.z + 7, 8)), self.at(z=lax.rem(self.z + 1, 8))

    def partner(self):
        return self.at(core=1 - self.core)


def greet(devices):
    barrier = pltpu.get_barrier_semaphore()
    for device in devices:
        pl.semaphore_signal(barrier, inc=1, device_id=device, device_id_type=MESH)
    pl.semaphore_wait(barrier, len(devices))


class Links:
    def __init__(self, send, recv):
        self.send, self.recv, self.used, self.sent = send, recv, 0, []

    def take(self):
        self.used += 1
        return self.used - 1

    def copy(self, number, src, dst, device):
        return pltpu.make_async_remote_copy(
            src_ref=src,
            dst_ref=dst,
            send_sem=self.send.at[number],
            recv_sem=self.recv.at[number],
            device_id=device,
            device_id_type=MESH,
        )

    def start(self, number, src, dst, device):
        made = self.copy(number, src, dst, device)
        made.start()
        self.sent.append(made)

    def arrived(self, number, dst, device):
        self.copy(number, dst, dst, device).wait_recv()

    def drain(self):
        for made in self.sent:
            made.wait_send()
        self.sent = []


class Gather4:
    def __init__(self, links, ring, view, half, own=None):
        self.links, self.view, self.half = links, view, half
        self.me, self.minus, self.plus = ring
        self.own = view(self.me) if own is None else own
        self.n = [links.take() for _ in range(4)]

    def begin(self):
        self.links.start(self.n[0], self.own, self.view(self.me), self.plus)
        self.links.start(self.n[1], self.own, self.view(self.me), self.minus)

    def forward(self):
        left, right = lax.rem(self.me + 3, 4), lax.rem(self.me + 1, 4)
        self.links.arrived(self.n[0], self.view(left), self.plus)
        self.links.start(self.n[2], self.half(left, 0), self.half(left, 0), self.plus)
        self.links.arrived(self.n[1], self.view(right), self.minus)
        self.links.start(self.n[3], self.half(right, 1), self.half(right, 1), self.minus)

    def finish(self):
        across = lax.rem(self.me + 2, 4)
        self.links.arrived(self.n[2], self.half(across, 0), self.plus)
        self.links.arrived(self.n[3], self.half(across, 1), self.minus)


class Reduce4:
    def __init__(self, links, ring, part, slot, add):
        self.links, self.part, self.slot, self.add = links, part, slot, add
        self.me, self.minus, self.plus = ring
        self.n = [links.take() for _ in range(6)]

    def send_for(self, place):
        part, slot, n = self.part, self.slot, self.n
        block = lax.rem(self.me + place, 4)
        if place == 2:
            self.links.start(n[0], part(block, 0), slot(0), self.plus)
            self.links.start(n[1], part(block, 1), slot(1), self.minus)
        if place == 1:
            self.links.start(n[2], part(block, 1), slot(2), self.plus)
        if place == 3:
            self.links.start(n[3], part(block, 0), slot(3), self.minus)

    def begin(self):
        for place in (2, 1, 3):
            self.send_for(place)

    def mid(self):
        left, right = lax.rem(self.me + 3, 4), lax.rem(self.me + 1, 4)
        part, slot, n = self.part, self.slot, self.n
        self.links.arrived(n[0], slot(0), self.plus)
        self.add(slot(0), [slot(0), part(right, 0)])
        self.links.start(n[4], slot(0), slot(4), self.plus)
        self.links.arrived(n[1], slot(1), self.minus)
        self.add(slot(1), [slot(1), part(left, 1)])
        self.links.start(n[5], slot(1), slot(5), self.minus)

    def finish(self, out):
        part, slot, n = self.part, self.slot, self.n
        self.links.arrived(n[3], slot(3), self.minus)
        self.links.arrived(n[4], slot(4), self.plus)
        self.add(out(0), [part(self.me, 0), slot(3), slot(4)])
        self.links.arrived(n[2], slot(2), self.plus)
        self.links.arrived(n[5], slot(5), self.minus)
        self.add(out(1), [part(self.me, 1), slot(2), slot(5)])


def add_block(dst, terms):
    total = terms[0][...].astype(f32)
    for term in terms[1:]:
        total = total + term[...].astype(f32)
    dst[...] = total.astype(dst.dtype)


def add_blocks(dst, terms):
    def body(i, carry):
        total = terms[0][i].astype(f32)
        for term in terms[1:]:
            total = total + term[i].astype(f32)
        dst[i] = total.astype(dst.dtype)
        return carry

    lax.fori_loop(0, dst.shape[0], body, 0)


def remote_params(number):
    return pltpu.CompilerParams(
        collective_id=number, has_side_effects=True, vmem_limit_bytes=VMEM_LIMIT
    )


LOCAL = pltpu.CompilerParams(vmem_limit_bytes=VMEM_LIMIT)


GATHER_COPIES = 64


def gather_kernel(kw, vw, resp, prompt, q, og, info, W, XP, QP, OP, INFO, send, recv, local):
    me = Place()
    core, partner = me.core, me.partner()
    near_minus, near_plus = me.near_z()
    _, xm, xp = me.ring_x()
    _, ym, yp = me.ring_y()
    greet([xm, xp, ym, yp, near_minus, near_plus, partner])
    links = Links(send, recv)

    def columns(matrix, j):
        return matrix.at[:, pl.ds(pl.multiple_of((core * 2 + j) * HEAD, HEAD), HEAD)]

    own = [columns(kw, 0), columns(kw, 1), columns(vw, 0), columns(vw, 1)]
    x, y, zl = me.x, me.y, me.zl
    rows = lambda h: pl.ds(h * HALF, HALF)

    ax = Gather4(links, me.ring_x(), lambda c: W.at[0, y, c, zl], lambda c, h: W.at[0, y, c, zl, rows(h)], own[0])
    ay = Gather4(links, me.ring_y(), lambda c: W.at[0, c, :, zl], lambda c, h: W.at[0, c, :, zl, rows(h)])
    by = Gather4(links, me.ring_y(), lambda c: W.at[1, c, x, zl], lambda c, h: W.at[1, c, x, zl, rows(h)], own[1])
    bx = Gather4(links, me.ring_x(), lambda c: W.at[1, :, c, zl], lambda c, h: W.at[1, :, c, zl, rows(h)])
    cx = Gather4(links, me.ring_x(), lambda c: W.at[2, y, c], lambda c, h: W.at[2, y, c, h])
    cy = Gather4(links, me.ring_y(), lambda c: W.at[2, c], lambda c, h: W.at[2, c, :, h])
    dy = Gather4(links, me.ring_y(), lambda c: W.at[3, c, x], lambda c, h: W.at[3, c, x, h])
    dx = Gather4(links, me.ring_x(), lambda c: W.at[3, :, c], lambda c, h: W.at[3, :, c, h])
    zn = [(links.take(), links.take()) for _ in range(4)]

    def z_begin(t, src):
        links.start(zn[t][0], src(0), z_view(t, zl, 0), near_plus)
        links.start(zn[t][1], src(1), z_view(t, zl, 1), near_minus)

    def z_finish(t):
        links.arrived(zn[t][0], z_view(t, 1 - zl, 0), near_plus)
        links.arrived(zn[t][1], z_view(t, 1 - zl, 1), near_minus)

    def z_view(t, which, h):
        if t < 2:
            return W.at[t, :, :, which, rows(h)]
        return W.at[t, y, x, which, rows(h)]

    ax.begin()
    by.begin()
    for t in (2, 3):
        matrix_half = lambda h, t=t: vw.at[rows(h), pl.ds(pl.multiple_of((core * 2 + t - 2) * HEAD, HEAD), HEAD)]
        z_begin(t, matrix_half)

    locals_ = []

    def here(src, dst):
        made = pltpu.make_async_copy(src, dst, local.at[len(locals_)])
        made.start()
        locals_.append(made)

    for t in range(4):
        here(own[t], W.at[t, y, x, zl])
    here(info, INFO.at[0])
    swaps = []

    def swap(src, dst):
        number = links.take()
        links.start(number, src, dst, partner)
        swaps.append((number, dst))

    theirs = pl.ds(pl.multiple_of((1 - core) * 2048, 2048), 2048)
    swap(info, INFO.at[1])
    swap(resp.at[0], XP.at[pl.ds(0, TOK)])
    swap(prompt.at[0], XP.at[pl.ds(TOK, PRO)])
    swap(q.at[0, :, theirs], QP)
    swap(og.at[0, :, theirs], OP)

    ax.forward()
    by.forward()
    for made in locals_[:4]:
        made.wait()
    z_finish(2)
    cx.begin()
    z_finish(3)
    dy.begin()
    ax.finish()
    ay.begin()
    by.finish()
    bx.begin()
    cx.forward()
    dy.forward()
    cx.finish()
    cy.begin()
    dy.finish()
    dx.begin()
    ay.forward()
    bx.forward()
    ay.finish()
    z_begin(0, lambda h: z_view(0, zl, h))
    bx.finish()
    z_begin(1, lambda h: z_view(1, zl, h))
    cy.forward()
    dx.forward()
    cy.finish()
    dx.finish()
    z_finish(0)
    z_finish(1)
    for number, landing in swaps:
        links.arrived(number, landing, partner)
    for made in locals_[4:]:
        made.wait()
    links.drain()
    assert links.used <= GATHER_COPIES


def gather(kw, vw, resp, prompt, q, og, info):
    return pl.pallas_call(
        gather_kernel,
        out_shape=(
            jax.ShapeDtypeStruct((4, 4, 4, 2, ROWS, HEAD), bf16),
            jax.ShapeDtypeStruct((DEV, WIDTH), bf16),
            jax.ShapeDtypeStruct((TOK, 2048), bf16),
            jax.ShapeDtypeStruct((TOK, 2048), bf16),
            jax.ShapeDtypeStruct((2, 8, 128), jnp.int32),
        ),
        in_specs=[HBM] * 7,
        out_specs=(HBM,) * 5,
        scratch_shapes=[
            pltpu.SemaphoreType.DMA((GATHER_COPIES,)),
            pltpu.SemaphoreType.DMA((GATHER_COPIES,)),
            pltpu.SemaphoreType.DMA((8,)),
        ],
        compiler_params=remote_params(1),
        name="gather",
    )(kw, vw, resp, prompt, q, og, info)


K_STEP = 1024


def swap_halves(a):
    return pltpu.roll(a, 64, 1)


def tables_of(info, d, cos, sin):
    start = info[d, 0, 3]
    late = pl.multiple_of(192 - start, 16)
    row = lax.broadcasted_iota(jnp.int32, (TOK, HEAD), 0)
    out = []
    for table in (cos, sin):
        first = table[pl.ds(192, TOK), :]
        second = table[pl.ds(late, TOK), :]
        out.append(jnp.concatenate([jnp.where(row < start, first, second), table[pl.ds(128, PRO), :]], 0))
    return out


def project_kernel(info, resp, prompt, XP, W, cos, sin, gain, XT, raw, keys, vals, pkv, turns, acc):
    step = pl.program_id(0)
    left = jnp.concatenate([resp[0], prompt[0], XP[...]], 0)
    right = jnp.concatenate([W[t] for t in range(4)], 1)
    part = jnp.dot(left, right, preferred_element_type=f32)
    XT[...] = left.T

    @pl.when(step == 0)
    def _():
        acc[...] = part

    @pl.when(step > 0)
    def _():
        acc[...] += part

    @pl.when(step == pl.num_programs(0) - 1)
    def _():
        for d in range(2):
            c, s = tables_of(info, d, cos, sin)
            turns[d, 0], turns[d, 1] = c, s
            core = info[d, 1, 0]
            for j in range(2):
                k = acc[pl.ds(d * DEV, DEV), pl.ds(j * HEAD, HEAD)]
                raw[j, d] = k
                square = jnp.mean(k * k, axis=1, keepdims=True)
                normed = k * lax.rsqrt(square + 1e-06) * gain[...]
                turned = (normed * c + swap_halves(normed) * s).astype(bf16)
                keys[j, d] = turned
                pkv[j, core] = turned[TOK:]
                v = acc[pl.ds(d * DEV, DEV), pl.ds((2 + j) * HEAD, HEAD)].astype(bf16)
                vals[j, d] = v
                pkv[2 + j, core] = v[TOK:]


def project(info, resp, prompt, XP, W, cos, sin, gain):
    return pl.pallas_call(
        project_kernel,
        out_shape=(
            jax.ShapeDtypeStruct((WIDTH, 2 * DEV), bf16),
            jax.ShapeDtypeStruct((2, 2, DEV, HEAD), f32),
            jax.ShapeDtypeStruct((2, 2, DEV, HEAD), bf16),
            jax.ShapeDtypeStruct((2, 2, DEV, HEAD), bf16),
            jax.ShapeDtypeStruct((4, 2, PRO, HEAD), bf16),
            jax.ShapeDtypeStruct((2, 2, DEV, HEAD), f32),
        ),
        grid=(WIDTH // K_STEP,),
        in_specs=[
            SMEM,
            pl.BlockSpec((1, TOK, K_STEP), lambda i: (0, 0, i)),
            pl.BlockSpec((1, PRO, K_STEP), lambda i: (0, 0, i)),
            pl.BlockSpec((DEV, K_STEP), lambda i: (0, i)),
            pl.BlockSpec((4, K_STEP, HEAD), lambda i: (0, i, 0)),
            VMEM,
            VMEM,
            VMEM,
        ],
        out_specs=(pl.BlockSpec((K_STEP, 2 * DEV), lambda i: (i, 0)),) + (VMEM,) * 5,
        scratch_shapes=[pltpu.VMEM((2 * DEV, 512), f32)],
        compiler_params=LOCAL,
        name="project",
    )(info, resp, prompt, XP, W, cos, sin, gain)


SHARE_COPIES = 8


def share_kernel(pkv, everyone, send, recv, local):
    me = Place()
    ring = me.ring_zh()
    greet(ring[1:])
    links = Links(send, recv)
    own = pltpu.make_async_copy(pkv, everyone.at[me.zh], local)
    own.start()
    going = Gather4(
        links, ring, lambda c: everyone.at[c], lambda c, h: everyone.at[c, pl.ds(2 * h, 2)], pkv
    )
    going.begin()
    going.forward()
    going.finish()
    own.wait()
    links.drain()


def share(pkv):
    return pl.pallas_call(
        share_kernel,
        out_shape=jax.ShapeDtypeStruct((4, 4, 2, PRO, HEAD), bf16),
        in_specs=[VMEM],
        out_specs=VMEM,
        scratch_shapes=[
            pltpu.SemaphoreType.DMA((SHARE_COPIES,)),
            pltpu.SemaphoreType.DMA((SHARE_COPIES,)),
            pltpu.SemaphoreType.DMA,
        ],
        compiler_params=remote_params(2),
        name="share",
    )(pkv)


def attention_kernel(info, everyone, keys, vals, Q, OG, QP, OP, QG, RG, PP, probs, slopes, queries, cots, parts):
    d, j = pl.program_id(0), pl.program_id(1)

    @pl.when((d == 0) & (j == 0))
    def _():
        parts[...] = jnp.zeros_like(parts)

    slots = [info[d, 0, 0], info[d, 0, 1]]
    start, lens = info[d, 0, 3], [info[d, 0, 4], info[d, 0, 5]]
    places = [(lax.div(s, 2), lax.rem(s, 2)) for s in slots]
    K = jnp.concatenate([everyone[zh, j, c] for zh, c in places] + [keys[0, 0, :TOK]], 0)
    V = jnp.concatenate([everyone[zh, 2 + j, c] for zh, c in places] + [vals[0, 0, :TOK]], 0)

    key = lax.broadcasted_iota(jnp.int32, (2 * TOK, TOK), 0)
    row = lax.broadcasted_iota(jnp.int32, (2 * TOK, TOK), 1)
    late = row >= start
    first = jnp.where(late, start, 0)
    end = jnp.where(late, start + lens[1], lens[0])
    from_key = jnp.where(key < TOK, jnp.where(late, PRO, 0), first + TOK)
    to_key = jnp.where(key < TOK, jnp.where(late, TOK, PRO), jnp.minimum(end, row + 1) + TOK)
    allowed = (key >= from_key) & (key < to_key)
    line = lax.broadcasted_iota(jnp.int32, (TOK, HEAD), 0)
    used = line < jnp.where(line >= start, start + lens[1], lens[0])

    def stack(q, og):
        for h in range(8):
            lanes = pl.ds(h * HEAD, HEAD)
            block = pl.ds(h * TOK, TOK)
            queries[block, :] = q[:, lanes]
            cots[block, :] = jnp.where(used, og[:, lanes].astype(f32), 0.0).astype(bf16)

    pl.when(d == 0)(lambda: stack(Q.at[0], OG.at[0]))
    pl.when(d == 1)(lambda: stack(QP, OP))
    for h in range(8):
        lanes = pl.ds(h * HEAD, HEAD)
        block = pl.ds(h * TOK, TOK)
        q, cot = queries[block, :], cots[block, :]
        scores = lax.dot_general(K, q, (((1,), (1,)), ((), ())), preferred_element_type=f32)
        scores = jnp.where(allowed, scores * SCALE, -1e30)
        top = jnp.max(scores, axis=0, keepdims=True)
        weights = jnp.exp(scores - top)
        prob = weights / jnp.sum(weights, axis=0, keepdims=True)
        probs[:, block] = prob.astype(bf16)
        slope = lax.dot_general(V, cot, (((1,), (1,)), ((), ())), preferred_element_type=f32)
        slope = slope.astype(bf16).astype(f32)
        inner = jnp.sum(slope * prob, axis=0, keepdims=True)
        back = (prob * (slope - inner) * SCALE).astype(bf16)
        slopes[:, block] = back
        QG[0, :, lanes] = lax.dot_general(
            back, K, (((0,), (0,)), ((), ())), preferred_element_type=f32
        ).astype(bf16)
    dv = jnp.dot(probs[...], cots[...], preferred_element_type=f32)
    dk = jnp.dot(slopes[...], queries[...], preferred_element_type=f32)
    RG[0, 0, 0] = dk[TOK:].astype(bf16)
    RG[0, 0, 1] = dv[TOK:].astype(bf16)
    for s, (zh, c) in enumerate(places):
        parts[zh, j, c] += dk[s * PRO : (s + 1) * PRO]
        parts[zh, 2 + j, c] += dv[s * PRO : (s + 1) * PRO]

    @pl.when((d == 1) & (j == 1))
    def _():
        PP[...] = parts[...].astype(bf16)


def attention(info, everyone, keys, vals, Q, OG, QP, OP):
    own = pl.BlockSpec((1, TOK, 1024), lambda d, j, info: (0, 0, info[0, 1, 0] * 2 + jnp.maximum(d, j)))
    theirs = pl.BlockSpec((TOK, 1024), lambda d, j, info: (0, d * j))
    here = pl.BlockSpec((1, 1, DEV, HEAD), lambda d, j, info: (j, d, 0, 0))
    return pl.pallas_call(
        attention_kernel,
        out_shape=(
            jax.ShapeDtypeStruct((2, TOK, 2048), bf16),
            jax.ShapeDtypeStruct((2, 2, 2, TOK, HEAD), bf16),
            jax.ShapeDtypeStruct((4, 4, 2, PRO, HEAD), bf16),
        ),
        grid_spec=pltpu.PrefetchScalarGridSpec(
            num_scalar_prefetch=1,
            grid=(2, 2),
            in_specs=[VMEM, here, here, own, own, theirs, theirs],
            out_specs=(
                pl.BlockSpec((1, TOK, 1024), lambda d, j, info: (d, 0, j)),
                pl.BlockSpec((1, 1, 2, TOK, HEAD), lambda d, j, info: (j, d, 0, 0, 0)),
                VMEM,
            ),
            scratch_shapes=[
                pltpu.VMEM((256, 1024), bf16),
                pltpu.VMEM((256, 1024), bf16),
                pltpu.VMEM((1024, HEAD), bf16),
                pltpu.VMEM((1024, HEAD), bf16),
                pltpu.VMEM((4, 4, 2, PRO, HEAD), f32),
            ],
        ),
        compiler_params=LOCAL,
        name="attention",
    )(info, everyone, keys, vals, Q, OG, QP, OP)


RETURN_COPIES = 8


def return_kernel(PP, QG, PS, QO, land, send, recv):
    me = Place()
    ring, partner = me.ring_zh(), me.partner()
    greet([ring[1], ring[2], partner])
    links = Links(send, recv)

    def add(dst, terms):
        for i in range(2):
            for d in range(2):
                total = terms[0][i, d].astype(f32)
                for term in terms[1:]:
                    total = total + term[i, d].astype(f32)
                dst[i, d] = total.astype(dst.dtype)

    going = Reduce4(
        links, ring, lambda c, h: PP.at[c, pl.ds(2 * h, 2)], lambda i: land.at[i], add
    )
    going.begin()
    queries = links.take()
    links.start(queries, QG.at[1], QO, partner)
    going.mid()
    going.finish(lambda h: PS.at[pl.ds(2 * h, 2)])
    links.arrived(queries, QO, partner)
    links.drain()


def give_back(PP, QG):
    return pl.pallas_call(
        return_kernel,
        out_shape=(
            jax.ShapeDtypeStruct((4, 2, PRO, HEAD), f32),
            jax.ShapeDtypeStruct((TOK, 2048), bf16),
        ),
        in_specs=[VMEM, HBM],
        out_specs=(VMEM, HBM),
        scratch_shapes=[
            pltpu.VMEM((6, 2, 2, PRO, HEAD), bf16),
            pltpu.SemaphoreType.DMA((RETURN_COPIES,)),
            pltpu.SemaphoreType.DMA((RETURN_COPIES,)),
        ],
        compiler_params=remote_params(3),
        name="give_back",
    )(PP, QG)


SUM_COPIES = 64
I_STEP = 640


def sum_kernel(
    raw, RG, PS, turns, gain, XT, W,
    IG, WG,
    xt, w, w2, grads, theirs, D, one, acc1, two, acc2, near, acc3, three, wg, send, recv, local,
):
    me = Place()
    partner = me.partner()
    near_minus, near_plus = me.near_z()
    ring_x, ring_y, ring_zh = me.ring_x(), me.ring_y(), me.ring_zh()
    fetch = pltpu.make_async_copy(XT, xt, local.at[0])
    fetch.start()
    weights = pltpu.make_async_copy(W, w, local.at[1])
    weights.start()
    greet([*ring_x[1:], *ring_y[1:], *ring_zh[1:], near_minus, near_plus, partner])
    links = Links(send, recv)
    core, zl = me.core, me.zl
    swapped = links.take()
    links.start(swapped, W, w2, partner)

    for d in range(2):
        c, s = turns[d, 0], turns[d, 1]
        whose = core if d == 0 else 1 - core
        rows = pl.ds(d * DEV, DEV)
        for j in range(2):
            cot = jnp.concatenate([RG[j, d, 0].astype(f32), PS[j, whose]], 0)
            turned = (cot * c + swap_halves(cot * s)) * gain[...]
            k = raw[j, d]
            inverse = lax.rsqrt(jnp.mean(k * k, axis=1, keepdims=True) + 1e-06)
            along = jnp.mean(k * turned, axis=1, keepdims=True)
            back = inverse * turned - k * (inverse * inverse * inverse * along)
            grads[rows, pl.ds(j * HEAD, HEAD)] = back.astype(bf16)
            values = jnp.concatenate([RG[j, d, 1], PS[2 + j, whose].astype(bf16)], 0)
            grads[rows, pl.ds((2 + j) * HEAD, HEAD)] = values
    crossed = links.take()
    links.start(crossed, grads.at[pl.ds(DEV, DEV)], theirs, partner)
    fetch.wait()

    def term(y, x, kind):
        rows = pl.ds(pl.multiple_of((y * 4 + x) * 320, 320), 320)
        made = jnp.dot(
            xt[rows, :], grads[:, pl.ds(kind * 256, 256)], preferred_element_type=f32
        ).astype(bf16)
        for j in range(2):
            for h in range(2):
                D[2 * kind + j, y, x, h] = made[h * ROWS : (h + 1) * ROWS, j * HEAD : (j + 1) * HEAD]

    def terms_for(kind, place):
        def body(i, carry):
            if kind == 0:
                term(i, place, 0)
            else:
                term(place, i, 1)
            return carry

        lax.fori_loop(0, 4, body, 0)

    def input_part(i):
        rows = pl.ds(pl.multiple_of(i * I_STEP, I_STEP), I_STEP)
        total = 0.0
        for left, right in ((grads[pl.ds(0, DEV), :], w), (theirs[...], w2)):
            both = jnp.concatenate([right[t, rows, :] for t in range(4)], 1)
            total = total + lax.dot_general(
                left, both, (((1,), (1,)), ((), ())), preferred_element_type=f32
            )
        IG[:, rows] = total.astype(bf16)

    def input_parts(begin, end):
        def body(i, carry):
            input_part(i)
            return carry

        lax.fori_loop(begin, end, body, 0)

    first, second = [], []
    for t in range(4):
        if t < 2:
            part = lambda c, h, t=t: D.at[t, :, c, h]
        else:
            part = lambda c, h, t=t: D.at[t, c, :, h]
        ring = ring_x if t < 2 else ring_y
        other = ring_y if t < 2 else ring_x
        first.append(Reduce4(links, ring, part, lambda i, t=t: one.at[t, i], add_blocks))
        second.append(
            Reduce4(
                links,
                other,
                lambda c, h, t=t: acc1.at[t, c, h],
                lambda i, t=t: two.at[t, i],
                add_block,
            )
        )
    for place in (2, 1, 3, 0):
        for kind, at in ((0, me.x), (1, me.y)):
            terms_for(kind, lax.rem(at + place, 4))
            for t in (2 * kind, 2 * kind + 1):
                first[t].send_for(place)
    order = (0, 2, 1, 3)
    weights.wait()
    links.arrived(crossed, theirs, partner)
    links.arrived(swapped, w2, partner)
    for t in order[:2]:
        first[t].mid()
    input_parts(0, 2)
    for t in order[2:]:
        first[t].mid()
    input_parts(2, 5)
    for t in order:
        first[t].finish(lambda h, t=t: acc1.at[t, :, h])
        second[t].begin()
        if t == 2:
            input_parts(5, 6)
    for t in order:
        second[t].mid()
    input_parts(6, 7)
    for t in order:
        second[t].finish(lambda h, t=t: acc2.at[t, h])

    up, down = links.take(), links.take()
    links.start(up, acc2.at[:, 1 - zl, pl.ds(0, HALF)], near.at[0], near_plus)
    links.start(down, acc2.at[:, 1 - zl, pl.ds(HALF, HALF)], near.at[1], near_minus)
    input_parts(7, 8)
    links.arrived(up, near.at[0], near_plus)
    add_blocks(acc3.at[:, 0], [acc2.at[:, zl, pl.ds(0, HALF)], near.at[0]])
    links.arrived(down, near.at[1], near_minus)
    add_blocks(acc3.at[:, 1], [acc2.at[:, zl, pl.ds(HALF, HALF)], near.at[1]])

    third = Reduce4(links, ring_zh, lambda c, h: acc3.at[c, h], lambda i: three.at[i], add_block)
    third.begin()
    third.mid()
    third.finish(lambda h: wg.at[core, me.zh, h])
    last = Gather4(links, ring_zh, lambda c: wg.at[core, c], lambda c, h: wg.at[core, c, h])
    last.begin()
    last.forward()
    last.finish()
    across = links.take()
    links.start(across, wg.at[core], wg.at[core], partner)
    links.arrived(across, wg.at[1 - core], partner)
    WG[...] = wg[...]
    links.drain()
    assert links.used <= SUM_COPIES


def sum_terms(raw, RG, PS, turns, gain, XT, W):
    return pl.pallas_call(
        sum_kernel,
        out_shape=(
            jax.ShapeDtypeStruct((DEV, WIDTH), bf16),
            jax.ShapeDtypeStruct((2, 4, 2, HALF, HEAD), bf16),
        ),
        in_specs=[VMEM] * 5 + [HBM] * 2,
        out_specs=(VMEM, VMEM),
        scratch_shapes=[
            pltpu.VMEM((WIDTH, 2 * DEV), bf16),
            pltpu.VMEM((4, WIDTH, HEAD), bf16),
            pltpu.VMEM((4, WIDTH, HEAD), bf16),
            pltpu.VMEM((2 * DEV, 512), bf16),
            pltpu.VMEM((DEV, 512), bf16),
            pltpu.VMEM((4, 4, 4, 2, ROWS, HEAD), bf16),
            pltpu.VMEM((4, 6, 4, ROWS, HEAD), bf16),
            pltpu.VMEM((4, 4, 2, ROWS, HEAD), bf16),
            pltpu.VMEM((4, 6, ROWS, HEAD), bf16),
            pltpu.VMEM((4, 2, ROWS, HEAD), bf16),
            pltpu.VMEM((2, 4, HALF, HEAD), bf16),
            pltpu.VMEM((4, 2, HALF, HEAD), bf16),
            pltpu.VMEM((6, HALF, HEAD), bf16),
            pltpu.VMEM((2, 4, 2, HALF, HEAD), bf16),
            pltpu.SemaphoreType.DMA((SUM_COPIES,)),
            pltpu.SemaphoreType.DMA((SUM_COPIES,)),
            pltpu.SemaphoreType.DMA((2,)),
        ],
        compiler_params=remote_params(4),
        name="sum_terms",
    )(raw, RG, PS, turns, gain, XT, W)


def put_kernel(info, IG, WG, QG, QO, resp, prompt, qgrad, kout, vout):
    step = pl.program_id(0)
    core = info[0, 1, 0]
    resp[0] = IG[:TOK]
    prompt[0] = IG[TOK:]

    @pl.when(step == core)
    def _():
        qgrad[0] = QG[0]

    @pl.when(step != core)
    def _():
        qgrad[0] = QO[...]

    @pl.when(step == 0)
    def _():
        for c in range(2):
            for j in range(2):
                lanes = pl.ds((2 * c + j) * HEAD, HEAD)
                kout[:, lanes] = WG[c, j]
                vout[:, lanes] = WG[c, 2 + j]


def put(info, IG, WG, QG, QO):
    half = WIDTH // 2
    return pl.pallas_call(
        put_kernel,
        out_shape=(
            jax.ShapeDtypeStruct((1, TOK, WIDTH), bf16),
            jax.ShapeDtypeStruct((1, PRO, WIDTH), bf16),
            jax.ShapeDtypeStruct((1, TOK, 4096), bf16),
            jax.ShapeDtypeStruct((ROWS, 512), bf16),
            jax.ShapeDtypeStruct((ROWS, 512), bf16),
        ),
        grid=(2,),
        in_specs=[
            SMEM,
            pl.BlockSpec((DEV, half), lambda i: (0, i)),
            VMEM,
            pl.BlockSpec((1, TOK, 2048), lambda i: (0, 0, 0)),
            VMEM,
        ],
        out_specs=(
            pl.BlockSpec((1, TOK, half), lambda i: (0, 0, i)),
            pl.BlockSpec((1, PRO, half), lambda i: (0, 0, i)),
            pl.BlockSpec((1, TOK, 2048), lambda i: (0, 0, i)),
            VMEM,
            VMEM,
        ),
        compiler_params=LOCAL,
        name="put",
    )(info, IG, WG, QG, QO)


def local(
    queries, out_grad, resp_in, prompt_in, key_matrix, value_matrix, key_gain, seg_prompt, seg_start, seg_len, owner
):
    cos, sin = rotary_tables()
    gain = key_gain.reshape(1, HEAD)
    match = seg_prompt[0][:, None] == jnp.arange(8, dtype=jnp.int32)[None, :]
    slots = jnp.sum(jnp.where(match, owner[0][None, :], 0), 1)
    line = jnp.concatenate([slots, seg_start[0], seg_len[0], jnp.zeros((122,), jnp.int32)])
    core = lax.rem(lax.axis_index("grp"), 2).astype(jnp.int32)
    info = jnp.concatenate([line[None], jnp.broadcast_to(core, (7, 128))], 0)

    W, XP, QP, OP, both = gather(key_matrix, value_matrix, resp_in, prompt_in, queries, out_grad, info)
    flat = W.reshape(4, WIDTH, HEAD)
    XT, raw, keys, vals, pkv, turns = project(both, resp_in, prompt_in, XP, flat, cos, sin, gain)
    everyone = share(pkv)
    QG, RG, PP = attention(both, everyone, keys, vals, queries, out_grad, QP, OP)
    PS, QO = give_back(PP, QG)
    IG, WG = sum_terms(raw, RG, PS, turns, gain, XT, flat)
    resp, prompt, qgrad, kout, vout = put(both, IG, WG.reshape(2, 4, ROWS, HEAD), QG, QO)
    return qgrad, resp, prompt, kout, vout


def solution(mesh):
    in_specs = (
        P("fsdp", "grp", None),
        P("fsdp", "grp", None),
        P("fsdp", "grp", None),
        P("fsdp", "grp", None),
        P("fsdp", None),
        P("fsdp", None),
        P(),
        P("fsdp", "grp"),
        P("fsdp", "grp"),
        P("fsdp", "grp"),
        P("fsdp", None),
    )
    out_specs = (
        P("fsdp", "grp", None),
        P("fsdp", "grp", None),
        P("fsdp", "grp", None),
        P("fsdp", None),
        P("fsdp", None),
    )
    return jax.shard_map(local, mesh=mesh, in_specs=in_specs, out_specs=out_specs, check_vma=False)
```

```python
import functools
import math

import jax
import jax.numpy as jnp
import numpy as np
from jax import lax
from jax.experimental import pallas as pl
from jax.experimental.pallas import tpu as pltpu
from jax.sharding import PartitionSpec as P

MESH = pl.DeviceIdType.MESH
HBM = pl.BlockSpec(memory_space=pltpu.HBM)
SMEM = pl.BlockSpec(memory_space=pltpu.SMEM)
VMEM = pl.BlockSpec(memory_space=pltpu.VMEM)
VMEM_LIMIT = 60 * 1024 * 1024

WIDTH = 5120
HEAD = 128
ROWS = 160
HALF = 80
TOK = 128
PRO = 64
DEV = TOK + PRO
SCALE = 1.0 / math.sqrt(HEAD)
BASE = 1000000.0
bf16 = jnp.bfloat16
f32 = jnp.float32


def rotary_tables():
    frequency = np.float32(BASE) ** (-np.arange(64, dtype=np.float32) / np.float32(64))
    angles = np.arange(-128, 192, dtype=np.float32)[:, None] * frequency[None, :].astype(np.float32)
    angles = angles.astype(np.float32).astype(np.float64)
    cos, sin = np.cos(angles), np.sin(angles)
    return (
        np.concatenate([cos, cos], 1).astype(np.float32),
        np.concatenate([-sin, sin], 1).astype(np.float32),
    )


class Place:
    def __init__(self):
        g, f = lax.axis_index("grp"), lax.axis_index("fsdp")
        self.core, self.zh = lax.rem(g, 2), lax.div(g, 2)
        self.zl = lax.rem(f, 2)
        self.x = lax.rem(lax.div(f, 2), 4)
        self.y = lax.div(f, 8)
        self.z = self.zh * 2 + self.zl

    def at(self, y=None, x=None, z=None, core=None):
        y = self.y if y is None else y
        x = self.x if x is None else x
        z = self.z if z is None else z
        core = self.core if core is None else core
        return {"grp": lax.div(z, 2) * 2 + core, "fsdp": (y * 4 + x) * 2 + lax.rem(z, 2)}

    def ring_x(self):
        return self.x, self.at(x=lax.rem(self.x + 3, 4)), self.at(x=lax.rem(self.x + 1, 4))

    def ring_y(self):
        return self.y, self.at(y=lax.rem(self.y + 3, 4)), self.at(y=lax.rem(self.y + 1, 4))

    def ring_zh(self):
        return self.zh, self.at(z=lax.rem(self.z + 6, 8)), self.at(z=lax.rem(self.z + 2, 8))

    def near_z(self):
        return self.at(z=lax.rem(self.z + 7, 8)), self.at(z=lax.rem(self.z + 1, 8))

    def partner(self):
        return self.at(core=1 - self.core)


def greet(devices):
    barrier = pltpu.get_barrier_semaphore()
    for device in devices:
        pl.semaphore_signal(barrier, inc=1, device_id=device, device_id_type=MESH)
    pl.semaphore_wait(barrier, len(devices))


class Links:
    def __init__(self, send, recv):
        self.send, self.recv, self.used, self.sent = send, recv, 0, []

    def take(self):
        self.used += 1
        return self.used - 1

    def copy(self, number, src, dst, device):
        return pltpu.make_async_remote_copy(
            src_ref=src,
            dst_ref=dst,
            send_sem=self.send.at[number],
            recv_sem=self.recv.at[number],
            device_id=device,
            device_id_type=MESH,
        )

    def start(self, number, src, dst, device):
        made = self.copy(number, src, dst, device)
        made.start()
        self.sent.append(made)

    def arrived(self, number, dst, device):
        self.copy(number, dst, dst, device).wait_recv()

    def drain(self):
        for made in self.sent:
            made.wait_send()
        self.sent = []


class Gather4:
    def __init__(self, links, ring, view, half, own=None):
        self.links, self.view, self.half = links, view, half
        self.me, self.minus, self.plus = ring
        self.own = view(self.me) if own is None else own
        self.n = [links.take() for _ in range(4)]

    def begin(self):
        self.links.start(self.n[0], self.own, self.view(self.me), self.plus)
        self.links.start(self.n[1], self.own, self.view(self.me), self.minus)

    def forward(self):
        left, right = lax.rem(self.me + 3, 4), lax.rem(self.me + 1, 4)
        self.links.arrived(self.n[0], self.view(left), self.plus)
        self.links.start(self.n[2], self.half(left, 0), self.half(left, 0), self.plus)
        self.links.arrived(self.n[1], self.view(right), self.minus)
        self.links.start(self.n[3], self.half(right, 1), self.half(right, 1), self.minus)

    def finish(self):
        across = lax.rem(self.me + 2, 4)
        self.links.arrived(self.n[2], self.half(across, 0), self.plus)
        self.links.arrived(self.n[3], self.half(across, 1), self.minus)


class Reduce4:
    def __init__(self, links, ring, part, slot, add):
        self.links, self.part, self.slot, self.add = links, part, slot, add
        self.me, self.minus, self.plus = ring
        self.n = [links.take() for _ in range(6)]

    def send_for(self, place):
        part, slot, n = self.part, self.slot, self.n
        block = lax.rem(self.me + place, 4)
        if place == 2:
            self.links.start(n[0], part(block, 0), slot(0), self.plus)
            self.links.start(n[1], part(block, 1), slot(1), self.minus)
        if place == 1:
            self.links.start(n[2], part(block, 1), slot(2), self.plus)
        if place == 3:
            self.links.start(n[3], part(block, 0), slot(3), self.minus)

    def begin(self):
        for place in (2, 1, 3):
            self.send_for(place)

    def mid(self):
        left, right = lax.rem(self.me + 3, 4), lax.rem(self.me + 1, 4)
        part, slot, n = self.part, self.slot, self.n
        self.links.arrived(n[0], slot(0), self.plus)
        self.add(slot(0), [slot(0), part(right, 0)])
        self.links.start(n[4], slot(0), slot(4), self.plus)
        self.links.arrived(n[1], slot(1), self.minus)
        self.add(slot(1), [slot(1), part(left, 1)])
        self.links.start(n[5], slot(1), slot(5), self.minus)

    def finish(self, out):
        part, slot, n = self.part, self.slot, self.n
        self.links.arrived(n[3], slot(3), self.minus)
        self.links.arrived(n[4], slot(4), self.plus)
        self.add(out(0), [part(self.me, 0), slot(3), slot(4)])
        self.links.arrived(n[2], slot(2), self.plus)
        self.links.arrived(n[5], slot(5), self.minus)
        self.add(out(1), [part(self.me, 1), slot(2), slot(5)])


def add_block(dst, terms):
    total = terms[0][...].astype(f32)
    for term in terms[1:]:
        total = total + term[...].astype(f32)
    dst[...] = total.astype(dst.dtype)


def add_blocks(dst, terms):
    def body(i, carry):
        total = terms[0][i].astype(f32)
        for term in terms[1:]:
            total = total + term[i].astype(f32)
        dst[i] = total.astype(dst.dtype)
        return carry

    lax.fori_loop(0, dst.shape[0], body, 0)


def remote_params(number):
    return pltpu.CompilerParams(
        collective_id=number, has_side_effects=True, vmem_limit_bytes=VMEM_LIMIT
    )


LOCAL = pltpu.CompilerParams(vmem_limit_bytes=VMEM_LIMIT)


GATHER_COPIES = 64


def gather_kernel(kw, vw, resp, prompt, q, og, sp, ss, sl, W, XP, QP, OP, SP, SS, SL, send, recv, local):
    me = Place()
    core, partner = me.core, me.partner()
    near_minus, near_plus = me.near_z()
    _, xm, xp = me.ring_x()
    _, ym, yp = me.ring_y()
    greet([xm, xp, ym, yp, near_minus, near_plus, partner])
    links = Links(send, recv)

    def columns(matrix, j):
        return matrix.at[:, pl.ds(pl.multiple_of((core * 2 + j) * HEAD, HEAD), HEAD)]

    own = [columns(kw, 0), columns(kw, 1), columns(vw, 0), columns(vw, 1)]
    x, y, zl = me.x, me.y, me.zl
    rows = lambda h: pl.ds(h * HALF, HALF)

    ax = Gather4(links, me.ring_x(), lambda c: W.at[0, y, c, zl], lambda c, h: W.at[0, y, c, zl, rows(h)], own[0])
    ay = Gather4(links, me.ring_y(), lambda c: W.at[0, c, :, zl], lambda c, h: W.at[0, c, :, zl, rows(h)])
    by = Gather4(links, me.ring_y(), lambda c: W.at[1, c, x, zl], lambda c, h: W.at[1, c, x, zl, rows(h)], own[1])
    bx = Gather4(links, me.ring_x(), lambda c: W.at[1, :, c, zl], lambda c, h: W.at[1, :, c, zl, rows(h)])
    cx = Gather4(links, me.ring_x(), lambda c: W.at[2, y, c], lambda c, h: W.at[2, y, c, h])
    cy = Gather4(links, me.ring_y(), lambda c: W.at[2, c], lambda c, h: W.at[2, c, :, h])
    dy = Gather4(links, me.ring_y(), lambda c: W.at[3, c, x], lambda c, h: W.at[3, c, x, h])
    dx = Gather4(links, me.ring_x(), lambda c: W.at[3, :, c], lambda c, h: W.at[3, :, c, h])

    zn = {}

    def z_view(t, place, which, h):
        if t == 0:
            return W.at[0, lax.rem(y + place, 4), :, which, rows(h)]
        if t == 1:
            return W.at[1, :, lax.rem(x + place, 4), which, rows(h)]
        return W.at[t, y, x, which, rows(h)]

    def z_begin(t, place, src=None):
        zn[t, place] = links.take(), links.take()
        for h, device in ((0, near_plus), (1, near_minus)):
            view = z_view(t, place, zl, h)
            links.start(zn[t, place][h], view if src is None else src(h), view, device)

    def z_finish(t, place):
        for h, device in ((0, near_plus), (1, near_minus)):
            links.arrived(zn[t, place][h], z_view(t, place, 1 - zl, h), device)

    ax.begin()
    by.begin()
    for t in (2, 3):
        matrix_half = lambda h, t=t: vw.at[rows(h), pl.ds(pl.multiple_of((core * 2 + t - 2) * HEAD, HEAD), HEAD)]
        z_begin(t, 0, matrix_half)

    locals_ = []

    def here(src, dst):
        made = pltpu.make_async_copy(src, dst, local.at[len(locals_)])
        made.start()
        locals_.append(made)

    for t in range(4):
        here(own[t], W.at[t, y, x, zl])
    swaps = []

    def swap(src, dst):
        number = links.take()
        links.start(number, src, dst, partner)
        swaps.append((number, dst))

    theirs = pl.ds(pl.multiple_of((1 - core) * 2048, 2048), 2048)
    swap(sp, SP)
    swap(ss, SS)
    swap(sl, SL)
    swap(resp.at[0], XP.at[pl.ds(0, TOK)])
    swap(prompt.at[0], XP.at[pl.ds(TOK, PRO)])
    swap(q.at[0, :, theirs], QP)
    swap(og.at[0, :, theirs], OP)

    ax.forward()
    by.forward()
    for made in locals_:
        made.wait()
    z_finish(2, 0)
    cx.begin()
    z_finish(3, 0)
    dy.begin()
    ax.finish()
    ay.begin()
    z_begin(0, 0)
    by.finish()
    bx.begin()
    z_begin(1, 0)
    cx.forward()
    dy.forward()
    cx.finish()
    cy.begin()
    dy.finish()
    dx.begin()
    ay.forward()
    z_begin(0, 3)
    z_begin(0, 1)
    bx.forward()
    z_begin(1, 3)
    z_begin(1, 1)
    ay.finish()
    z_begin(0, 2)
    bx.finish()
    z_begin(1, 2)
    cy.forward()
    dx.forward()
    for place in range(4):
        z_finish(0, place)
        z_finish(1, place)
    cy.finish()
    dx.finish()
    for number, landing in swaps:
        links.arrived(number, landing, partner)
    links.drain()
    assert links.used <= GATHER_COPIES


def gather(kw, vw, resp, prompt, q, og, sp, ss, sl):
    return pl.pallas_call(
        gather_kernel,
        out_shape=(
            jax.ShapeDtypeStruct((4, 4, 4, 2, ROWS, HEAD), bf16),
            jax.ShapeDtypeStruct((DEV, WIDTH), bf16),
            jax.ShapeDtypeStruct((TOK, 2048), bf16),
            jax.ShapeDtypeStruct((TOK, 2048), bf16),
            jax.ShapeDtypeStruct((1, 2), jnp.int32),
            jax.ShapeDtypeStruct((1, 2), jnp.int32),
            jax.ShapeDtypeStruct((1, 2), jnp.int32),
        ),
        in_specs=[HBM] * 9,
        out_specs=(HBM,) * 7,
        scratch_shapes=[
            pltpu.SemaphoreType.DMA((GATHER_COPIES,)),
            pltpu.SemaphoreType.DMA((GATHER_COPIES,)),
            pltpu.SemaphoreType.DMA((4,)),
        ],
        compiler_params=remote_params(1),
        name="gather",
    )(kw, vw, resp, prompt, q, og, sp, ss, sl)


K_STEP = 1024


def swap_halves(a):
    return pltpu.roll(a, 64, 1)


def tables_of(starts, cos, sin):
    start = starts[0, 1]
    late = pl.multiple_of(192 - start, 16)
    row = lax.broadcasted_iota(jnp.int32, (TOK, HEAD), 0)
    out = []
    for table in (cos, sin):
        first = table[pl.ds(192, TOK), :]
        second = table[pl.ds(late, TOK), :]
        out.append(jnp.concatenate([jnp.where(row < start, first, second), table[pl.ds(128, PRO), :]], 0))
    return out


def project_kernel(ss, SS, resp, prompt, XP, W, cos, sin, gain, XT, raw, keys, vals, pkv, turns, acc):
    step = pl.program_id(0)
    left = jnp.concatenate([resp[0], prompt[0], XP[...]], 0)
    right = jnp.concatenate([W[t] for t in range(4)], 1)
    part = jnp.dot(left, right, preferred_element_type=f32)
    XT[...] = left.T

    @pl.when(step == 0)
    def _():
        acc[...] = part

    @pl.when(step > 0)
    def _():
        acc[...] += part

    @pl.when(step == pl.num_programs(0) - 1)
    def _():
        for d in range(2):
            c, s = tables_of((ss, SS)[d], cos, sin)
            turns[d, 0], turns[d, 1] = c, s
            core = lax.rem(lax.axis_index("grp") + d, 2)
            for j in range(2):
                k = acc[pl.ds(d * DEV, DEV), pl.ds(j * HEAD, HEAD)]
                raw[j, d] = k
                square = jnp.mean(k * k, axis=1, keepdims=True)
                normed = k * lax.rsqrt(square + 1e-06) * gain[...]
                turned = (normed * c + swap_halves(normed) * s).astype(bf16)
                keys[j, d] = turned
                pkv[j, core] = turned[TOK:]
                v = acc[pl.ds(d * DEV, DEV), pl.ds((2 + j) * HEAD, HEAD)].astype(bf16)
                vals[j, d] = v
                pkv[2 + j, core] = v[TOK:]


def project(ss, SS, resp, prompt, XP, W, cos, sin, gain):
    return pl.pallas_call(
        project_kernel,
        out_shape=(
            jax.ShapeDtypeStruct((WIDTH, 2 * DEV), bf16),
            jax.ShapeDtypeStruct((2, 2, DEV, HEAD), f32),
            jax.ShapeDtypeStruct((2, 2, DEV, HEAD), bf16),
            jax.ShapeDtypeStruct((2, 2, DEV, HEAD), bf16),
            jax.ShapeDtypeStruct((4, 2, PRO, HEAD), bf16),
            jax.ShapeDtypeStruct((2, 2, DEV, HEAD), f32),
        ),
        grid=(WIDTH // K_STEP,),
        in_specs=[
            SMEM,
            SMEM,
            pl.BlockSpec((1, TOK, K_STEP), lambda i: (0, 0, i)),
            pl.BlockSpec((1, PRO, K_STEP), lambda i: (0, 0, i)),
            pl.BlockSpec((DEV, K_STEP), lambda i: (0, i)),
            pl.BlockSpec((4, K_STEP, HEAD), lambda i: (0, i, 0)),
            VMEM,
            VMEM,
            VMEM,
        ],
        out_specs=(pl.BlockSpec((K_STEP, 2 * DEV), lambda i: (i, 0)),) + (VMEM,) * 5,
        scratch_shapes=[pltpu.VMEM((2 * DEV, 512), f32)],
        compiler_params=LOCAL,
        name="project",
    )(ss, SS, resp, prompt, XP, W, cos, sin, gain)


SHARE_COPIES = 8


def share_kernel(pkv, everyone, send, recv, local):
    me = Place()
    ring = me.ring_zh()
    greet(ring[1:])
    links = Links(send, recv)
    own = pltpu.make_async_copy(pkv, everyone.at[me.zh], local)
    own.start()
    going = Gather4(
        links, ring, lambda c: everyone.at[c], lambda c, h: everyone.at[c, pl.ds(2 * h, 2)], pkv
    )
    going.begin()
    going.forward()
    going.finish()
    own.wait()
    links.drain()


def share(pkv):
    return pl.pallas_call(
        share_kernel,
        out_shape=jax.ShapeDtypeStruct((4, 4, 2, PRO, HEAD), bf16),
        in_specs=[VMEM],
        out_specs=VMEM,
        scratch_shapes=[
            pltpu.SemaphoreType.DMA((SHARE_COPIES,)),
            pltpu.SemaphoreType.DMA((SHARE_COPIES,)),
            pltpu.SemaphoreType.DMA,
        ],
        compiler_params=remote_params(2),
        name="share",
    )(pkv)


def attention_kernel(
    sp, ss, sl, SP, SS, SL, owner, everyone, keys, vals, Q, OG, QP, OP,
    QG, RG, PP, probs, slopes, queries, cots, parts,
):
    d, j = pl.program_id(0), pl.program_id(1)

    @pl.when((d == 0) & (j == 0))
    def _():
        parts[...] = jnp.zeros_like(parts)

    def number(own, other, i):
        return jnp.where(d == 0, own[0, i], other[0, i])

    slots = [owner[0, number(sp, SP, i)] for i in range(2)]
    start, lens = number(ss, SS, 1), [number(sl, SL, i) for i in range(2)]
    places = [(lax.div(s, 2), lax.rem(s, 2)) for s in slots]
    K = jnp.concatenate([everyone[zh, j, c] for zh, c in places] + [keys[0, 0, :TOK]], 0)
    V = jnp.concatenate([everyone[zh, 2 + j, c] for zh, c in places] + [vals[0, 0, :TOK]], 0)

    key = lax.broadcasted_iota(jnp.int32, (2 * TOK, TOK), 0)
    row = lax.broadcasted_iota(jnp.int32, (2 * TOK, TOK), 1)
    late = row >= start
    first = jnp.where(late, start, 0)
    end = jnp.where(late, start + lens[1], lens[0])
    from_key = jnp.where(key < TOK, jnp.where(late, PRO, 0), first + TOK)
    to_key = jnp.where(key < TOK, jnp.where(late, TOK, PRO), jnp.minimum(end, row + 1) + TOK)
    bias = jnp.where((key >= from_key) & (key < to_key), 0.0, -1e30)
    bias = jnp.concatenate([bias, bias], 1)
    line = lax.broadcasted_iota(jnp.int32, (TOK, HEAD), 0)
    used = line < jnp.where(line >= start, start + lens[1], lens[0])

    def stack(q, og):
        for h in range(8):
            lanes = pl.ds(h * HEAD, HEAD)
            block = pl.ds(h * TOK, TOK)
            queries[block, :] = q[:, lanes]
            cots[block, :] = jnp.where(used, og[:, lanes].astype(f32), 0.0).astype(bf16)

    pl.when(d == 0)(lambda: stack(Q.at[0], OG.at[0]))
    pl.when(d == 1)(lambda: stack(QP, OP))
    for pair in range(4):
        block = pl.ds(pair * 2 * TOK, 2 * TOK)
        q, cot = queries[block, :], cots[block, :]
        scores = lax.dot_general(K, q, (((1,), (1,)), ((), ())), preferred_element_type=f32)
        scores = scores * SCALE + bias
        top = jnp.max(scores, axis=0, keepdims=True)
        weights = jnp.exp(scores - top)
        prob = weights * (1.0 / jnp.sum(weights, axis=0, keepdims=True))
        probs[:, block] = prob.astype(bf16)
        slope = lax.dot_general(V, cot, (((1,), (1,)), ((), ())), preferred_element_type=f32)
        slope = slope.astype(bf16).astype(f32)
        inner = jnp.sum(slope * prob, axis=0, keepdims=True)
        back = (prob * ((slope - inner) * SCALE)).astype(bf16)
        slopes[:, block] = back
        made = lax.dot_general(
            back, K, (((0,), (0,)), ((), ())), preferred_element_type=f32
        ).astype(bf16)
        for i in range(2):
            QG[0, :, pl.ds((2 * pair + i) * HEAD, HEAD)] = made[i * TOK : (i + 1) * TOK]
    dv = jnp.dot(probs[...], cots[...], preferred_element_type=f32)
    dk = jnp.dot(slopes[...], queries[...], preferred_element_type=f32)
    RG[0, 0, 0] = dk[TOK:].astype(bf16)
    RG[0, 0, 1] = dv[TOK:].astype(bf16)
    for s, (zh, c) in enumerate(places):
        parts[zh, j, c] += dk[s * PRO : (s + 1) * PRO]
        parts[zh, 2 + j, c] += dv[s * PRO : (s + 1) * PRO]

    @pl.when((d == 1) & (j == 1))
    def _():
        PP[...] = parts[...].astype(bf16)


def attention(numbers, everyone, keys, vals, Q, OG, QP, OP):
    core = lambda: lax.rem(lax.axis_index("grp"), 2)
    own = pl.BlockSpec((1, TOK, 1024), lambda d, j: (0, 0, core() * 2 + jnp.maximum(d, j)))
    theirs = pl.BlockSpec((TOK, 1024), lambda d, j: (0, d * j))
    here = pl.BlockSpec((1, 1, DEV, HEAD), lambda d, j: (j, d, 0, 0))
    return pl.pallas_call(
        attention_kernel,
        out_shape=(
            jax.ShapeDtypeStruct((2, TOK, 2048), bf16),
            jax.ShapeDtypeStruct((2, 2, 2, TOK, HEAD), bf16),
            jax.ShapeDtypeStruct((4, 4, 2, PRO, HEAD), bf16),
        ),
        grid=(2, 2),
        in_specs=[SMEM] * 7 + [VMEM, here, here, own, own, theirs, theirs],
        out_specs=(
            pl.BlockSpec((1, TOK, 1024), lambda d, j: (d, 0, j)),
            pl.BlockSpec((1, 1, 2, TOK, HEAD), lambda d, j: (j, d, 0, 0, 0)),
            VMEM,
        ),
        scratch_shapes=[
            pltpu.VMEM((256, 1024), bf16),
            pltpu.VMEM((256, 1024), bf16),
            pltpu.VMEM((1024, HEAD), bf16),
            pltpu.VMEM((1024, HEAD), bf16),
            pltpu.VMEM((4, 4, 2, PRO, HEAD), f32),
        ],
        compiler_params=LOCAL,
        name="attention",
    )(*numbers, everyone, keys, vals, Q, OG, QP, OP)


RETURN_COPIES = 8


def return_kernel(PP, QG, PS, QO, land, send, recv):
    me = Place()
    ring, partner = me.ring_zh(), me.partner()
    greet([ring[1], ring[2], partner])
    links = Links(send, recv)

    def add(dst, terms):
        for i in range(2):
            for d in range(2):
                total = terms[0][i, d].astype(f32)
                for term in terms[1:]:
                    total = total + term[i, d].astype(f32)
                dst[i, d] = total.astype(dst.dtype)

    going = Reduce4(
        links, ring, lambda c, h: PP.at[c, pl.ds(2 * h, 2)], lambda i: land.at[i], add
    )
    going.begin()
    queries = links.take()
    links.start(queries, QG.at[1], QO, partner)
    going.mid()
    going.finish(lambda h: PS.at[pl.ds(2 * h, 2)])
    links.arrived(queries, QO, partner)
    links.drain()


def give_back(PP, QG):
    return pl.pallas_call(
        return_kernel,
        out_shape=(
            jax.ShapeDtypeStruct((4, 2, PRO, HEAD), f32),
            jax.ShapeDtypeStruct((TOK, 2048), bf16),
        ),
        in_specs=[VMEM, HBM],
        out_specs=(VMEM, HBM),
        scratch_shapes=[
            pltpu.VMEM((6, 2, 2, PRO, HEAD), bf16),
            pltpu.SemaphoreType.DMA((RETURN_COPIES,)),
            pltpu.SemaphoreType.DMA((RETURN_COPIES,)),
        ],
        compiler_params=remote_params(3),
        name="give_back",
    )(PP, QG)


SUM_COPIES = 80
I_STEP = 640


def sum_kernel(
    raw, RG, PS, turns, gain, XT, W,
    IG, WG,
    xt, w, w2, grads, theirs, D, one, acc1, two, acc2, near, acc3, three, wg, send, recv, local,
):
    me = Place()
    partner = me.partner()
    near_minus, near_plus = me.near_z()
    ring_x, ring_y, ring_zh = me.ring_x(), me.ring_y(), me.ring_zh()
    fetch = pltpu.make_async_copy(XT, xt, local.at[0])
    fetch.start()
    weights = pltpu.make_async_copy(W, w, local.at[1])
    weights.start()
    greet([*ring_x[1:], *ring_y[1:], *ring_zh[1:], near_minus, near_plus, partner])
    links = Links(send, recv)
    core, zl = me.core, me.zl
    swapped = links.take()
    links.start(swapped, W, w2, partner)

    for d in range(2):
        c, s = turns[d, 0], turns[d, 1]
        whose = core if d == 0 else 1 - core
        rows = pl.ds(d * DEV, DEV)
        for j in range(2):
            cot = jnp.concatenate([RG[j, d, 0].astype(f32), PS[j, whose]], 0)
            turned = (cot * c + swap_halves(cot * s)) * gain[...]
            k = raw[j, d]
            inverse = lax.rsqrt(jnp.mean(k * k, axis=1, keepdims=True) + 1e-06)
            along = jnp.mean(k * turned, axis=1, keepdims=True)
            back = inverse * turned - k * (inverse * inverse * inverse * along)
            grads[rows, pl.ds(j * HEAD, HEAD)] = back.astype(bf16)
            values = jnp.concatenate([RG[j, d, 1], PS[2 + j, whose].astype(bf16)], 0)
            grads[rows, pl.ds((2 + j) * HEAD, HEAD)] = values
    crossed = links.take()
    links.start(crossed, grads.at[pl.ds(DEV, DEV)], theirs, partner)
    fetch.wait()

    def term(y, x, kind):
        rows = pl.ds(pl.multiple_of((y * 4 + x) * 320, 320), 320)
        made = jnp.dot(
            xt[rows, :], grads[:, pl.ds(kind * 256, 256)], preferred_element_type=f32
        ).astype(bf16)
        for j in range(2):
            for h in range(2):
                D[2 * kind + j, y, x, h] = made[h * ROWS : (h + 1) * ROWS, j * HEAD : (j + 1) * HEAD]

    def terms_for(kind, place):
        def body(i, carry):
            if kind == 0:
                term(i, place, 0)
            else:
                term(place, i, 1)
            return carry

        lax.fori_loop(0, 4, body, 0)

    def input_part(i):
        rows = pl.ds(pl.multiple_of(i * I_STEP, I_STEP), I_STEP)
        total = 0.0
        for left, right in ((grads[pl.ds(0, DEV), :], w), (theirs[...], w2)):
            both = jnp.concatenate([right[t, rows, :] for t in range(4)], 1)
            total = total + lax.dot_general(
                left, both, (((1,), (1,)), ((), ())), preferred_element_type=f32
            )
        IG[:, rows] = total.astype(bf16)

    def input_parts(begin, end):
        def body(i, carry):
            input_part(i)
            return carry

        lax.fori_loop(begin, end, body, 0)

    first, second = [], []
    for t in range(4):
        if t < 2:
            part = lambda c, h, t=t: D.at[t, :, c, h]
        else:
            part = lambda c, h, t=t: D.at[t, c, :, h]
        ring = ring_x if t < 2 else ring_y
        other = ring_y if t < 2 else ring_x
        first.append(Reduce4(links, ring, part, lambda i, t=t: one.at[t, i], add_blocks))
        second.append(
            Reduce4(
                links,
                other,
                lambda c, h, t=t: acc1.at[t, c, h],
                lambda i, t=t: two.at[t, i],
                add_block,
            )
        )
    class Wave:
        def __init__(self, n):
            self.n, self.slots = n, (n, 2 + n)
            self.pair = [(links.take(), near_plus), (links.take(), near_minus)]
            self.third = Reduce4(
                links, ring_zh, lambda c, h: acc3.at[n, c, cut[h]], lambda i: three.at[n, i, thirds[i]], add_block
            )
            self.last = Gather4(
                links, ring_zh, lambda c: wg.at[core, n, c], lambda c, h: wg.at[core, n, c, cut[h]]
            )
            self.across = links.take()

        def near_begin(self):
            for kind, (number, device) in enumerate(self.pair):
                links.start(number, acc2.at[self.slots[kind], 1 - zl], near.at[self.n, kind], device)

        def near_finish(self):
            for kind, (number, device) in enumerate(self.pair):
                links.arrived(number, near.at[self.n, kind], device)
                for h in range(2):
                    rows = pl.ds(h * HALF, HALF)
                    add_block(
                        acc3.at[self.n, 2 * kind + h],
                        [acc2.at[self.slots[kind], zl, rows], near.at[self.n, kind, rows]],
                    )

        def third_finish(self):
            self.third.finish(lambda h: wg.at[core, self.n, me.zh, cut[h]])

        def across_begin(self):
            links.start(self.across, wg.at[core, self.n], wg.at[core, self.n], partner)

        def across_finish(self):
            links.arrived(self.across, wg.at[1 - core, self.n], partner)

    cut = (pl.ds(0, 48), pl.ds(48, 32))
    thirds = [cut[h] for h in (0, 1, 1, 0, 0, 1)]
    waves = Wave(0), Wave(1)

    for place in (2, 1, 3, 0):
        for kind, at in ((0, me.x), (1, me.y)):
            terms_for(kind, lax.rem(at + place, 4))
            first[2 * kind].send_for(place)
    first[0].mid()
    first[2].mid()
    first[1].begin()
    first[3].begin()
    weights.wait()
    links.arrived(crossed, theirs, partner)
    links.arrived(swapped, w2, partner)
    input_parts(0, 2)

    def turn(t):
        first[t].finish(lambda h: acc1.at[t, :, h])
        second[t].begin()

    def settle(t):
        second[t].finish(lambda h: acc2.at[t, h])

    turn(0)
    turn(2)
    input_parts(2, 4)
    first[1].mid()
    first[3].mid()
    second[0].mid()
    second[2].mid()
    input_parts(4, 7)
    settle(0)
    settle(2)
    waves[0].near_begin()
    turn(1)
    turn(3)
    waves[0].near_finish()
    waves[0].third.begin()
    input_parts(7, 8)
    second[1].mid()
    second[3].mid()
    waves[0].third.mid()
    settle(1)
    settle(3)
    waves[1].near_begin()
    waves[0].third_finish()
    waves[0].last.begin()
    waves[1].near_finish()
    waves[1].third.begin()
    waves[0].last.forward()
    waves[1].third.mid()
    waves[0].last.finish()
    waves[0].across_begin()
    waves[1].third_finish()
    waves[1].last.begin()
    waves[1].last.forward()
    waves[1].last.finish()
    waves[1].across_begin()
    waves[0].across_finish()
    waves[1].across_finish()
    WG[...] = wg[...]
    links.drain()
    assert links.used <= SUM_COPIES


def sum_terms(raw, RG, PS, turns, gain, XT, W):
    return pl.pallas_call(
        sum_kernel,
        out_shape=(
            jax.ShapeDtypeStruct((DEV, WIDTH), bf16),
            jax.ShapeDtypeStruct((2, 2, 4, HALF, HEAD), bf16),
        ),
        in_specs=[VMEM] * 5 + [HBM] * 2,
        out_specs=(VMEM, VMEM),
        scratch_shapes=[
            pltpu.VMEM((WIDTH, 2 * DEV), bf16),
            pltpu.VMEM((4, WIDTH, HEAD), bf16),
            pltpu.VMEM((4, WIDTH, HEAD), bf16),
            pltpu.VMEM((2 * DEV, 512), bf16),
            pltpu.VMEM((DEV, 512), bf16),
            pltpu.VMEM((4, 4, 4, 2, ROWS, HEAD), bf16),
            pltpu.VMEM((4, 6, 4, ROWS, HEAD), bf16),
            pltpu.VMEM((4, 4, 2, ROWS, HEAD), bf16),
            pltpu.VMEM((4, 6, ROWS, HEAD), bf16),
            pltpu.VMEM((4, 2, ROWS, HEAD), bf16),
            pltpu.VMEM((2, 2, ROWS, HEAD), bf16),
            pltpu.VMEM((2, 4, HALF, HEAD), bf16),
            pltpu.VMEM((2, 6, HALF, HEAD), bf16),
            pltpu.VMEM((2, 2, 4, HALF, HEAD), bf16),
            pltpu.SemaphoreType.DMA((SUM_COPIES,)),
            pltpu.SemaphoreType.DMA((SUM_COPIES,)),
            pltpu.SemaphoreType.DMA((2,)),
        ],
        compiler_params=remote_params(4),
        name="sum_terms",
    )(raw, RG, PS, turns, gain, XT, W)


def put_kernel(IG, WG, QG, QO, resp, prompt, qgrad, kout, vout):
    step = pl.program_id(0)
    core = lax.rem(lax.axis_index("grp"), 2)
    resp[0] = IG[:TOK]
    prompt[0] = IG[TOK:]

    @pl.when(step == core)
    def _():
        qgrad[0] = QG[0]

    @pl.when(step != core)
    def _():
        qgrad[0] = QO[...]

    @pl.when(step == 0)
    def _():
        for c in range(2):
            for j in range(2):
                lanes = pl.ds((2 * c + j) * HEAD, HEAD)
                kout[:, lanes] = WG[c, j, 0]
                vout[:, lanes] = WG[c, j, 1]


def put(IG, WG, QG, QO):
    half = WIDTH // 2
    return pl.pallas_call(
        put_kernel,
        out_shape=(
            jax.ShapeDtypeStruct((1, TOK, WIDTH), bf16),
            jax.ShapeDtypeStruct((1, PRO, WIDTH), bf16),
            jax.ShapeDtypeStruct((1, TOK, 4096), bf16),
            jax.ShapeDtypeStruct((ROWS, 512), bf16),
            jax.ShapeDtypeStruct((ROWS, 512), bf16),
        ),
        grid=(2,),
        in_specs=[
            pl.BlockSpec((DEV, half), lambda i: (0, i)),
            VMEM,
            pl.BlockSpec((1, TOK, 2048), lambda i: (0, 0, 0)),
            VMEM,
        ],
        out_specs=(
            pl.BlockSpec((1, TOK, half), lambda i: (0, 0, i)),
            pl.BlockSpec((1, PRO, half), lambda i: (0, 0, i)),
            pl.BlockSpec((1, TOK, 2048), lambda i: (0, 0, i)),
            VMEM,
            VMEM,
        ),
        compiler_params=LOCAL,
        name="put",
    )(IG, WG, QG, QO)


def local(
    queries, out_grad, resp_in, prompt_in, key_matrix, value_matrix, key_gain, seg_prompt, seg_start, seg_len, owner
):
    cos, sin = rotary_tables()
    gain = key_gain.reshape(1, HEAD)

    W, XP, QP, OP, SP, SS, SL = gather(
        key_matrix, value_matrix, resp_in, prompt_in, queries, out_grad, seg_prompt, seg_start, seg_len
    )
    flat = W.reshape(4, WIDTH, HEAD)
    XT, raw, keys, vals, pkv, turns = project(seg_start, SS, resp_in, prompt_in, XP, flat, cos, sin, gain)
    everyone = share(pkv)
    numbers = (seg_prompt, seg_start, seg_len, SP, SS, SL, owner)
    QG, RG, PP = attention(numbers, everyone, keys, vals, queries, out_grad, QP, OP)
    PS, QO = give_back(PP, QG)
    IG, WG = sum_terms(raw, RG, PS, turns, gain, XT, flat)
    resp, prompt, qgrad, kout, vout = put(IG, WG.reshape(2, 2, 2, ROWS, HEAD), QG, QO)
    return qgrad, resp, prompt, kout, vout


def solution(mesh):
    in_specs = (
        P("fsdp", "grp", None),
        P("fsdp", "grp", None),
        P("fsdp", "grp", None),
        P("fsdp", "grp", None),
        P("fsdp", None),
        P("fsdp", None),
        P(),
        P("fsdp", "grp"),
        P("fsdp", "grp"),
        P("fsdp", "grp"),
        P("fsdp", None),
    )
    out_specs = (
        P("fsdp", "grp", None),
        P("fsdp", "grp", None),
        P("fsdp", "grp", None),
        P("fsdp", None),
        P("fsdp", None),
    )
    return jax.shard_map(local, mesh=mesh, in_specs=in_specs, out_specs=out_specs, check_vma=False)
```

```python
import functools
import math

import jax
import jax.numpy as jnp
import numpy as np
from jax import lax
from jax.experimental import pallas as pl
from jax.experimental.pallas import tpu as pltpu
from jax.sharding import PartitionSpec as P

MESH = pl.DeviceIdType.MESH
HBM = pl.BlockSpec(memory_space=pltpu.HBM)
SMEM = pl.BlockSpec(memory_space=pltpu.SMEM)
VMEM = pl.BlockSpec(memory_space=pltpu.VMEM)
VMEM_LIMIT = 60 * 1024 * 1024

WIDTH = 5120
HEAD = 128
ROWS = 160
HALF = 80
TOK = 128
PRO = 64
DEV = TOK + PRO
SCALE = 1.0 / math.sqrt(HEAD)
BASE = 1000000.0
bf16 = jnp.bfloat16
f32 = jnp.float32


def rotary_tables():
    frequency = np.float32(BASE) ** (-np.arange(64, dtype=np.float32) / np.float32(64))
    angles = np.arange(-128, 192, dtype=np.float32)[:, None] * frequency[None, :].astype(np.float32)
    angles = angles.astype(np.float32).astype(np.float64)
    cos, sin = np.cos(angles), np.sin(angles)
    return (
        np.concatenate([cos, cos], 1).astype(np.float32),
        np.concatenate([-sin, sin], 1).astype(np.float32),
    )


class Place:
    def __init__(self):
        g, f = lax.axis_index("grp"), lax.axis_index("fsdp")
        self.core, self.zh = lax.rem(g, 2), lax.div(g, 2)
        self.zl = lax.rem(f, 2)
        self.x = lax.rem(lax.div(f, 2), 4)
        self.y = lax.div(f, 8)
        self.z = self.zh * 2 + self.zl

    def at(self, y=None, x=None, z=None, core=None):
        y = self.y if y is None else y
        x = self.x if x is None else x
        z = self.z if z is None else z
        core = self.core if core is None else core
        return {"grp": lax.div(z, 2) * 2 + core, "fsdp": (y * 4 + x) * 2 + lax.rem(z, 2)}

    def ring_x(self):
        return self.x, self.at(x=lax.rem(self.x + 3, 4)), self.at(x=lax.rem(self.x + 1, 4))

    def ring_y(self):
        return self.y, self.at(y=lax.rem(self.y + 3, 4)), self.at(y=lax.rem(self.y + 1, 4))

    def ring_zh(self):
        return self.zh, self.at(z=lax.rem(self.z + 6, 8)), self.at(z=lax.rem(self.z + 2, 8))

    def near_z(self):
        return self.at(z=lax.rem(self.z + 7, 8)), self.at(z=lax.rem(self.z + 1, 8))

    def first_axis(self, kind):
        return self.x * (1 - kind) + self.y * kind

    def ring_of(self, kind):
        def moved(step):
            return self.at(x=lax.rem(self.x + step * (1 - kind), 4), y=lax.rem(self.y + step * kind, 4))

        return self.first_axis(kind), moved(3), moved(1)

    def partner(self):
        return self.at(core=1 - self.core)


def greet(devices):
    barrier = pltpu.get_barrier_semaphore()
    for device in devices:
        pl.semaphore_signal(barrier, inc=1, device_id=device, device_id_type=MESH)
    pl.semaphore_wait(barrier, len(devices))


class Links:
    def __init__(self, send, recv):
        self.send, self.recv, self.used, self.sent = send, recv, 0, []

    def take(self):
        self.used += 1
        return self.used - 1

    def copy(self, number, src, dst, device):
        return pltpu.make_async_remote_copy(
            src_ref=src,
            dst_ref=dst,
            send_sem=self.send.at[number],
            recv_sem=self.recv.at[number],
            device_id=device,
            device_id_type=MESH,
        )

    def start(self, number, src, dst, device):
        made = self.copy(number, src, dst, device)
        made.start()
        self.sent.append(made)

    def arrived(self, number, dst, device):
        self.copy(number, dst, dst, device).wait_recv()

    def drain(self):
        for made in self.sent:
            made.wait_send()
        self.sent = []


class Gather4:
    def __init__(self, links, ring, view, half, own=None):
        self.links, self.view, self.half = links, view, half
        self.me, self.minus, self.plus = ring
        self.own = view(self.me) if own is None else own
        self.n = [links.take() for _ in range(4)]

    def begin(self):
        self.links.start(self.n[0], self.own, self.view(self.me), self.plus)
        self.links.start(self.n[1], self.own, self.view(self.me), self.minus)

    def forward(self):
        left, right = lax.rem(self.me + 3, 4), lax.rem(self.me + 1, 4)
        self.links.arrived(self.n[0], self.view(left), self.plus)
        self.links.start(self.n[2], self.half(left, 0), self.half(left, 0), self.plus)
        self.links.arrived(self.n[1], self.view(right), self.minus)
        self.links.start(self.n[3], self.half(right, 1), self.half(right, 1), self.minus)

    def finish(self):
        across = lax.rem(self.me + 2, 4)
        self.links.arrived(self.n[2], self.half(across, 0), self.plus)
        self.links.arrived(self.n[3], self.half(across, 1), self.minus)


class Reduce4:
    def __init__(self, links, ring, part, slot, add):
        self.links, self.part, self.slot, self.add = links, part, slot, add
        self.me, self.minus, self.plus = ring
        self.n = [links.take() for _ in range(6)]

    def send_for(self, place):
        part, slot, n = self.part, self.slot, self.n
        block = lax.rem(self.me + place, 4)
        if place == 2:
            self.links.start(n[0], part(block, 0), slot(0), self.plus)
            self.links.start(n[1], part(block, 1), slot(1), self.minus)
        if place == 1:
            self.links.start(n[2], part(block, 1), slot(2), self.plus)
        if place == 3:
            self.links.start(n[3], part(block, 0), slot(3), self.minus)

    def begin(self):
        for place in (2, 1, 3):
            self.send_for(place)

    def mid(self):
        left, right = lax.rem(self.me + 3, 4), lax.rem(self.me + 1, 4)
        part, slot, n = self.part, self.slot, self.n
        self.links.arrived(n[0], slot(0), self.plus)
        self.add(slot(0), [slot(0), part(right, 0)])
        self.links.start(n[4], slot(0), slot(4), self.plus)
        self.links.arrived(n[1], slot(1), self.minus)
        self.add(slot(1), [slot(1), part(left, 1)])
        self.links.start(n[5], slot(1), slot(5), self.minus)

    def finish(self, out):
        part, slot, n = self.part, self.slot, self.n
        self.links.arrived(n[3], slot(3), self.minus)
        self.links.arrived(n[4], slot(4), self.plus)
        self.add(out(0), [part(self.me, 0), slot(3), slot(4)])
        self.links.arrived(n[2], slot(2), self.plus)
        self.links.arrived(n[5], slot(5), self.minus)
        self.add(out(1), [part(self.me, 1), slot(2), slot(5)])


def add_block(dst, terms):
    total = terms[0][...].astype(f32)
    for term in terms[1:]:
        total = total + term[...].astype(f32)
    dst[...] = total.astype(dst.dtype)


def add_blocks(dst, terms):
    def body(i, carry):
        total = terms[0][i].astype(f32)
        for term in terms[1:]:
            total = total + term[i].astype(f32)
        dst[i] = total.astype(dst.dtype)
        return carry

    lax.fori_loop(0, dst.shape[0], body, 0)


class Move4:
    def __init__(self, links, me, XT, XG, relay, zl):
        self.links, self.me, self.XT, self.XG, self.relay, self.zl = links, me, XT, XG, relay, zl
        self.place, self.minus, self.plus = me.ring_of(me.core)
        self.n = [links.take() for _ in range(9)]
        self.held = [pl.ds(0, 2), pl.ds(2, 2)]

    def from_place(self, steps):
        return lax.rem(self.place + steps, 4)

    def begin(self):
        mine = self.XG.at[self.me.core, self.place]
        jobs = (
            (0, 2, 0, self.relay.at[0], self.plus),
            (1, 2, 1, self.relay.at[1], self.minus),
            (2, 1, None, mine, self.plus),
            (3, 3, None, mine, self.minus),
        )

        def start(kind):
            for n, steps, h, dst, device in jobs:
                c = self.from_place(steps)
                rows = pl.ds(0, 4) if h is None else self.held[h]
                src = self.XT.at[rows, c, self.zl] if kind == 0 else self.XT.at[c, rows, self.zl]
                self.links.copy(self.n[n], src, dst, device).start()

        pl.when(self.me.core == 0)(lambda: start(0))
        pl.when(self.me.core == 1)(lambda: start(1))
        for n, steps, h, dst, device in jobs:
            self.links.sent.append(self.links.copy(self.n[n], dst, dst, device))

    def forward(self):
        core, n = self.me.core, self.n
        self.links.arrived(n[0], self.relay.at[0], self.plus)
        self.links.start(n[4], self.relay.at[0], self.XG.at[core, self.from_place(3), self.held[0]], self.plus)
        self.links.arrived(n[1], self.relay.at[1], self.minus)
        self.links.start(n[5], self.relay.at[1], self.XG.at[core, self.from_place(1), self.held[1]], self.minus)

    def hand_over(self, steps):
        core, n, partner = self.me.core, self.n, self.me.partner()
        view = self.XG.at[core, self.from_place(steps)]
        if steps == 3:
            self.links.arrived(n[2], view, self.plus)
        elif steps == 1:
            self.links.arrived(n[3], view, self.minus)
        else:
            c = self.from_place(2)
            self.links.arrived(n[4], self.XG.at[core, c, self.held[0]], self.plus)
            self.links.arrived(n[5], self.XG.at[core, c, self.held[1]], self.minus)
        self.links.start(n[5 + steps], view, view, partner)

    def finish(self):
        other = 1 - self.me.core
        for steps in (1, 2, 3):
            c = lax.rem(self.me.first_axis(other) + steps, 4)
            self.links.arrived(self.n[5 + steps], self.XG.at[other, c], self.me.partner())


X_GATHERED = jax.ShapeDtypeStruct((2, 4, 4, ROWS, 2 * DEV), bf16)
W_SHAPE = jax.ShapeDtypeStruct((2, 4, 4, 2, ROWS, HEAD), bf16)
RELAY = pltpu.VMEM((2, 2, ROWS, 2 * DEV), bf16)


def remote_params(number, limit=None):
    return pltpu.CompilerParams(
        collective_id=number, has_side_effects=True, vmem_limit_bytes=limit or VMEM_LIMIT
    )


LOCAL = pltpu.CompilerParams(vmem_limit_bytes=VMEM_LIMIT)


GATHER_COPIES = 64


def gather_kernel(kw, vw, resp, prompt, q, og, sp, ss, sl, W, XP, QP, OP, SP, SS, SL, send, recv, local):
    me = Place()
    core, partner = me.core, me.partner()
    near_minus, near_plus = me.near_z()
    _, xm, xp = me.ring_x()
    _, ym, yp = me.ring_y()
    greet([xm, xp, ym, yp, near_minus, near_plus, partner])
    links = Links(send, recv)

    def columns(matrix, j):
        return matrix.at[:, pl.ds(pl.multiple_of((core * 2 + j) * HEAD, HEAD), HEAD)]

    own = [columns(kw, 0), columns(kw, 1), columns(vw, 0), columns(vw, 1)]
    x, y, zl = me.x, me.y, me.zl
    rows = lambda h: pl.ds(h * HALF, HALF)

    ax = Gather4(links, me.ring_x(), lambda c: W.at[0, y, c, zl], lambda c, h: W.at[0, y, c, zl, rows(h)], own[0])
    ay = Gather4(links, me.ring_y(), lambda c: W.at[0, c, :, zl], lambda c, h: W.at[0, c, :, zl, rows(h)])
    by = Gather4(links, me.ring_y(), lambda c: W.at[1, c, x, zl], lambda c, h: W.at[1, c, x, zl, rows(h)], own[1])
    bx = Gather4(links, me.ring_x(), lambda c: W.at[1, :, c, zl], lambda c, h: W.at[1, :, c, zl, rows(h)])
    cx = Gather4(links, me.ring_x(), lambda c: W.at[2, y, c], lambda c, h: W.at[2, y, c, h])
    cy = Gather4(links, me.ring_y(), lambda c: W.at[2, c], lambda c, h: W.at[2, c, :, h])
    dy = Gather4(links, me.ring_y(), lambda c: W.at[3, c, x], lambda c, h: W.at[3, c, x, h])
    dx = Gather4(links, me.ring_x(), lambda c: W.at[3, :, c], lambda c, h: W.at[3, :, c, h])

    zn = {}

    def z_view(t, place, which, h):
        if t == 0:
            return W.at[0, lax.rem(y + place, 4), :, which, rows(h)]
        if t == 1:
            return W.at[1, :, lax.rem(x + place, 4), which, rows(h)]
        return W.at[t, y, x, which, rows(h)]

    def z_begin(t, place, src=None):
        zn[t, place] = links.take(), links.take()
        for h, device in ((0, near_plus), (1, near_minus)):
            view = z_view(t, place, zl, h)
            links.start(zn[t, place][h], view if src is None else src(h), view, device)

    def z_finish(t, place):
        for h, device in ((0, near_plus), (1, near_minus)):
            links.arrived(zn[t, place][h], z_view(t, place, 1 - zl, h), device)

    ax.begin()
    by.begin()
    for t in (2, 3):
        matrix_half = lambda h, t=t: vw.at[rows(h), pl.ds(pl.multiple_of((core * 2 + t - 2) * HEAD, HEAD), HEAD)]
        z_begin(t, 0, matrix_half)

    locals_ = []

    def here(src, dst):
        made = pltpu.make_async_copy(src, dst, local.at[len(locals_)])
        made.start()
        locals_.append(made)

    for t in range(4):
        here(own[t], W.at[t, y, x, zl])
    swaps = []

    def swap(src, dst):
        number = links.take()
        links.start(number, src, dst, partner)
        swaps.append((number, dst))

    theirs = pl.ds(pl.multiple_of((1 - core) * 2048, 2048), 2048)
    swap(sp, SP)
    swap(ss, SS)
    swap(sl, SL)
    swap(resp.at[0], XP.at[pl.ds(0, TOK)])
    swap(prompt.at[0], XP.at[pl.ds(TOK, PRO)])
    swap(q.at[0, :, theirs], QP)
    swap(og.at[0, :, theirs], OP)

    ax.forward()
    by.forward()
    for made in locals_:
        made.wait()
    z_finish(2, 0)
    cx.begin()
    z_finish(3, 0)
    dy.begin()
    ax.finish()
    ay.begin()
    z_begin(0, 0)
    by.finish()
    bx.begin()
    z_begin(1, 0)
    cx.forward()
    dy.forward()
    cx.finish()
    cy.begin()
    dy.finish()
    dx.begin()
    ay.forward()
    z_begin(0, 3)
    z_begin(0, 1)
    bx.forward()
    z_begin(1, 3)
    z_begin(1, 1)
    ay.finish()
    z_begin(0, 2)
    bx.finish()
    z_begin(1, 2)
    cy.forward()
    dx.forward()
    for place in range(4):
        z_finish(0, place)
        z_finish(1, place)
    cy.finish()
    dx.finish()
    for number, landing in swaps:
        links.arrived(number, landing, partner)
    links.drain()
    assert links.used <= GATHER_COPIES


def gather(kw, vw, resp, prompt, q, og, sp, ss, sl):
    return pl.pallas_call(
        gather_kernel,
        out_shape=(
            jax.ShapeDtypeStruct((4, 4, 4, 2, ROWS, HEAD), bf16),
            jax.ShapeDtypeStruct((DEV, WIDTH), bf16),
            jax.ShapeDtypeStruct((TOK, 2048), bf16),
            jax.ShapeDtypeStruct((TOK, 2048), bf16),
            jax.ShapeDtypeStruct((1, 2), jnp.int32),
            jax.ShapeDtypeStruct((1, 2), jnp.int32),
            jax.ShapeDtypeStruct((1, 2), jnp.int32),
        ),
        in_specs=[HBM] * 9,
        out_specs=(HBM,) * 7,
        scratch_shapes=[
            pltpu.SemaphoreType.DMA((GATHER_COPIES,)),
            pltpu.SemaphoreType.DMA((GATHER_COPIES,)),
            pltpu.SemaphoreType.DMA((4,)),
        ],
        compiler_params=remote_params(1),
        name="gather",
    )(kw, vw, resp, prompt, q, og, sp, ss, sl)


K_STEP = 1024


def swap_halves(a):
    return pltpu.roll(a, 64, 1)


def tables_of(starts, cos, sin):
    start = starts[0, 1]
    late = pl.multiple_of(192 - start, 16)
    row = lax.broadcasted_iota(jnp.int32, (TOK, HEAD), 0)
    out = []
    for table in (cos, sin):
        first = table[pl.ds(192, TOK), :]
        second = table[pl.ds(late, TOK), :]
        out.append(jnp.concatenate([jnp.where(row < start, first, second), table[pl.ds(128, PRO), :]], 0))
    return out


def project_kernel(ss, SS, resp, prompt, XP, W, cos, sin, gain, XT, raw, keys, vals, pkv, turns, acc):
    step = pl.program_id(0)
    left = jnp.concatenate([resp[0], prompt[0], XP[...]], 0)
    right = jnp.concatenate([W[t] for t in range(4)], 1)
    part = jnp.dot(left, right, preferred_element_type=f32)
    XT[...] = left.T

    @pl.when(step == 0)
    def _():
        acc[...] = part

    @pl.when(step > 0)
    def _():
        acc[...] += part

    @pl.when(step == pl.num_programs(0) - 1)
    def _():
        for d in range(2):
            c, s = tables_of((ss, SS)[d], cos, sin)
            turns[d, 0], turns[d, 1] = c, s
            core = lax.rem(lax.axis_index("grp") + d, 2)
            for j in range(2):
                k = acc[pl.ds(d * DEV, DEV), pl.ds(j * HEAD, HEAD)]
                raw[j, d] = k
                square = jnp.mean(k * k, axis=1, keepdims=True)
                normed = k * lax.rsqrt(square + 1e-06) * gain[...]
                turned = (normed * c + swap_halves(normed) * s).astype(bf16)
                keys[j, d] = turned
                pkv[j, core] = turned[TOK:]
                v = acc[pl.ds(d * DEV, DEV), pl.ds((2 + j) * HEAD, HEAD)].astype(bf16)
                vals[j, d] = v
                pkv[2 + j, core] = v[TOK:]


def project(ss, SS, resp, prompt, XP, W, cos, sin, gain):
    return pl.pallas_call(
        project_kernel,
        out_shape=(
            jax.ShapeDtypeStruct((WIDTH, 2 * DEV), bf16),
            jax.ShapeDtypeStruct((2, 2, DEV, HEAD), f32),
            jax.ShapeDtypeStruct((2, 2, DEV, HEAD), bf16),
            jax.ShapeDtypeStruct((2, 2, DEV, HEAD), bf16),
            jax.ShapeDtypeStruct((4, 2, PRO, HEAD), bf16),
            jax.ShapeDtypeStruct((2, 2, DEV, HEAD), f32),
        ),
        grid=(WIDTH // K_STEP,),
        in_specs=[
            SMEM,
            SMEM,
            pl.BlockSpec((1, TOK, K_STEP), lambda i: (0, 0, i)),
            pl.BlockSpec((1, PRO, K_STEP), lambda i: (0, 0, i)),
            pl.BlockSpec((DEV, K_STEP), lambda i: (0, i)),
            pl.BlockSpec((4, K_STEP, HEAD), lambda i: (0, i, 0)),
            VMEM,
            VMEM,
            VMEM,
        ],
        out_specs=(pl.BlockSpec((K_STEP, 2 * DEV), lambda i: (i, 0)),) + (VMEM,) * 5,
        scratch_shapes=[pltpu.VMEM((2 * DEV, 512), f32)],
        compiler_params=LOCAL,
        name="project",
    )(ss, SS, resp, prompt, XP, W, cos, sin, gain)


SHARE_COPIES = 16


def share_kernel(pkv, XT, W, everyone, XG, W2, relay, send, recv, local):
    me = Place()
    ring = me.ring_zh()
    links = Links(send, recv)
    going = Gather4(
        links, ring, lambda c: everyone.at[c], lambda c, h: everyone.at[c, pl.ds(2 * h, 2)], pkv
    )
    columns = Move4(links, me, XT, XG, relay, 0)
    weights = links.take()
    greet([ring[1], ring[2], columns.minus, columns.plus, me.partner()])
    own = pltpu.make_async_copy(pkv, everyone.at[me.zh], local)
    own.start()
    going.begin()
    columns.begin()
    links.start(weights, W.at[pl.ds(0, 2)], W2, me.partner())
    going.forward()
    columns.forward()
    columns.hand_over(3)
    columns.hand_over(1)
    going.finish()
    columns.hand_over(2)
    own.wait()
    columns.finish()
    links.arrived(weights, W2, me.partner())
    links.drain()
    assert links.used <= SHARE_COPIES


def share(pkv, XT, W):
    return pl.pallas_call(
        share_kernel,
        out_shape=(jax.ShapeDtypeStruct((4, 4, 2, PRO, HEAD), bf16), X_GATHERED, W_SHAPE),
        in_specs=[VMEM, HBM, HBM],
        out_specs=(VMEM, HBM, HBM),
        scratch_shapes=[
            RELAY,
            pltpu.SemaphoreType.DMA((SHARE_COPIES,)),
            pltpu.SemaphoreType.DMA((SHARE_COPIES,)),
            pltpu.SemaphoreType.DMA,
        ],
        compiler_params=remote_params(2),
        name="share",
    )(pkv, XT, W)


def attention_kernel(
    sp, ss, sl, SP, SS, SL, owner, everyone, keys, vals, Q, OG, QP, OP,
    QG, RG, PP, probs, slopes, queries, cots, parts,
):
    d, j = pl.program_id(0), pl.program_id(1)

    @pl.when((d == 0) & (j == 0))
    def _():
        parts[...] = jnp.zeros_like(parts)

    def number(own, other, i):
        return jnp.where(d == 0, own[0, i], other[0, i])

    slots = [owner[0, number(sp, SP, i)] for i in range(2)]
    start, lens = number(ss, SS, 1), [number(sl, SL, i) for i in range(2)]
    places = [(lax.div(s, 2), lax.rem(s, 2)) for s in slots]
    K = jnp.concatenate([everyone[zh, j, c] for zh, c in places] + [keys[0, 0, :TOK]], 0)
    V = jnp.concatenate([everyone[zh, 2 + j, c] for zh, c in places] + [vals[0, 0, :TOK]], 0)

    key = lax.broadcasted_iota(jnp.int32, (2 * TOK, TOK), 0)
    row = lax.broadcasted_iota(jnp.int32, (2 * TOK, TOK), 1)
    late = row >= start
    first = jnp.where(late, start, 0)
    end = jnp.where(late, start + lens[1], lens[0])
    from_key = jnp.where(key < TOK, jnp.where(late, PRO, 0), first + TOK)
    to_key = jnp.where(key < TOK, jnp.where(late, TOK, PRO), jnp.minimum(end, row + 1) + TOK)
    bias = jnp.where((key >= from_key) & (key < to_key), 0.0, -1e30)
    bias = jnp.concatenate([bias, bias], 1)
    line = lax.broadcasted_iota(jnp.int32, (TOK, HEAD), 0)
    used = line < jnp.where(line >= start, start + lens[1], lens[0])

    def stack(q, og):
        for h in range(8):
            lanes = pl.ds(h * HEAD, HEAD)
            block = pl.ds(h * TOK, TOK)
            queries[block, :] = q[:, lanes]
            cots[block, :] = jnp.where(used, og[:, lanes].astype(f32), 0.0).astype(bf16)

    pl.when(d == 0)(lambda: stack(Q.at[0], OG.at[0]))
    pl.when(d == 1)(lambda: stack(QP, OP))
    for pair in range(4):
        block = pl.ds(pair * 2 * TOK, 2 * TOK)
        q, cot = queries[block, :], cots[block, :]
        scores = lax.dot_general(K, q, (((1,), (1,)), ((), ())), preferred_element_type=f32)
        scores = scores * SCALE + bias
        top = jnp.max(scores, axis=0, keepdims=True)
        weights = jnp.exp(scores - top)
        prob = weights * (1.0 / jnp.sum(weights, axis=0, keepdims=True))
        probs[:, block] = prob.astype(bf16)
        slope = lax.dot_general(V, cot, (((1,), (1,)), ((), ())), preferred_element_type=f32)
        slope = slope.astype(bf16).astype(f32)
        inner = jnp.sum(slope * prob, axis=0, keepdims=True)
        back = (prob * ((slope - inner) * SCALE)).astype(bf16)
        slopes[:, block] = back
        made = lax.dot_general(
            back, K, (((0,), (0,)), ((), ())), preferred_element_type=f32
        ).astype(bf16)
        for i in range(2):
            QG[0, :, pl.ds((2 * pair + i) * HEAD, HEAD)] = made[i * TOK : (i + 1) * TOK]
    dv = jnp.dot(probs[...], cots[...], preferred_element_type=f32)
    dk = jnp.dot(slopes[...], queries[...], preferred_element_type=f32)
    RG[0, 0, 0] = dk[TOK:].astype(bf16)
    RG[0, 0, 1] = dv[TOK:].astype(bf16)
    for s, (zh, c) in enumerate(places):
        parts[zh, j, c] += dk[s * PRO : (s + 1) * PRO]
        parts[zh, 2 + j, c] += dv[s * PRO : (s + 1) * PRO]

    @pl.when((d == 1) & (j == 1))
    def _():
        PP[...] = parts[...].astype(bf16)


def attention(numbers, everyone, keys, vals, Q, OG, QP, OP):
    core = lambda: lax.rem(lax.axis_index("grp"), 2)
    own = pl.BlockSpec((1, TOK, 1024), lambda d, j: (0, 0, core() * 2 + jnp.maximum(d, j)))
    theirs = pl.BlockSpec((TOK, 1024), lambda d, j: (0, d * j))
    here = pl.BlockSpec((1, 1, DEV, HEAD), lambda d, j: (j, d, 0, 0))
    return pl.pallas_call(
        attention_kernel,
        out_shape=(
            jax.ShapeDtypeStruct((2, TOK, 2048), bf16),
            jax.ShapeDtypeStruct((2, 2, 2, TOK, HEAD), bf16),
            jax.ShapeDtypeStruct((4, 4, 2, PRO, HEAD), bf16),
        ),
        grid=(2, 2),
        in_specs=[SMEM] * 7 + [VMEM, here, here, own, own, theirs, theirs],
        out_specs=(
            pl.BlockSpec((1, TOK, 1024), lambda d, j: (d, 0, j)),
            pl.BlockSpec((1, 1, 2, TOK, HEAD), lambda d, j: (j, d, 0, 0, 0)),
            VMEM,
        ),
        scratch_shapes=[
            pltpu.VMEM((256, 1024), bf16),
            pltpu.VMEM((256, 1024), bf16),
            pltpu.VMEM((1024, HEAD), bf16),
            pltpu.VMEM((1024, HEAD), bf16),
            pltpu.VMEM((4, 4, 2, PRO, HEAD), f32),
        ],
        compiler_params=LOCAL,
        name="attention",
    )(*numbers, everyone, keys, vals, Q, OG, QP, OP)


RETURN_COPIES = 24


def return_kernel(PP, QG, XT, W, PS, QO, XG, W2, land, relay, send, recv):
    me = Place()
    ring, partner = me.ring_zh(), me.partner()
    links = Links(send, recv)
    columns = Move4(links, me, XT, XG, relay, 1)
    greet([ring[1], ring[2], columns.minus, columns.plus, partner])

    def add(dst, terms):
        for i in range(2):
            for d in range(2):
                total = terms[0][i, d].astype(f32)
                for term in terms[1:]:
                    total = total + term[i, d].astype(f32)
                dst[i, d] = total.astype(dst.dtype)

    going = Reduce4(
        links, ring, lambda c, h: PP.at[c, pl.ds(2 * h, 2)], lambda i: land.at[i], add
    )
    going.begin()
    columns.begin()
    queries, weights = links.take(), links.take()
    links.start(queries, QG.at[1], QO, partner)
    links.start(weights, W.at[pl.ds(2, 2)], W2, partner)
    going.mid()
    columns.forward()
    columns.hand_over(3)
    columns.hand_over(1)
    going.finish(lambda h: PS.at[pl.ds(2 * h, 2)])
    columns.hand_over(2)
    links.arrived(queries, QO, partner)
    columns.finish()
    links.arrived(weights, W2, partner)
    links.drain()
    assert links.used <= RETURN_COPIES


def give_back(PP, QG, XT, W):
    return pl.pallas_call(
        return_kernel,
        out_shape=(
            jax.ShapeDtypeStruct((4, 2, PRO, HEAD), f32),
            jax.ShapeDtypeStruct((TOK, 2048), bf16),
            X_GATHERED,
            W_SHAPE,
        ),
        in_specs=[VMEM, HBM, HBM, HBM],
        out_specs=(VMEM, HBM, HBM, HBM),
        scratch_shapes=[
            pltpu.VMEM((6, 2, 2, PRO, HEAD), bf16),
            RELAY,
            pltpu.SemaphoreType.DMA((RETURN_COPIES,)),
            pltpu.SemaphoreType.DMA((RETURN_COPIES,)),
        ],
        compiler_params=remote_params(3),
        name="give_back",
    )(PP, QG, XT, W)


SUM_COPIES = 80
I_STEP = 640


def sum_kernel(
    raw, RG, PS, turns, gain, XT, XA, XB, W, WA, WB,
    IG, WG,
    xg, w, w2, gg, theirs, acc, acc1, two, acc2, near, acc3, three, wg, send, recv, local,
):
    me = Place()
    partner = me.partner()
    near_minus, near_plus = me.near_z()
    ring_x, ring_y, ring_zh = me.ring_x(), me.ring_y(), me.ring_zh()
    core, zl = me.core, me.zl
    place = (me.x, me.y)
    fetched = {}

    def fetch(name, src, dst):
        made = pltpu.make_async_copy(src, dst, local.at[sum(len(f) for f in fetched.values())])
        made.start()
        fetched.setdefault(name, []).append(made)

    for z in range(2):
        fetch(0, XT.at[:, me.x, z], xg.at[z, 0, me.x])
        fetch(0, XT.at[me.y, :, z], xg.at[z, 1, me.y])
    for steps in (3, 1, 2):
        for kind in range(2):
            c = lax.rem(place[kind] + steps, 4)
            fetch(steps, XA.at[kind, c], xg.at[0, kind, c])
            fetch(steps, XB.at[kind, c], xg.at[1, kind, c])
    fetch("w", W, w)
    fetch("w", WA, w2.at[pl.ds(0, 2)])
    fetch("w", WB, w2.at[pl.ds(2, 2)])

    def ready(name):
        for made in fetched[name]:
            made.wait()

    greet([*ring_x[1:], *ring_y[1:], *ring_zh[1:], near_minus, near_plus, partner])
    links = Links(send, recv)

    for d in range(2):
        c, s = turns[d, 0], turns[d, 1]
        whose = core if d == 0 else 1 - core
        rows = pl.ds(d * DEV, DEV)
        for j in range(2):
            cot = jnp.concatenate([RG[j, d, 0].astype(f32), PS[j, whose]], 0)
            turned = (cot * c + swap_halves(cot * s)) * gain[...]
            k = raw[j, d]
            inverse = lax.rsqrt(jnp.mean(k * k, axis=1, keepdims=True) + 1e-06)
            along = jnp.mean(k * turned, axis=1, keepdims=True)
            back = inverse * turned - k * (inverse * inverse * inverse * along)
            gg[0, me.x, rows, pl.ds(j * HEAD, HEAD)] = back.astype(bf16)
            values = jnp.concatenate([RG[j, d, 1], PS[2 + j, whose].astype(bf16)], 0)
            gg[1, me.y, rows, pl.ds(j * HEAD, HEAD)] = values
    rounds = []
    for kind, ring in ((0, ring_x), (1, ring_y)):
        rounds.append(
            Gather4(
                links,
                ring,
                lambda c, kind=kind: gg.at[kind, c],
                lambda c, h, kind=kind: gg.at[kind, c, pl.ds(h * DEV, DEV)],
            )
        )
    for going in rounds:
        going.begin()
    crossed = links.take(), links.take()
    for kind in range(2):
        links.start(crossed[kind], gg.at[kind, place[kind], pl.ds(DEV, DEV)], theirs.at[kind], partner)

    def terms_of(steps):
        def body(i, carry):
            kind, z = lax.div(i, 2), lax.rem(i, 2)
            c = lax.rem(me.first_axis(kind) + steps, 4)
            left = jnp.concatenate([xg[z, kind, c, o] for o in range(4)], 0)
            swapped = 0 if steps == 0 else lax.rem(kind + core, 2)
            halves = [pl.ds(pl.multiple_of(h * DEV, DEV), DEV) for h in (swapped, 1 - swapped)]
            right = jnp.concatenate([gg[kind, c, h] for h in halves], 0)
            made = jnp.dot(left, right, preferred_element_type=f32)
            if steps != 0:
                made = made + acc[kind, z]
            if steps != 2:
                acc[kind, z] = made
            else:
                made = made.astype(bf16)
                for j in range(2):
                    for o in range(4):
                        acc1[2 * kind + j, o, z] = made[o * ROWS : (o + 1) * ROWS, j * HEAD : (j + 1) * HEAD]
            return carry

        lax.fori_loop(0, 4, body, 0)

    def input_part(i):
        rows = pl.ds(pl.multiple_of(i * I_STEP, I_STEP), I_STEP)
        total = 0.0
        mine = jnp.concatenate([gg[0, me.x, pl.ds(0, DEV)], gg[1, me.y, pl.ds(0, DEV)]], 1)
        others = jnp.concatenate([theirs[0], theirs[1]], 1)
        for left, right in ((mine, w), (others, w2)):
            both = jnp.concatenate([right[t, pl.ds(i * 4, 4)].reshape(I_STEP, HEAD) for t in range(4)], 1)
            total = total + lax.dot_general(
                left, both, (((1,), (1,)), ((), ())), preferred_element_type=f32
            )
        IG[:, rows] = total.astype(bf16)

    def input_parts(begin, end):
        def body(i, carry):
            input_part(i)
            return carry

        lax.fori_loop(begin, end, body, 0)

    second = []
    for t in range(4):
        second.append(
            Reduce4(
                links,
                ring_y if t < 2 else ring_x,
                lambda c, h, t=t: acc1.at[t, c, h],
                lambda i, t=t: two.at[t, i],
                add_block,
            )
        )

    class Wave:
        def __init__(self, n):
            self.n, self.slots = n, (n, 2 + n)
            self.pair = [(links.take(), near_plus), (links.take(), near_minus)]
            self.third = Reduce4(
                links, ring_zh, lambda c, h: acc3.at[n, c, cut[h]], lambda i: three.at[n, i, thirds[i]], add_block
            )
            self.last = Gather4(
                links, ring_zh, lambda c: wg.at[core, n, c], lambda c, h: wg.at[core, n, c, cut[h]]
            )
            self.across = links.take()

        def near_begin(self):
            for kind, (number, device) in enumerate(self.pair):
                links.start(number, acc2.at[self.slots[kind], 1 - zl], near.at[self.n, kind], device)

        def near_finish(self):
            for kind, (number, device) in enumerate(self.pair):
                links.arrived(number, near.at[self.n, kind], device)
                for h in range(2):
                    rows = pl.ds(h * HALF, HALF)
                    add_block(
                        acc3.at[self.n, 2 * kind + h],
                        [acc2.at[self.slots[kind], zl, rows], near.at[self.n, kind, rows]],
                    )

        def third_finish(self):
            self.third.finish(lambda h: wg.at[core, self.n, me.zh, cut[h]])

        def across_begin(self):
            links.start(self.across, wg.at[core, self.n], wg.at[core, self.n], partner)

        def across_finish(self):
            links.arrived(self.across, wg.at[1 - core, self.n], partner)

    cut = (pl.ds(0, 48), pl.ds(48, 32))
    thirds = [cut[h] for h in (0, 1, 1, 0, 0, 1)]
    waves = Wave(0), Wave(1)

    ready(0)
    terms_of(0)
    for going in rounds:
        going.forward()
    ready(3)
    terms_of(3)
    ready(1)
    terms_of(1)
    for going in rounds:
        going.finish()
    ready(2)
    terms_of(2)
    for t in (0, 2, 1, 3):
        second[t].begin()
    ready("w")
    for kind in range(2):
        links.arrived(crossed[kind], theirs.at[kind], partner)

    def settle(t):
        second[t].finish(lambda h: acc2.at[t, h])

    input_parts(0, 1)
    second[0].mid()
    second[2].mid()
    second[1].mid()
    second[3].mid()
    input_parts(1, 2)
    settle(0)
    settle(2)
    waves[0].near_begin()
    input_parts(2, 3)
    waves[0].near_finish()
    waves[0].third.begin()
    settle(1)
    settle(3)
    waves[1].near_begin()
    waves[0].third.mid()
    waves[1].near_finish()
    waves[1].third.begin()
    input_parts(3, 4)
    waves[0].third_finish()
    waves[0].last.begin()
    waves[1].third.mid()
    input_parts(4, 5)
    waves[0].last.forward()
    waves[1].third_finish()
    waves[1].last.begin()
    input_parts(5, 7)
    waves[0].last.finish()
    waves[0].across_begin()
    waves[1].last.forward()
    input_parts(7, 8)
    waves[1].last.finish()
    waves[1].across_begin()
    waves[0].across_finish()
    waves[1].across_finish()
    WG[...] = wg[...]
    links.drain()
    assert links.used <= SUM_COPIES


def sum_terms(raw, RG, PS, turns, gain, XT, XA, XB, W, WA, WB):
    return pl.pallas_call(
        sum_kernel,
        out_shape=(
            jax.ShapeDtypeStruct((DEV, WIDTH), bf16),
            jax.ShapeDtypeStruct((2, 2, 4, HALF, HEAD), bf16),
        ),
        in_specs=[VMEM] * 5 + [HBM] * 6,
        out_specs=(VMEM, VMEM),
        scratch_shapes=[
            pltpu.VMEM((2, 2, 4, 4, ROWS, 2 * DEV), bf16),
            pltpu.VMEM((4, 32, ROWS, HEAD), bf16),
            pltpu.VMEM((4, 32, ROWS, HEAD), bf16),
            pltpu.VMEM((2, 4, 2 * DEV, 256), bf16),
            pltpu.VMEM((2, DEV, 256), bf16),
            pltpu.VMEM((2, 2, 4 * ROWS, 256), f32),
            pltpu.VMEM((4, 4, 2, ROWS, HEAD), bf16),
            pltpu.VMEM((4, 6, ROWS, HEAD), bf16),
            pltpu.VMEM((4, 2, ROWS, HEAD), bf16),
            pltpu.VMEM((2, 2, ROWS, HEAD), bf16),
            pltpu.VMEM((2, 4, HALF, HEAD), bf16),
            pltpu.VMEM((2, 6, HALF, HEAD), bf16),
            pltpu.VMEM((2, 2, 4, HALF, HEAD), bf16),
            pltpu.SemaphoreType.DMA((SUM_COPIES,)),
            pltpu.SemaphoreType.DMA((SUM_COPIES,)),
            pltpu.SemaphoreType.DMA((20,)),
        ],
        compiler_params=remote_params(4),
        name="sum_terms",
    )(raw, RG, PS, turns, gain, XT, XA, XB, W, WA, WB)


def put_kernel(IG, WG, QG, QO, resp, prompt, qgrad, kout, vout):
    step = pl.program_id(0)
    core = lax.rem(lax.axis_index("grp"), 2)
    resp[0] = IG[:TOK]
    prompt[0] = IG[TOK:]

    @pl.when(step == core)
    def _():
        qgrad[0] = QG[0]

    @pl.when(step != core)
    def _():
        qgrad[0] = QO[...]

    @pl.when(step == 0)
    def _():
        for c in range(2):
            for j in range(2):
                lanes = pl.ds((2 * c + j) * HEAD, HEAD)
                kout[:, lanes] = WG[c, j, 0]
                vout[:, lanes] = WG[c, j, 1]


def put(IG, WG, QG, QO):
    half = WIDTH // 2
    return pl.pallas_call(
        put_kernel,
        out_shape=(
            jax.ShapeDtypeStruct((1, TOK, WIDTH), bf16),
            jax.ShapeDtypeStruct((1, PRO, WIDTH), bf16),
            jax.ShapeDtypeStruct((1, TOK, 4096), bf16),
            jax.ShapeDtypeStruct((ROWS, 512), bf16),
            jax.ShapeDtypeStruct((ROWS, 512), bf16),
        ),
        grid=(2,),
        in_specs=[
            pl.BlockSpec((DEV, half), lambda i: (0, i)),
            VMEM,
            pl.BlockSpec((1, TOK, 2048), lambda i: (0, 0, 0)),
            VMEM,
        ],
        out_specs=(
            pl.BlockSpec((1, TOK, half), lambda i: (0, 0, i)),
            pl.BlockSpec((1, PRO, half), lambda i: (0, 0, i)),
            pl.BlockSpec((1, TOK, 2048), lambda i: (0, 0, i)),
            VMEM,
            VMEM,
        ),
        compiler_params=LOCAL,
        name="put",
    )(IG, WG, QG, QO)


def local(
    queries, out_grad, resp_in, prompt_in, key_matrix, value_matrix, key_gain, seg_prompt, seg_start, seg_len, owner
):
    cos, sin = rotary_tables()
    gain = key_gain.reshape(1, HEAD)

    W, XP, QP, OP, SP, SS, SL = gather(
        key_matrix, value_matrix, resp_in, prompt_in, queries, out_grad, seg_prompt, seg_start, seg_len
    )
    flat = W.reshape(4, WIDTH, HEAD)
    XT, raw, keys, vals, pkv, turns = project(seg_start, SS, resp_in, prompt_in, XP, flat, cos, sin, gain)
    XT = XT.reshape(4, 4, 2, ROWS, 2 * DEV)
    everyone, XA, WA = share(pkv, XT, W)
    numbers = (seg_prompt, seg_start, seg_len, SP, SS, SL, owner)
    QG, RG, PP = attention(numbers, everyone, keys, vals, queries, out_grad, QP, OP)
    PS, QO, XB, WB = give_back(PP, QG, XT, W)
    pieces = [a.reshape(-1, 32, ROWS, HEAD) for a in (W, WA, WB)]
    IG, WG = sum_terms(raw, RG, PS, turns, gain, XT, XA, XB, *pieces)
    resp, prompt, qgrad, kout, vout = put(IG, WG.reshape(2, 2, 2, ROWS, HEAD), QG, QO)
    return qgrad, resp, prompt, kout, vout


def solution(mesh):
    in_specs = (
        P("fsdp", "grp", None),
        P("fsdp", "grp", None),
        P("fsdp", "grp", None),
        P("fsdp", "grp", None),
        P("fsdp", None),
        P("fsdp", None),
        P(),
        P("fsdp", "grp"),
        P("fsdp", "grp"),
        P("fsdp", "grp"),
        P("fsdp", None),
    )
    out_specs = (
        P("fsdp", "grp", None),
        P("fsdp", "grp", None),
        P("fsdp", "grp", None),
        P("fsdp", None),
        P("fsdp", None),
    )
    return jax.shard_map(local, mesh=mesh, in_specs=in_specs, out_specs=out_specs, check_vma=False)
```

```python
import functools
import math

import jax
import jax.numpy as jnp
import numpy as np
from jax import lax
from jax.experimental import pallas as pl
from jax.experimental.pallas import tpu as pltpu
from jax.sharding import PartitionSpec as P

MESH = pl.DeviceIdType.MESH
HBM = pl.BlockSpec(memory_space=pltpu.HBM)
SMEM = pl.BlockSpec(memory_space=pltpu.SMEM)
VMEM = pl.BlockSpec(memory_space=pltpu.VMEM)
VMEM_LIMIT = 60 * 1024 * 1024

WIDTH = 5120
HEAD = 128
ROWS = 160
HALF = 80
TOK = 128
PRO = 64
DEV = TOK + PRO
SCALE = 1.0 / math.sqrt(HEAD)
BASE = 1000000.0
bf16 = jnp.bfloat16
f32 = jnp.float32


def rotary_tables():
    frequency = np.float32(BASE) ** (-np.arange(64, dtype=np.float32) / np.float32(64))
    angles = np.arange(-128, 192, dtype=np.float32)[:, None] * frequency[None, :].astype(np.float32)
    angles = angles.astype(np.float32).astype(np.float64)
    cos, sin = np.cos(angles), np.sin(angles)
    return (
        np.concatenate([cos, cos], 1).astype(np.float32),
        np.concatenate([-sin, sin], 1).astype(np.float32),
    )


class Place:
    def __init__(self):
        g, f = lax.axis_index("grp"), lax.axis_index("fsdp")
        self.core, self.zh = lax.rem(g, 2), lax.div(g, 2)
        self.zl = lax.rem(f, 2)
        self.x = lax.rem(lax.div(f, 2), 4)
        self.y = lax.div(f, 8)
        self.z = self.zh * 2 + self.zl

    def at(self, y=None, x=None, z=None, core=None):
        y = self.y if y is None else y
        x = self.x if x is None else x
        z = self.z if z is None else z
        core = self.core if core is None else core
        return {"grp": lax.div(z, 2) * 2 + core, "fsdp": (y * 4 + x) * 2 + lax.rem(z, 2)}

    def ring_x(self):
        return self.x, self.at(x=lax.rem(self.x + 3, 4)), self.at(x=lax.rem(self.x + 1, 4))

    def ring_y(self):
        return self.y, self.at(y=lax.rem(self.y + 3, 4)), self.at(y=lax.rem(self.y + 1, 4))

    def ring_zh(self):
        return self.zh, self.at(z=lax.rem(self.z + 6, 8)), self.at(z=lax.rem(self.z + 2, 8))

    def near_z(self):
        return self.at(z=lax.rem(self.z + 7, 8)), self.at(z=lax.rem(self.z + 1, 8))

    def first_axis(self, kind):
        return self.x * (1 - kind) + self.y * kind

    def ring_of(self, kind):
        def moved(step):
            return self.at(x=lax.rem(self.x + step * (1 - kind), 4), y=lax.rem(self.y + step * kind, 4))

        return self.first_axis(kind), moved(3), moved(1)

    def partner(self):
        return self.at(core=1 - self.core)


def greet(devices):
    barrier = pltpu.get_barrier_semaphore()
    for device in devices:
        pl.semaphore_signal(barrier, inc=1, device_id=device, device_id_type=MESH)
    pl.semaphore_wait(barrier, len(devices))


class Links:
    def __init__(self, send, recv):
        self.send, self.recv, self.used, self.sent = send, recv, 0, []

    def take(self):
        self.used += 1
        return self.used - 1

    def copy(self, number, src, dst, device):
        return pltpu.make_async_remote_copy(
            src_ref=src,
            dst_ref=dst,
            send_sem=self.send.at[number],
            recv_sem=self.recv.at[number],
            device_id=device,
            device_id_type=MESH,
        )

    def start(self, number, src, dst, device):
        made = self.copy(number, src, dst, device)
        made.start()
        self.sent.append(made)

    def arrived(self, number, dst, device):
        self.copy(number, dst, dst, device).wait_recv()

    def drain(self):
        for made in self.sent:
            made.wait_send()
        self.sent = []


class Gather4:
    def __init__(self, links, ring, view, half, own=None):
        self.links, self.view, self.half = links, view, half
        self.me, self.minus, self.plus = ring
        self.own = view(self.me) if own is None else own
        self.n = [links.take() for _ in range(4)]

    def begin(self):
        self.links.start(self.n[0], self.own, self.view(self.me), self.plus)
        self.links.start(self.n[1], self.own, self.view(self.me), self.minus)

    def forward(self):
        left, right = lax.rem(self.me + 3, 4), lax.rem(self.me + 1, 4)
        self.links.arrived(self.n[0], self.view(left), self.plus)
        self.links.start(self.n[2], self.half(left, 0), self.half(left, 0), self.plus)
        self.links.arrived(self.n[1], self.view(right), self.minus)
        self.links.start(self.n[3], self.half(right, 1), self.half(right, 1), self.minus)

    def finish(self):
        across = lax.rem(self.me + 2, 4)
        self.links.arrived(self.n[2], self.half(across, 0), self.plus)
        self.links.arrived(self.n[3], self.half(across, 1), self.minus)


class Reduce4:
    def __init__(self, links, ring, part, slot, add):
        self.links, self.part, self.slot, self.add = links, part, slot, add
        self.me, self.minus, self.plus = ring
        self.n = [links.take() for _ in range(6)]

    def send_for(self, place):
        part, slot, n = self.part, self.slot, self.n
        block = lax.rem(self.me + place, 4)
        if place == 2:
            self.links.start(n[0], part(block, 0), slot(0), self.plus)
            self.links.start(n[1], part(block, 1), slot(1), self.minus)
        if place == 1:
            self.links.start(n[2], part(block, 1), slot(2), self.plus)
        if place == 3:
            self.links.start(n[3], part(block, 0), slot(3), self.minus)

    def begin(self):
        for place in (2, 1, 3):
            self.send_for(place)

    def mid(self):
        left, right = lax.rem(self.me + 3, 4), lax.rem(self.me + 1, 4)
        part, slot, n = self.part, self.slot, self.n
        self.links.arrived(n[0], slot(0), self.plus)
        self.add(slot(0), [slot(0), part(right, 0)])
        self.links.start(n[4], slot(0), slot(4), self.plus)
        self.links.arrived(n[1], slot(1), self.minus)
        self.add(slot(1), [slot(1), part(left, 1)])
        self.links.start(n[5], slot(1), slot(5), self.minus)

    def finish(self, out):
        part, slot, n = self.part, self.slot, self.n
        self.links.arrived(n[3], slot(3), self.minus)
        self.links.arrived(n[4], slot(4), self.plus)
        self.add(out(0), [part(self.me, 0), slot(3), slot(4)])
        self.links.arrived(n[2], slot(2), self.plus)
        self.links.arrived(n[5], slot(5), self.minus)
        self.add(out(1), [part(self.me, 1), slot(2), slot(5)])


def add_block(dst, terms):
    total = terms[0][...].astype(f32)
    for term in terms[1:]:
        total = total + term[...].astype(f32)
    dst[...] = total.astype(dst.dtype)


def add_blocks(dst, terms):
    def body(i, carry):
        total = terms[0][i].astype(f32)
        for term in terms[1:]:
            total = total + term[i].astype(f32)
        dst[i] = total.astype(dst.dtype)
        return carry

    lax.fori_loop(0, dst.shape[0], body, 0)


class Move4:
    def __init__(self, links, me, XT, XG, relay, zl):
        self.links, self.me, self.XT, self.XG, self.relay, self.zl = links, me, XT, XG, relay, zl
        self.place, self.minus, self.plus = me.ring_of(me.core)
        self.n = [links.take() for _ in range(9)]
        self.held = [pl.ds(0, 2), pl.ds(2, 2)]

    def from_place(self, steps):
        return lax.rem(self.place + steps, 4)

    def begin(self):
        mine = self.XG.at[self.me.core, self.place]
        jobs = (
            (0, 2, 0, self.relay.at[0], self.plus),
            (1, 2, 1, self.relay.at[1], self.minus),
            (2, 1, None, mine, self.plus),
            (3, 3, None, mine, self.minus),
        )

        def start(kind):
            for n, steps, h, dst, device in jobs:
                c = self.from_place(steps)
                rows = pl.ds(0, 4) if h is None else self.held[h]
                src = self.XT.at[rows, c, self.zl] if kind == 0 else self.XT.at[c, rows, self.zl]
                self.links.copy(self.n[n], src, dst, device).start()

        pl.when(self.me.core == 0)(lambda: start(0))
        pl.when(self.me.core == 1)(lambda: start(1))
        for n, steps, h, dst, device in jobs:
            self.links.sent.append(self.links.copy(self.n[n], dst, dst, device))

    def forward(self):
        core, n = self.me.core, self.n
        self.links.arrived(n[0], self.relay.at[0], self.plus)
        self.links.start(n[4], self.relay.at[0], self.XG.at[core, self.from_place(3), self.held[0]], self.plus)
        self.links.arrived(n[1], self.relay.at[1], self.minus)
        self.links.start(n[5], self.relay.at[1], self.XG.at[core, self.from_place(1), self.held[1]], self.minus)

    def hand_over(self, steps):
        core, n, partner = self.me.core, self.n, self.me.partner()
        view = self.XG.at[core, self.from_place(steps)]
        if steps == 3:
            self.links.arrived(n[2], view, self.plus)
        elif steps == 1:
            self.links.arrived(n[3], view, self.minus)
        else:
            c = self.from_place(2)
            self.links.arrived(n[4], self.XG.at[core, c, self.held[0]], self.plus)
            self.links.arrived(n[5], self.XG.at[core, c, self.held[1]], self.minus)
        self.links.start(n[5 + steps], view, view, partner)

    def finish(self):
        other = 1 - self.me.core
        for steps in (1, 2, 3):
            c = lax.rem(self.me.first_axis(other) + steps, 4)
            self.links.arrived(self.n[5 + steps], self.XG.at[other, c], self.me.partner())


def remote_params(number, limit=None):
    return pltpu.CompilerParams(
        collective_id=number, has_side_effects=True, vmem_limit_bytes=limit or VMEM_LIMIT
    )


LOCAL = pltpu.CompilerParams(vmem_limit_bytes=VMEM_LIMIT)


GATHER_COPIES = 64


def gather_kernel(kw, vw, resp, prompt, q, og, sp, ss, sl, W, XP, QP, OP, SP, SS, SL, send, recv, local):
    me = Place()
    core, partner = me.core, me.partner()
    near_minus, near_plus = me.near_z()
    _, xm, xp = me.ring_x()
    _, ym, yp = me.ring_y()
    greet([xm, xp, ym, yp, near_minus, near_plus, partner])
    links = Links(send, recv)

    def columns(matrix, j):
        return matrix.at[:, pl.ds(pl.multiple_of((core * 2 + j) * HEAD, HEAD), HEAD)]

    own = [columns(kw, 0), columns(kw, 1), columns(vw, 0), columns(vw, 1)]
    x, y, zl = me.x, me.y, me.zl
    rows = lambda h: pl.ds(h * HALF, HALF)

    ax = Gather4(links, me.ring_x(), lambda c: W.at[0, y, c, zl], lambda c, h: W.at[0, y, c, zl, rows(h)], own[0])
    ay = Gather4(links, me.ring_y(), lambda c: W.at[0, c, :, zl], lambda c, h: W.at[0, c, :, zl, rows(h)])
    by = Gather4(links, me.ring_y(), lambda c: W.at[1, c, x, zl], lambda c, h: W.at[1, c, x, zl, rows(h)], own[1])
    bx = Gather4(links, me.ring_x(), lambda c: W.at[1, :, c, zl], lambda c, h: W.at[1, :, c, zl, rows(h)])
    cx = Gather4(links, me.ring_x(), lambda c: W.at[2, y, c], lambda c, h: W.at[2, y, c, h])
    cy = Gather4(links, me.ring_y(), lambda c: W.at[2, c], lambda c, h: W.at[2, c, :, h])
    dy = Gather4(links, me.ring_y(), lambda c: W.at[3, c, x], lambda c, h: W.at[3, c, x, h])
    dx = Gather4(links, me.ring_x(), lambda c: W.at[3, :, c], lambda c, h: W.at[3, :, c, h])

    zn = {}

    def z_view(t, place, which, h):
        if t == 0:
            return W.at[0, lax.rem(y + place, 4), :, which, rows(h)]
        if t == 1:
            return W.at[1, :, lax.rem(x + place, 4), which, rows(h)]
        return W.at[t, y, x, which, rows(h)]

    def z_begin(t, place, src=None):
        zn[t, place] = links.take(), links.take()
        for h, device in ((0, near_plus), (1, near_minus)):
            view = z_view(t, place, zl, h)
            links.start(zn[t, place][h], view if src is None else src(h), view, device)

    def z_finish(t, place):
        for h, device in ((0, near_plus), (1, near_minus)):
            links.arrived(zn[t, place][h], z_view(t, place, 1 - zl, h), device)

    ax.begin()
    by.begin()
    for t in (2, 3):
        matrix_half = lambda h, t=t: vw.at[rows(h), pl.ds(pl.multiple_of((core * 2 + t - 2) * HEAD, HEAD), HEAD)]
        z_begin(t, 0, matrix_half)

    locals_ = []

    def here(src, dst):
        made = pltpu.make_async_copy(src, dst, local.at[len(locals_)])
        made.start()
        locals_.append(made)

    for t in range(4):
        here(own[t], W.at[t, y, x, zl])
    swaps = []

    def swap(src, dst):
        number = links.take()
        links.start(number, src, dst, partner)
        swaps.append((number, dst))

    theirs = pl.ds(pl.multiple_of((1 - core) * 2048, 2048), 2048)
    swap(sp, SP)
    swap(ss, SS)
    swap(sl, SL)
    swap(resp.at[0], XP.at[pl.ds(0, TOK)])
    swap(prompt.at[0], XP.at[pl.ds(TOK, PRO)])
    swap(q.at[0, :, theirs], QP)
    swap(og.at[0, :, theirs], OP)

    ax.forward()
    by.forward()
    for made in locals_:
        made.wait()
    z_finish(2, 0)
    cx.begin()
    z_finish(3, 0)
    dy.begin()
    ax.finish()
    ay.begin()
    z_begin(0, 0)
    by.finish()
    bx.begin()
    z_begin(1, 0)
    cx.forward()
    dy.forward()
    cx.finish()
    cy.begin()
    dy.finish()
    dx.begin()
    ay.forward()
    z_begin(0, 3)
    z_begin(0, 1)
    bx.forward()
    z_begin(1, 3)
    z_begin(1, 1)
    ay.finish()
    z_begin(0, 2)
    bx.finish()
    z_begin(1, 2)
    cy.forward()
    dx.forward()
    for place in range(4):
        z_finish(0, place)
        z_finish(1, place)
    cy.finish()
    dx.finish()
    for number, landing in swaps:
        links.arrived(number, landing, partner)
    links.drain()
    assert links.used <= GATHER_COPIES


def gather(kw, vw, resp, prompt, q, og, sp, ss, sl):
    return pl.pallas_call(
        gather_kernel,
        out_shape=(
            jax.ShapeDtypeStruct((4, 4, 4, 2, ROWS, HEAD), bf16),
            jax.ShapeDtypeStruct((DEV, WIDTH), bf16),
            jax.ShapeDtypeStruct((TOK, 2048), bf16),
            jax.ShapeDtypeStruct((TOK, 2048), bf16),
            jax.ShapeDtypeStruct((1, 2), jnp.int32),
            jax.ShapeDtypeStruct((1, 2), jnp.int32),
            jax.ShapeDtypeStruct((1, 2), jnp.int32),
        ),
        in_specs=[HBM] * 9,
        out_specs=(HBM,) * 7,
        scratch_shapes=[
            pltpu.SemaphoreType.DMA((GATHER_COPIES,)),
            pltpu.SemaphoreType.DMA((GATHER_COPIES,)),
            pltpu.SemaphoreType.DMA((4,)),
        ],
        compiler_params=remote_params(1),
        name="gather",
    )(kw, vw, resp, prompt, q, og, sp, ss, sl)


K_STEP = 1024


def swap_halves(a):
    return pltpu.roll(a, 64, 1)


def tables_of(starts, cos, sin):
    start = starts[0, 1]
    late = pl.multiple_of(192 - start, 16)
    row = lax.broadcasted_iota(jnp.int32, (TOK, HEAD), 0)
    out = []
    for table in (cos, sin):
        first = table[pl.ds(192, TOK), :]
        second = table[pl.ds(late, TOK), :]
        out.append(jnp.concatenate([jnp.where(row < start, first, second), table[pl.ds(128, PRO), :]], 0))
    return out


def project_kernel(ss, SS, resp, prompt, XP, W, cos, sin, gain, XT, raw, keys, vals, pkv, turns, acc):
    step = pl.program_id(0)
    left = jnp.concatenate([resp[0], prompt[0], XP[...]], 0)
    right = jnp.concatenate([W[t] for t in range(4)], 1)
    part = jnp.dot(left, right, preferred_element_type=f32)
    XT[...] = left.T

    @pl.when(step == 0)
    def _():
        acc[...] = part

    @pl.when(step > 0)
    def _():
        acc[...] += part

    @pl.when(step == pl.num_programs(0) - 1)
    def _():
        for d in range(2):
            c, s = tables_of((ss, SS)[d], cos, sin)
            turns[d, 0], turns[d, 1] = c, s
            core = lax.rem(lax.axis_index("grp") + d, 2)
            for j in range(2):
                k = acc[pl.ds(d * DEV, DEV), pl.ds(j * HEAD, HEAD)]
                raw[j, d] = k
                square = jnp.mean(k * k, axis=1, keepdims=True)
                normed = k * lax.rsqrt(square + 1e-06) * gain[...]
                turned = (normed * c + swap_halves(normed) * s).astype(bf16)
                keys[j, d] = turned
                pkv[j, core] = turned[TOK:]
                v = acc[pl.ds(d * DEV, DEV), pl.ds((2 + j) * HEAD, HEAD)].astype(bf16)
                vals[j, d] = v
                pkv[2 + j, core] = v[TOK:]


def project(ss, SS, resp, prompt, XP, W, cos, sin, gain):
    return pl.pallas_call(
        project_kernel,
        out_shape=(
            jax.ShapeDtypeStruct((WIDTH, 2 * DEV), bf16),
            jax.ShapeDtypeStruct((2, 2, DEV, HEAD), f32),
            jax.ShapeDtypeStruct((2, 2, DEV, HEAD), bf16),
            jax.ShapeDtypeStruct((2, 2, DEV, HEAD), bf16),
            jax.ShapeDtypeStruct((4, 2, PRO, HEAD), bf16),
            jax.ShapeDtypeStruct((2, 2, DEV, HEAD), f32),
        ),
        grid=(WIDTH // K_STEP,),
        in_specs=[
            SMEM,
            SMEM,
            pl.BlockSpec((1, TOK, K_STEP), lambda i: (0, 0, i)),
            pl.BlockSpec((1, PRO, K_STEP), lambda i: (0, 0, i)),
            pl.BlockSpec((DEV, K_STEP), lambda i: (0, i)),
            pl.BlockSpec((4, K_STEP, HEAD), lambda i: (0, i, 0)),
            VMEM,
            VMEM,
            VMEM,
        ],
        out_specs=(pl.BlockSpec((K_STEP, 2 * DEV), lambda i: (i, 0)),) + (VMEM,) * 5,
        scratch_shapes=[pltpu.VMEM((2 * DEV, 512), f32)],
        compiler_params=LOCAL,
        name="project",
    )(ss, SS, resp, prompt, XP, W, cos, sin, gain)


ATTEND_COPIES = 40


def attend_kernel(
    sp, ss, sl, SP, SS, SL, owner, pkv, keys, vals, q, og, QP, OP, XT, W,
    QG, QO, RG, PS, XG, W2,
    everyone, queries, cots, rows_q, rows_g, probs, slopes, made_q, parts, PP, land, relay, send, recv, local,
):
    me = Place()
    core, partner = me.core, me.partner()
    ring = me.ring_zh()
    links = Links(send, recv)
    out = Gather4(links, ring, lambda c: everyone.at[c], lambda c, h: everyone.at[c, pl.ds(2 * h, 2)], pkv)
    columns = [Move4(links, me, XT, XG.at[z], relay.at[z], z) for z in range(2)]
    weights, swapped = links.take(), links.take()
    greet([ring[1], ring[2], columns[0].minus, columns[0].plus, partner])
    mine = pl.ds(pl.multiple_of(core * 2048, 2048), 2048)
    locals_ = []
    out.begin()
    for src, dst in (
        (pkv, everyone.at[me.zh]),
        (q.at[0, :, mine], rows_q.at[0]),
        (og.at[0, :, mine], rows_g.at[0]),
        (QP, rows_q.at[1]),
        (OP, rows_g.at[1]),
    ):
        made = pltpu.make_async_copy(src, dst, local.at[len(locals_)])
        made.start()
        locals_.append(made)
    columns[0].begin()
    columns[1].begin()
    links.start(weights, W, W2, partner)
    parts[...] = jnp.zeros_like(parts)
    out.forward()
    columns[0].forward()
    out.finish()
    for made in locals_:
        made.wait()

    def attend(i, carry):
        d, j = lax.div(i, 2), lax.rem(i, 2)

        def number(own, other, n):
            return jnp.where(d == 0, own[0, n], other[0, n])

        def slot_of(prompt):
            slot = 0
            for p in range(8):
                slot = slot + jnp.where(prompt == p, owner[0, p], 0)
            return slot

        slots = [slot_of(number(sp, SP, n)) for n in range(2)]
        start, lens = number(ss, SS, 1), [number(sl, SL, n) for n in range(2)]
        chosen = [[jnp.where(s == slot, 1.0, 0.0) for slot in range(8)] for s in slots]

        def pick(t, own):
            blocks = []
            for one in chosen:
                total = 0.0
                for slot in range(8):
                    total = total + everyone[slot // 2, t, slot % 2].astype(f32) * one[slot]
                blocks.append(total.astype(bf16))
            return jnp.concatenate(blocks + [own], 0)

        K = pick(j, keys[j, d, :TOK])
        V = pick(2 + j, vals[j, d, :TOK])

        key = lax.broadcasted_iota(jnp.int32, (2 * TOK, TOK), 0)
        row = lax.broadcasted_iota(jnp.int32, (2 * TOK, TOK), 1)
        late = row >= start
        first = jnp.where(late, start, 0)
        end = jnp.where(late, start + lens[1], lens[0])
        from_key = jnp.where(key < TOK, jnp.where(late, PRO, 0), first + TOK)
        to_key = jnp.where(key < TOK, jnp.where(late, TOK, PRO), jnp.minimum(end, row + 1) + TOK)
        bias = jnp.where((key >= from_key) & (key < to_key), 0.0, -1e30)
        bias = jnp.concatenate([bias, bias], 1)
        line = lax.broadcasted_iota(jnp.int32, (TOK, HEAD), 0)
        used = line < jnp.where(line >= start, start + lens[1], lens[0])

        def lanes(h):
            return pl.ds(pl.multiple_of(j * 1024 + h * HEAD, HEAD), HEAD)

        for h in range(8):
            block = pl.ds(h * TOK, TOK)
            queries[block, :] = rows_q[d, :, lanes(h)]
            cots[block, :] = jnp.where(used, rows_g[d, :, lanes(h)].astype(f32), 0.0).astype(bf16)
        for pair in range(4):
            block = pl.ds(pair * 2 * TOK, 2 * TOK)
            query, cot = queries[block, :], cots[block, :]
            scores = lax.dot_general(K, query, (((1,), (1,)), ((), ())), preferred_element_type=f32)
            scores = scores * SCALE + bias
            top = jnp.max(scores, axis=0, keepdims=True)
            exps = jnp.exp(scores - top)
            prob = exps * (1.0 / jnp.sum(exps, axis=0, keepdims=True))
            probs[:, block] = prob.astype(bf16)
            slope = lax.dot_general(V, cot, (((1,), (1,)), ((), ())), preferred_element_type=f32)
            slope = slope.astype(bf16).astype(f32)
            inner = jnp.sum(slope * prob, axis=0, keepdims=True)
            back = (prob * ((slope - inner) * SCALE)).astype(bf16)
            slopes[:, block] = back
            grad = lax.dot_general(
                back, K, (((0,), (0,)), ((), ())), preferred_element_type=f32
            ).astype(bf16)
            for n in range(2):
                made_q[d, :, lanes(2 * pair + n)] = grad[n * TOK : (n + 1) * TOK]
        dv = jnp.dot(probs[...], cots[...], preferred_element_type=f32)
        dk = jnp.dot(slopes[...], queries[...], preferred_element_type=f32)
        RG[j, d, 0] = dk[TOK:].astype(bf16)
        RG[j, d, 1] = dv[TOK:].astype(bf16)
        for slot in range(8):
            for t, grad in ((j, dk), (2 + j, dv)):
                parts[slot // 2, t, slot % 2] += (
                    grad[:PRO] * chosen[0][slot] + grad[PRO:TOK] * chosen[1][slot]
                )
        return carry

    lax.fori_loop(2, 4, attend, 0)
    links.start(swapped, made_q.at[1], QO, partner)
    columns[1].forward()
    for steps in (3, 1, 2):
        columns[0].hand_over(steps)
    lax.fori_loop(0, 2, attend, 0)
    PP[...] = parts[...].astype(bf16)

    def add(dst, terms):
        for i in range(2):
            for d in range(2):
                total = terms[0][i, d].astype(f32)
                for term in terms[1:]:
                    total = total + term[i, d].astype(f32)
                dst[i, d] = total.astype(dst.dtype)

    home = Reduce4(links, ring, lambda c, h: PP.at[c, pl.ds(2 * h, 2)], lambda i: land.at[i], add)
    home.begin()
    for steps in (3, 1, 2):
        columns[1].hand_over(steps)
    QG[...] = made_q[0]
    home.mid()
    home.finish(lambda h: PS.at[pl.ds(2 * h, 2)])
    columns[0].finish()
    columns[1].finish()
    links.arrived(weights, W2, partner)
    links.arrived(swapped, QO, partner)
    links.drain()
    assert links.used <= ATTEND_COPIES


def attend(numbers, pkv, keys, vals, q, og, QP, OP, XT, W):
    return pl.pallas_call(
        attend_kernel,
        out_shape=(
            jax.ShapeDtypeStruct((TOK, 2048), bf16),
            jax.ShapeDtypeStruct((TOK, 2048), bf16),
            jax.ShapeDtypeStruct((2, 2, 2, TOK, HEAD), bf16),
            jax.ShapeDtypeStruct((4, 2, PRO, HEAD), f32),
            jax.ShapeDtypeStruct((2, 2, 4, 4, ROWS, 2 * DEV), bf16),
            jax.ShapeDtypeStruct((4, 4, 4, 2, ROWS, HEAD), bf16),
        ),
        in_specs=[SMEM] * 7 + [VMEM] * 3 + [HBM] * 6,
        out_specs=(VMEM, HBM, VMEM, VMEM, HBM, HBM),
        scratch_shapes=[
            pltpu.VMEM((4, 4, 2, PRO, HEAD), bf16),
            pltpu.VMEM((1024, HEAD), bf16),
            pltpu.VMEM((1024, HEAD), bf16),
            pltpu.VMEM((2, TOK, 2048), bf16),
            pltpu.VMEM((2, TOK, 2048), bf16),
            pltpu.VMEM((256, 1024), bf16),
            pltpu.VMEM((256, 1024), bf16),
            pltpu.VMEM((2, TOK, 2048), bf16),
            pltpu.VMEM((4, 4, 2, PRO, HEAD), f32),
            pltpu.VMEM((4, 4, 2, PRO, HEAD), bf16),
            pltpu.VMEM((6, 2, 2, PRO, HEAD), bf16),
            pltpu.VMEM((2, 2, 2, ROWS, 2 * DEV), bf16),
            pltpu.SemaphoreType.DMA((ATTEND_COPIES,)),
            pltpu.SemaphoreType.DMA((ATTEND_COPIES,)),
            pltpu.SemaphoreType.DMA((5,)),
        ],
        compiler_params=remote_params(2),
        name="attend",
    )(*numbers, pkv, keys, vals, q, og, QP, OP, XT, W)


SUM_COPIES = 80
I_STEP = 640


def sum_kernel(
    raw, RG, PS, turns, gain, XT, XG, W, W2,
    IG, WG,
    xg, w, w2, gg, theirs, acc, acc1, two, acc2, near, acc3, three, wg, send, recv, local,
):
    me = Place()
    partner = me.partner()
    near_minus, near_plus = me.near_z()
    ring_x, ring_y, ring_zh = me.ring_x(), me.ring_y(), me.ring_zh()
    core, zl = me.core, me.zl
    place = (me.x, me.y)
    fetched = {}

    def fetch(name, src, dst):
        made = pltpu.make_async_copy(src, dst, local.at[sum(len(f) for f in fetched.values())])
        made.start()
        fetched.setdefault(name, []).append(made)

    for z in range(2):
        fetch(0, XT.at[:, me.x, z], xg.at[z, 0, me.x])
        fetch(0, XT.at[me.y, :, z], xg.at[z, 1, me.y])
    for steps in (3, 1, 2):
        for kind in range(2):
            c = lax.rem(place[kind] + steps, 4)
            for z in range(2):
                fetch(steps, XG.at[z, kind, c], xg.at[z, kind, c])
    fetch("w", W, w)
    fetch("w", W2, w2)

    def ready(name):
        for made in fetched[name]:
            made.wait()

    greet([*ring_x[1:], *ring_y[1:], *ring_zh[1:], near_minus, near_plus, partner])
    links = Links(send, recv)

    for d in range(2):
        c, s = turns[d, 0], turns[d, 1]
        whose = core if d == 0 else 1 - core
        rows = pl.ds(d * DEV, DEV)
        for j in range(2):
            cot = jnp.concatenate([RG[j, d, 0].astype(f32), PS[j, whose]], 0)
            turned = (cot * c + swap_halves(cot * s)) * gain[...]
            k = raw[j, d]
            inverse = lax.rsqrt(jnp.mean(k * k, axis=1, keepdims=True) + 1e-06)
            along = jnp.mean(k * turned, axis=1, keepdims=True)
            back = inverse * turned - k * (inverse * inverse * inverse * along)
            gg[0, me.x, rows, pl.ds(j * HEAD, HEAD)] = back.astype(bf16)
            values = jnp.concatenate([RG[j, d, 1], PS[2 + j, whose].astype(bf16)], 0)
            gg[1, me.y, rows, pl.ds(j * HEAD, HEAD)] = values
    rounds = []
    for kind, ring in ((0, ring_x), (1, ring_y)):
        rounds.append(
            Gather4(
                links,
                ring,
                lambda c, kind=kind: gg.at[kind, c],
                lambda c, h, kind=kind: gg.at[kind, c, pl.ds(h * DEV, DEV)],
            )
        )
    for going in rounds:
        going.begin()
    crossed = links.take(), links.take()
    for kind in range(2):
        links.start(crossed[kind], gg.at[kind, place[kind], pl.ds(DEV, DEV)], theirs.at[kind], partner)

    def terms_of(steps):
        def body(i, carry):
            kind, z = lax.div(i, 2), lax.rem(i, 2)
            c = lax.rem(me.first_axis(kind) + steps, 4)
            left = jnp.concatenate([xg[z, kind, c, o] for o in range(4)], 0)
            swapped = 0 if steps == 0 else lax.rem(kind + core, 2)
            halves = [pl.ds(pl.multiple_of(h * DEV, DEV), DEV) for h in (swapped, 1 - swapped)]
            right = jnp.concatenate([gg[kind, c, h] for h in halves], 0)
            made = jnp.dot(left, right, preferred_element_type=f32)
            if steps != 0:
                made = made + acc[kind, z]
            if steps != 2:
                acc[kind, z] = made
            else:
                made = made.astype(bf16)
                for j in range(2):
                    for o in range(4):
                        acc1[2 * kind + j, o, z] = made[o * ROWS : (o + 1) * ROWS, j * HEAD : (j + 1) * HEAD]
            return carry

        lax.fori_loop(0, 4, body, 0)

    def input_part(i):
        rows = pl.ds(pl.multiple_of(i * I_STEP, I_STEP), I_STEP)
        total = 0.0
        mine = jnp.concatenate([gg[0, me.x, pl.ds(0, DEV)], gg[1, me.y, pl.ds(0, DEV)]], 1)
        others = jnp.concatenate([theirs[0], theirs[1]], 1)
        for left, right in ((mine, w), (others, w2)):
            both = jnp.concatenate([right[t, pl.ds(i * 4, 4)].reshape(I_STEP, HEAD) for t in range(4)], 1)
            total = total + lax.dot_general(
                left, both, (((1,), (1,)), ((), ())), preferred_element_type=f32
            )
        IG[:, rows] = total.astype(bf16)

    def input_parts(begin, end):
        def body(i, carry):
            input_part(i)
            return carry

        lax.fori_loop(begin, end, body, 0)

    second = []
    for t in range(4):
        second.append(
            Reduce4(
                links,
                ring_y if t < 2 else ring_x,
                lambda c, h, t=t: acc1.at[t, c, h],
                lambda i, t=t: two.at[t, i],
                add_block,
            )
        )

    class Wave:
        def __init__(self, n):
            self.n, self.slots = n, (n, 2 + n)
            self.pair = [(links.take(), near_plus), (links.take(), near_minus)]
            self.third = Reduce4(
                links, ring_zh, lambda c, h: acc3.at[n, c, cut[h]], lambda i: three.at[n, i, thirds[i]], add_block
            )
            self.last = Gather4(
                links, ring_zh, lambda c: wg.at[core, n, c], lambda c, h: wg.at[core, n, c, cut[h]]
            )
            self.across = links.take()

        def near_begin(self):
            for kind, (number, device) in enumerate(self.pair):
                links.start(number, acc2.at[self.slots[kind], 1 - zl], near.at[self.n, kind], device)

        def near_finish(self):
            for kind, (number, device) in enumerate(self.pair):
                links.arrived(number, near.at[self.n, kind], device)
                for h in range(2):
                    rows = pl.ds(h * HALF, HALF)
                    add_block(
                        acc3.at[self.n, 2 * kind + h],
                        [acc2.at[self.slots[kind], zl, rows], near.at[self.n, kind, rows]],
                    )

        def third_finish(self):
            self.third.finish(lambda h: wg.at[core, self.n, me.zh, cut[h]])

        def across_begin(self):
            links.start(self.across, wg.at[core, self.n], wg.at[core, self.n], partner)

        def across_finish(self):
            links.arrived(self.across, wg.at[1 - core, self.n], partner)

    cut = (pl.ds(0, 48), pl.ds(48, 32))
    thirds = [cut[h] for h in (0, 1, 1, 0, 0, 1)]
    waves = Wave(0), Wave(1)

    ready(0)
    terms_of(0)
    for going in rounds:
        going.forward()
    ready(3)
    terms_of(3)
    ready(1)
    terms_of(1)
    for going in rounds:
        going.finish()
    ready(2)
    terms_of(2)
    for t in (0, 2, 1, 3):
        second[t].begin()
    ready("w")
    for kind in range(2):
        links.arrived(crossed[kind], theirs.at[kind], partner)

    def settle(t):
        second[t].finish(lambda h: acc2.at[t, h])

    input_parts(0, 1)
    second[0].mid()
    second[2].mid()
    second[1].mid()
    second[3].mid()
    input_parts(1, 2)
    settle(0)
    settle(2)
    waves[0].near_begin()
    input_parts(2, 3)
    waves[0].near_finish()
    waves[0].third.begin()
    settle(1)
    settle(3)
    waves[1].near_begin()
    waves[0].third.mid()
    waves[1].near_finish()
    waves[1].third.begin()
    input_parts(3, 4)
    waves[0].third_finish()
    waves[0].last.begin()
    waves[1].third.mid()
    input_parts(4, 5)
    waves[0].last.forward()
    waves[1].third_finish()
    waves[1].last.begin()
    input_parts(5, 7)
    waves[0].last.finish()
    waves[0].across_begin()
    waves[1].last.forward()
    input_parts(7, 8)
    waves[1].last.finish()
    waves[1].across_begin()
    waves[0].across_finish()
    waves[1].across_finish()
    WG[...] = wg[...]
    links.drain()
    assert links.used <= SUM_COPIES


def sum_terms(raw, RG, PS, turns, gain, XT, XG, W, W2):
    return pl.pallas_call(
        sum_kernel,
        out_shape=(
            jax.ShapeDtypeStruct((DEV, WIDTH), bf16),
            jax.ShapeDtypeStruct((2, 2, 4, HALF, HEAD), bf16),
        ),
        in_specs=[VMEM] * 5 + [HBM] * 4,
        out_specs=(VMEM, VMEM),
        scratch_shapes=[
            pltpu.VMEM((2, 2, 4, 4, ROWS, 2 * DEV), bf16),
            pltpu.VMEM((4, 32, ROWS, HEAD), bf16),
            pltpu.VMEM((4, 32, ROWS, HEAD), bf16),
            pltpu.VMEM((2, 4, 2 * DEV, 256), bf16),
            pltpu.VMEM((2, DEV, 256), bf16),
            pltpu.VMEM((2, 2, 4 * ROWS, 256), f32),
            pltpu.VMEM((4, 4, 2, ROWS, HEAD), bf16),
            pltpu.VMEM((4, 6, ROWS, HEAD), bf16),
            pltpu.VMEM((4, 2, ROWS, HEAD), bf16),
            pltpu.VMEM((2, 2, ROWS, HEAD), bf16),
            pltpu.VMEM((2, 4, HALF, HEAD), bf16),
            pltpu.VMEM((2, 6, HALF, HEAD), bf16),
            pltpu.VMEM((2, 2, 4, HALF, HEAD), bf16),
            pltpu.SemaphoreType.DMA((SUM_COPIES,)),
            pltpu.SemaphoreType.DMA((SUM_COPIES,)),
            pltpu.SemaphoreType.DMA((20,)),
        ],
        compiler_params=remote_params(4),
        name="sum_terms",
    )(raw, RG, PS, turns, gain, XT, XG, W, W2)


def put_kernel(IG, WG, QG, QO, resp, prompt, qgrad, kout, vout):
    step = pl.program_id(0)
    core = lax.rem(lax.axis_index("grp"), 2)
    resp[0] = IG[:TOK]
    prompt[0] = IG[TOK:]

    @pl.when(step == core)
    def _():
        qgrad[0] = QG[...]

    @pl.when(step != core)
    def _():
        qgrad[0] = QO[...]

    @pl.when(step == 0)
    def _():
        for c in range(2):
            for j in range(2):
                lanes = pl.ds((2 * c + j) * HEAD, HEAD)
                kout[:, lanes] = WG[c, j, 0]
                vout[:, lanes] = WG[c, j, 1]


def put(IG, WG, QG, QO):
    half = WIDTH // 2
    return pl.pallas_call(
        put_kernel,
        out_shape=(
            jax.ShapeDtypeStruct((1, TOK, WIDTH), bf16),
            jax.ShapeDtypeStruct((1, PRO, WIDTH), bf16),
            jax.ShapeDtypeStruct((1, TOK, 4096), bf16),
            jax.ShapeDtypeStruct((ROWS, 512), bf16),
            jax.ShapeDtypeStruct((ROWS, 512), bf16),
        ),
        grid=(2,),
        in_specs=[
            pl.BlockSpec((DEV, half), lambda i: (0, i)),
            VMEM,
            VMEM,
            VMEM,
        ],
        out_specs=(
            pl.BlockSpec((1, TOK, half), lambda i: (0, 0, i)),
            pl.BlockSpec((1, PRO, half), lambda i: (0, 0, i)),
            pl.BlockSpec((1, TOK, 2048), lambda i: (0, 0, i)),
            VMEM,
            VMEM,
        ),
        compiler_params=LOCAL,
        name="put",
    )(IG, WG, QG, QO)


def local(
    queries, out_grad, resp_in, prompt_in, key_matrix, value_matrix, key_gain, seg_prompt, seg_start, seg_len, owner
):
    cos, sin = rotary_tables()
    gain = key_gain.reshape(1, HEAD)

    W, XP, QP, OP, SP, SS, SL = gather(
        key_matrix, value_matrix, resp_in, prompt_in, queries, out_grad, seg_prompt, seg_start, seg_len
    )
    flat = W.reshape(4, WIDTH, HEAD)
    XT, raw, keys, vals, pkv, turns = project(seg_start, SS, resp_in, prompt_in, XP, flat, cos, sin, gain)
    XT = XT.reshape(4, 4, 2, ROWS, 2 * DEV)
    numbers = (seg_prompt, seg_start, seg_len, SP, SS, SL, owner)
    QG, QO, RG, PS, XG, W2 = attend(numbers, pkv, keys, vals, queries, out_grad, QP, OP, XT, W)
    pieces = [a.reshape(4, 32, ROWS, HEAD) for a in (W, W2)]
    IG, WG = sum_terms(raw, RG, PS, turns, gain, XT, XG, *pieces)
    resp, prompt, qgrad, kout, vout = put(IG, WG.reshape(2, 2, 2, ROWS, HEAD), QG, QO)
    return qgrad, resp, prompt, kout, vout


def solution(mesh):
    in_specs = (
        P("fsdp", "grp", None),
        P("fsdp", "grp", None),
        P("fsdp", "grp", None),
        P("fsdp", "grp", None),
        P("fsdp", None),
        P("fsdp", None),
        P(),
        P("fsdp", "grp"),
        P("fsdp", "grp"),
        P("fsdp", "grp"),
        P("fsdp", None),
    )
    out_specs = (
        P("fsdp", "grp", None),
        P("fsdp", "grp", None),
        P("fsdp", "grp", None),
        P("fsdp", None),
        P("fsdp", None),
    )
    return jax.shard_map(local, mesh=mesh, in_specs=in_specs, out_specs=out_specs, check_vma=False)
```

```python
import functools
import math

import jax
import jax.numpy as jnp
import numpy as np
from jax import lax
from jax.experimental import pallas as pl
from jax.experimental.pallas import tpu as pltpu
from jax.sharding import PartitionSpec as P

MESH = pl.DeviceIdType.MESH
HBM = pl.BlockSpec(memory_space=pltpu.HBM)
SMEM = pl.BlockSpec(memory_space=pltpu.SMEM)
VMEM = pl.BlockSpec(memory_space=pltpu.VMEM)
VMEM_LIMIT = 60 * 1024 * 1024

WIDTH = 5120
HEAD = 128
ROWS = 160
HALF = 80
TOK = 128
PRO = 64
DEV = TOK + PRO
SCALE = 1.0 / math.sqrt(HEAD)
BASE = 1000000.0
bf16 = jnp.bfloat16
f32 = jnp.float32


def rotary_tables():
    frequency = np.float32(BASE) ** (-np.arange(64, dtype=np.float32) / np.float32(64))
    angles = np.arange(-128, 192, dtype=np.float32)[:, None] * frequency[None, :].astype(np.float32)
    angles = angles.astype(np.float32).astype(np.float64)
    cos, sin = np.cos(angles), np.sin(angles)
    return (
        np.concatenate([cos, cos], 1).astype(np.float32),
        np.concatenate([-sin, sin], 1).astype(np.float32),
    )


class Place:
    def __init__(self):
        g, f = lax.axis_index("grp"), lax.axis_index("fsdp")
        self.core, self.zh = lax.rem(g, 2), lax.div(g, 2)
        self.zl = lax.rem(f, 2)
        self.x = lax.rem(lax.div(f, 2), 4)
        self.y = lax.div(f, 8)
        self.z = self.zh * 2 + self.zl

    def at(self, y=None, x=None, z=None, core=None):
        y = self.y if y is None else y
        x = self.x if x is None else x
        z = self.z if z is None else z
        core = self.core if core is None else core
        return {"grp": lax.div(z, 2) * 2 + core, "fsdp": (y * 4 + x) * 2 + lax.rem(z, 2)}

    def ring_x(self):
        return self.x, self.at(x=lax.rem(self.x + 3, 4)), self.at(x=lax.rem(self.x + 1, 4))

    def ring_y(self):
        return self.y, self.at(y=lax.rem(self.y + 3, 4)), self.at(y=lax.rem(self.y + 1, 4))

    def ring_zh(self):
        return self.zh, self.at(z=lax.rem(self.z + 6, 8)), self.at(z=lax.rem(self.z + 2, 8))

    def near_z(self):
        return self.at(z=lax.rem(self.z + 7, 8)), self.at(z=lax.rem(self.z + 1, 8))

    def first_axis(self, kind):
        return self.x * (1 - kind) + self.y * kind

    def ring_of(self, kind):
        def moved(step):
            return self.at(x=lax.rem(self.x + step * (1 - kind), 4), y=lax.rem(self.y + step * kind, 4))

        return self.first_axis(kind), moved(3), moved(1)

    def partner(self):
        return self.at(core=1 - self.core)


def greet(devices):
    barrier = pltpu.get_barrier_semaphore()
    for device in devices:
        pl.semaphore_signal(barrier, inc=1, device_id=device, device_id_type=MESH)
    pl.semaphore_wait(barrier, len(devices))


class Links:
    def __init__(self, send, recv):
        self.send, self.recv, self.used, self.sent = send, recv, 0, []

    def take(self):
        self.used += 1
        return self.used - 1

    def copy(self, number, src, dst, device):
        return pltpu.make_async_remote_copy(
            src_ref=src,
            dst_ref=dst,
            send_sem=self.send.at[number],
            recv_sem=self.recv.at[number],
            device_id=device,
            device_id_type=MESH,
        )

    def start(self, number, src, dst, device):
        made = self.copy(number, src, dst, device)
        made.start()
        self.sent.append(made)

    def arrived(self, number, dst, device):
        self.copy(number, dst, dst, device).wait_recv()

    def drain(self):
        for made in self.sent:
            made.wait_send()
        self.sent = []


class Gather4:
    def __init__(self, links, ring, view, half, own=None):
        self.links, self.view, self.half = links, view, half
        self.me, self.minus, self.plus = ring
        self.own = view(self.me) if own is None else own
        self.n = [links.take() for _ in range(4)]

    def begin(self):
        self.links.start(self.n[0], self.own, self.view(self.me), self.plus)
        self.links.start(self.n[1], self.own, self.view(self.me), self.minus)

    def forward(self):
        left, right = lax.rem(self.me + 3, 4), lax.rem(self.me + 1, 4)
        self.links.arrived(self.n[0], self.view(left), self.plus)
        self.links.start(self.n[2], self.half(left, 0), self.half(left, 0), self.plus)
        self.links.arrived(self.n[1], self.view(right), self.minus)
        self.links.start(self.n[3], self.half(right, 1), self.half(right, 1), self.minus)

    def finish(self):
        across = lax.rem(self.me + 2, 4)
        self.links.arrived(self.n[2], self.half(across, 0), self.plus)
        self.links.arrived(self.n[3], self.half(across, 1), self.minus)


class Reduce4:
    def __init__(self, links, ring, part, slot, add):
        self.links, self.part, self.slot, self.add = links, part, slot, add
        self.me, self.minus, self.plus = ring
        self.n = [links.take() for _ in range(6)]

    def send_for(self, place):
        part, slot, n = self.part, self.slot, self.n
        block = lax.rem(self.me + place, 4)
        if place == 2:
            self.links.start(n[0], part(block, 0), slot(0), self.plus)
            self.links.start(n[1], part(block, 1), slot(1), self.minus)
        if place == 1:
            self.links.start(n[2], part(block, 1), slot(2), self.plus)
        if place == 3:
            self.links.start(n[3], part(block, 0), slot(3), self.minus)

    def begin(self):
        for place in (2, 1, 3):
            self.send_for(place)

    def mid(self):
        left, right = lax.rem(self.me + 3, 4), lax.rem(self.me + 1, 4)
        part, slot, n = self.part, self.slot, self.n
        self.links.arrived(n[0], slot(0), self.plus)
        self.add(slot(0), [slot(0), part(right, 0)])
        self.links.start(n[4], slot(0), slot(4), self.plus)
        self.links.arrived(n[1], slot(1), self.minus)
        self.add(slot(1), [slot(1), part(left, 1)])
        self.links.start(n[5], slot(1), slot(5), self.minus)

    def finish(self, out):
        part, slot, n = self.part, self.slot, self.n
        self.links.arrived(n[3], slot(3), self.minus)
        self.links.arrived(n[4], slot(4), self.plus)
        self.add(out(0), [part(self.me, 0), slot(3), slot(4)])
        self.links.arrived(n[2], slot(2), self.plus)
        self.links.arrived(n[5], slot(5), self.minus)
        self.add(out(1), [part(self.me, 1), slot(2), slot(5)])


def add_block(dst, terms):
    total = terms[0][...].astype(f32)
    for term in terms[1:]:
        total = total + term[...].astype(f32)
    dst[...] = total.astype(dst.dtype)


def add_blocks(dst, terms):
    def body(i, carry):
        total = terms[0][i].astype(f32)
        for term in terms[1:]:
            total = total + term[i].astype(f32)
        dst[i] = total.astype(dst.dtype)
        return carry

    lax.fori_loop(0, dst.shape[0], body, 0)


class Move4:
    def __init__(self, links, me, XT, XG, relay, zl):
        self.links, self.me, self.XT, self.XG, self.relay, self.zl = links, me, XT, XG, relay, zl
        self.place, self.minus, self.plus = me.ring_of(me.core)
        self.n = [links.take() for _ in range(9)]
        self.held = [pl.ds(0, 2), pl.ds(2, 2)]

    def from_place(self, steps):
        return lax.rem(self.place + steps, 4)

    def send(self, jobs):
        def start(kind):
            for n, steps, h, dst, device in jobs:
                c = self.from_place(steps)
                rows = pl.ds(0, 4) if h is None else self.held[h]
                src = self.XT.at[rows, c, self.zl] if kind == 0 else self.XT.at[c, rows, self.zl]
                self.links.copy(self.n[n], src, dst, device).start()

        pl.when(self.me.core == 0)(lambda: start(0))
        pl.when(self.me.core == 1)(lambda: start(1))
        for n, steps, h, dst, device in jobs:
            self.links.sent.append(self.links.copy(self.n[n], dst, dst, device))

    def begin(self):
        self.send([(0, 2, 0, self.relay.at[0], self.plus), (1, 2, 1, self.relay.at[1], self.minus)])

    def direct(self):
        mine = self.XG.at[self.me.core, self.place]
        self.send([(2, 1, None, mine, self.plus), (3, 3, None, mine, self.minus)])

    def forward(self):
        core, n = self.me.core, self.n
        self.links.arrived(n[0], self.relay.at[0], self.plus)
        self.links.start(n[4], self.relay.at[0], self.XG.at[core, self.from_place(3), self.held[0]], self.plus)
        self.links.arrived(n[1], self.relay.at[1], self.minus)
        self.links.start(n[5], self.relay.at[1], self.XG.at[core, self.from_place(1), self.held[1]], self.minus)

    def hand_over(self, steps):
        core, n, partner = self.me.core, self.n, self.me.partner()
        view = self.XG.at[core, self.from_place(steps)]
        if steps == 3:
            self.links.arrived(n[2], view, self.plus)
        elif steps == 1:
            self.links.arrived(n[3], view, self.minus)
        else:
            c = self.from_place(2)
            self.links.arrived(n[4], self.XG.at[core, c, self.held[0]], self.plus)
            self.links.arrived(n[5], self.XG.at[core, c, self.held[1]], self.minus)
        self.links.start(n[5 + steps], view, view, partner)

    def finish(self):
        other = 1 - self.me.core
        for steps in (1, 2, 3):
            c = lax.rem(self.me.first_axis(other) + steps, 4)
            self.links.arrived(self.n[5 + steps], self.XG.at[other, c], self.me.partner())


def remote_params(number, limit=None):
    return pltpu.CompilerParams(
        collective_id=number, has_side_effects=True, vmem_limit_bytes=limit or VMEM_LIMIT
    )


LOCAL = pltpu.CompilerParams(vmem_limit_bytes=VMEM_LIMIT)


GATHER_COPIES = 64


def gather_kernel(kw, vw, resp, prompt, q, og, sp, ss, sl, W, XP, QP, OP, SP, SS, SL, send, recv, local):
    me = Place()
    core, partner = me.core, me.partner()
    near_minus, near_plus = me.near_z()
    _, xm, xp = me.ring_x()
    _, ym, yp = me.ring_y()
    greet([xm, xp, ym, yp, near_minus, near_plus, partner])
    links = Links(send, recv)

    def columns(matrix, j):
        return matrix.at[:, pl.ds(pl.multiple_of((core * 2 + j) * HEAD, HEAD), HEAD)]

    own = [columns(kw, 0), columns(kw, 1), columns(vw, 0), columns(vw, 1)]
    x, y, zl = me.x, me.y, me.zl
    rows = lambda h: pl.ds(h * HALF, HALF)

    ax = Gather4(links, me.ring_x(), lambda c: W.at[0, y, c, zl], lambda c, h: W.at[0, y, c, zl, rows(h)], own[0])
    ay = Gather4(links, me.ring_y(), lambda c: W.at[0, c, :, zl], lambda c, h: W.at[0, c, :, zl, rows(h)])
    by = Gather4(links, me.ring_y(), lambda c: W.at[1, c, x, zl], lambda c, h: W.at[1, c, x, zl, rows(h)], own[1])
    bx = Gather4(links, me.ring_x(), lambda c: W.at[1, :, c, zl], lambda c, h: W.at[1, :, c, zl, rows(h)])
    cx = Gather4(links, me.ring_x(), lambda c: W.at[2, y, c], lambda c, h: W.at[2, y, c, h])
    cy = Gather4(links, me.ring_y(), lambda c: W.at[2, c], lambda c, h: W.at[2, c, :, h])
    dy = Gather4(links, me.ring_y(), lambda c: W.at[3, c, x], lambda c, h: W.at[3, c, x, h])
    dx = Gather4(links, me.ring_x(), lambda c: W.at[3, :, c], lambda c, h: W.at[3, :, c, h])

    zn = {}

    def z_view(t, place, which, h):
        if t == 0:
            return W.at[0, lax.rem(y + place, 4), :, which, rows(h)]
        if t == 1:
            return W.at[1, :, lax.rem(x + place, 4), which, rows(h)]
        return W.at[t, y, x, which, rows(h)]

    def z_begin(t, place, src=None):
        zn[t, place] = links.take(), links.take()
        for h, device in ((0, near_plus), (1, near_minus)):
            view = z_view(t, place, zl, h)
            links.start(zn[t, place][h], view if src is None else src(h), view, device)

    def z_finish(t, place):
        for h, device in ((0, near_plus), (1, near_minus)):
            links.arrived(zn[t, place][h], z_view(t, place, 1 - zl, h), device)

    ax.begin()
    by.begin()
    for t in (2, 3):
        matrix_half = lambda h, t=t: vw.at[rows(h), pl.ds(pl.multiple_of((core * 2 + t - 2) * HEAD, HEAD), HEAD)]
        z_begin(t, 0, matrix_half)

    locals_ = []

    def here(src, dst):
        made = pltpu.make_async_copy(src, dst, local.at[len(locals_)])
        made.start()
        locals_.append(made)

    for t in range(4):
        here(own[t], W.at[t, y, x, zl])
    swaps = []

    def swap(src, dst):
        number = links.take()
        links.start(number, src, dst, partner)
        swaps.append((number, dst))

    theirs = pl.ds(pl.multiple_of((1 - core) * 2048, 2048), 2048)
    swap(sp, SP)
    swap(ss, SS)
    swap(sl, SL)
    swap(resp.at[0], XP.at[pl.ds(0, TOK)])
    swap(prompt.at[0], XP.at[pl.ds(TOK, PRO)])
    swap(q.at[0, :, theirs], QP)
    swap(og.at[0, :, theirs], OP)

    ax.forward()
    by.forward()
    for made in locals_:
        made.wait()
    z_finish(2, 0)
    cx.begin()
    z_finish(3, 0)
    dy.begin()
    ax.finish()
    ay.begin()
    z_begin(0, 0)
    by.finish()
    bx.begin()
    z_begin(1, 0)
    cx.forward()
    dy.forward()
    cx.finish()
    cy.begin()
    dy.finish()
    dx.begin()
    ay.forward()
    z_begin(0, 3)
    z_begin(0, 1)
    bx.forward()
    z_begin(1, 3)
    z_begin(1, 1)
    ay.finish()
    z_begin(0, 2)
    bx.finish()
    z_begin(1, 2)
    cy.forward()
    dx.forward()
    for place in range(4):
        z_finish(0, place)
        z_finish(1, place)
    cy.finish()
    dx.finish()
    for number, landing in swaps:
        links.arrived(number, landing, partner)
    links.drain()
    assert links.used <= GATHER_COPIES


def gather(kw, vw, resp, prompt, q, og, sp, ss, sl):
    return pl.pallas_call(
        gather_kernel,
        out_shape=(
            jax.ShapeDtypeStruct((4, 4, 4, 2, ROWS, HEAD), bf16),
            jax.ShapeDtypeStruct((DEV, WIDTH), bf16),
            jax.ShapeDtypeStruct((TOK, 2048), bf16),
            jax.ShapeDtypeStruct((TOK, 2048), bf16),
            jax.ShapeDtypeStruct((1, 2), jnp.int32),
            jax.ShapeDtypeStruct((1, 2), jnp.int32),
            jax.ShapeDtypeStruct((1, 2), jnp.int32),
        ),
        in_specs=[HBM] * 9,
        out_specs=(HBM,) * 7,
        scratch_shapes=[
            pltpu.SemaphoreType.DMA((GATHER_COPIES,)),
            pltpu.SemaphoreType.DMA((GATHER_COPIES,)),
            pltpu.SemaphoreType.DMA((4,)),
        ],
        compiler_params=remote_params(1),
        name="gather",
    )(kw, vw, resp, prompt, q, og, sp, ss, sl)


K_STEP = 1024


def swap_halves(a):
    return pltpu.roll(a, 64, 1)


def tables_of(starts, cos, sin):
    start = starts[0, 1]
    late = pl.multiple_of(192 - start, 16)
    row = lax.broadcasted_iota(jnp.int32, (TOK, HEAD), 0)
    out = []
    for table in (cos, sin):
        first = table[pl.ds(192, TOK), :]
        second = table[pl.ds(late, TOK), :]
        out.append(jnp.concatenate([jnp.where(row < start, first, second), table[pl.ds(128, PRO), :]], 0))
    return out


def project_kernel(ss, SS, resp, prompt, XP, W, cos, sin, gain, XT, raw, keys, vals, pkv, turns, acc):
    step = pl.program_id(0)
    left = jnp.concatenate([resp[0], prompt[0], XP[...]], 0)
    right = jnp.concatenate([W[t] for t in range(4)], 1)
    part = jnp.dot(left, right, preferred_element_type=f32)
    XT[...] = left.T

    @pl.when(step == 0)
    def _():
        acc[...] = part

    @pl.when(step > 0)
    def _():
        acc[...] += part

    @pl.when(step == pl.num_programs(0) - 1)
    def _():
        for d in range(2):
            c, s = tables_of((ss, SS)[d], cos, sin)
            turns[d, 0], turns[d, 1] = c, s
            core = lax.rem(lax.axis_index("grp") + d, 2)
            for j in range(2):
                k = acc[pl.ds(d * DEV, DEV), pl.ds(j * HEAD, HEAD)]
                raw[j, d] = k
                square = jnp.mean(k * k, axis=1, keepdims=True)
                normed = k * lax.rsqrt(square + 1e-06) * gain[...]
                turned = (normed * c + swap_halves(normed) * s).astype(bf16)
                keys[j, d] = turned
                pkv[j, core] = turned[TOK:]
                v = acc[pl.ds(d * DEV, DEV), pl.ds((2 + j) * HEAD, HEAD)].astype(bf16)
                vals[j, d] = v
                pkv[2 + j, core] = v[TOK:]


def project(ss, SS, resp, prompt, XP, W, cos, sin, gain):
    return pl.pallas_call(
        project_kernel,
        out_shape=(
            jax.ShapeDtypeStruct((WIDTH, 2 * DEV), bf16),
            jax.ShapeDtypeStruct((2, 2, DEV, HEAD), f32),
            jax.ShapeDtypeStruct((2, 2, DEV, HEAD), bf16),
            jax.ShapeDtypeStruct((2, 2, DEV, HEAD), bf16),
            jax.ShapeDtypeStruct((4, 2, PRO, HEAD), bf16),
            jax.ShapeDtypeStruct((2, 2, DEV, HEAD), f32),
        ),
        grid=(WIDTH // K_STEP,),
        in_specs=[
            SMEM,
            SMEM,
            pl.BlockSpec((1, TOK, K_STEP), lambda i: (0, 0, i)),
            pl.BlockSpec((1, PRO, K_STEP), lambda i: (0, 0, i)),
            pl.BlockSpec((DEV, K_STEP), lambda i: (0, i)),
            pl.BlockSpec((4, K_STEP, HEAD), lambda i: (0, i, 0)),
            VMEM,
            VMEM,
            VMEM,
        ],
        out_specs=(pl.BlockSpec((K_STEP, 2 * DEV), lambda i: (i, 0)),) + (VMEM,) * 5,
        scratch_shapes=[pltpu.VMEM((2 * DEV, 512), f32)],
        compiler_params=LOCAL,
        name="project",
    )(ss, SS, resp, prompt, XP, W, cos, sin, gain)


ATTEND_COPIES = 40


def attend_kernel(
    sp, ss, sl, SP, SS, SL, owner, pkv, keys, vals, q, og, QP, OP, XT, W,
    QG, QO, RG, PS, XG, W2,
    everyone, queries, cots, rows_q, rows_g, probs, slopes, made_q, parts, PP, land, relay, send, recv, local,
):
    me = Place()
    core, partner = me.core, me.partner()
    ring = me.ring_zh()
    links = Links(send, recv)
    out = Gather4(links, ring, lambda c: everyone.at[c], lambda c, h: everyone.at[c, pl.ds(2 * h, 2)], pkv)
    columns = [Move4(links, me, XT, XG.at[z], relay.at[z], z) for z in range(2)]
    weights, swapped = links.take(), links.take()
    greet([ring[1], ring[2], columns[0].minus, columns[0].plus, partner])
    mine = pl.ds(pl.multiple_of(core * 2048, 2048), 2048)
    locals_ = []
    out.begin()
    for src, dst in (
        (pkv, everyone.at[me.zh]),
        (q.at[0, :, mine], rows_q.at[0]),
        (og.at[0, :, mine], rows_g.at[0]),
        (QP, rows_q.at[1]),
        (OP, rows_g.at[1]),
    ):
        made = pltpu.make_async_copy(src, dst, local.at[len(locals_)])
        made.start()
        locals_.append(made)
    columns[0].begin()
    columns[1].begin()
    links.start(weights, W, W2, partner)
    parts[...] = jnp.zeros_like(parts)
    out.forward()
    out.finish()
    for half in columns:
        half.forward()
    for half in columns:
        half.direct()
    for made in locals_:
        made.wait()

    def attend(i, carry):
        d, j = lax.div(i, 2), lax.rem(i, 2)

        def number(own, other, n):
            return jnp.where(d == 0, own[0, n], other[0, n])

        def slot_of(prompt):
            slot = 0
            for p in range(8):
                slot = slot + jnp.where(prompt == p, owner[0, p], 0)
            return slot

        slots = [slot_of(number(sp, SP, n)) for n in range(2)]
        start, lens = number(ss, SS, 1), [number(sl, SL, n) for n in range(2)]
        chosen = [[jnp.where(s == slot, 1.0, 0.0) for slot in range(8)] for s in slots]

        def pick(t, own):
            blocks = []
            for one in chosen:
                total = 0.0
                for slot in range(8):
                    total = total + everyone[slot // 2, t, slot % 2].astype(f32) * one[slot]
                blocks.append(total.astype(bf16))
            return jnp.concatenate(blocks + [own], 0)

        K = pick(j, keys[j, d, :TOK])
        V = pick(2 + j, vals[j, d, :TOK])

        key = lax.broadcasted_iota(jnp.int32, (2 * TOK, TOK), 0)
        row = lax.broadcasted_iota(jnp.int32, (2 * TOK, TOK), 1)
        late = row >= start
        first = jnp.where(late, start, 0)
        end = jnp.where(late, start + lens[1], lens[0])
        from_key = jnp.where(key < TOK, jnp.where(late, PRO, 0), first + TOK)
        to_key = jnp.where(key < TOK, jnp.where(late, TOK, PRO), jnp.minimum(end, row + 1) + TOK)
        bias = jnp.where((key >= from_key) & (key < to_key), 0.0, -1e30)
        bias = jnp.concatenate([bias, bias], 1)
        line = lax.broadcasted_iota(jnp.int32, (TOK, HEAD), 0)
        used = line < jnp.where(line >= start, start + lens[1], lens[0])

        def lanes(h):
            return pl.ds(pl.multiple_of(j * 1024 + h * HEAD, HEAD), HEAD)

        for h in range(8):
            block = pl.ds(h * TOK, TOK)
            queries[block, :] = rows_q[d, :, lanes(h)]
            cots[block, :] = jnp.where(used, rows_g[d, :, lanes(h)].astype(f32), 0.0).astype(bf16)
        for pair in range(4):
            block = pl.ds(pair * 2 * TOK, 2 * TOK)
            query, cot = queries[block, :], cots[block, :]
            scores = lax.dot_general(K, query, (((1,), (1,)), ((), ())), preferred_element_type=f32)
            scores = scores * SCALE + bias
            top = jnp.max(scores, axis=0, keepdims=True)
            exps = jnp.exp(scores - top)
            prob = exps * (1.0 / jnp.sum(exps, axis=0, keepdims=True))
            probs[:, block] = prob.astype(bf16)
            slope = lax.dot_general(V, cot, (((1,), (1,)), ((), ())), preferred_element_type=f32)
            slope = slope.astype(bf16).astype(f32)
            inner = jnp.sum(slope * prob, axis=0, keepdims=True)
            back = (prob * ((slope - inner) * SCALE)).astype(bf16)
            slopes[:, block] = back
            grad = lax.dot_general(
                back, K, (((0,), (0,)), ((), ())), preferred_element_type=f32
            ).astype(bf16)
            for n in range(2):
                made_q[d, :, lanes(2 * pair + n)] = grad[n * TOK : (n + 1) * TOK]
        dv = jnp.dot(probs[...], cots[...], preferred_element_type=f32)
        dk = jnp.dot(slopes[...], queries[...], preferred_element_type=f32)
        RG[j, d, 0] = dk[TOK:].astype(bf16)
        RG[j, d, 1] = dv[TOK:].astype(bf16)
        for slot in range(8):
            for t, grad in ((j, dk), (2 + j, dv)):
                parts[slot // 2, t, slot % 2] += (
                    grad[:PRO] * chosen[0][slot] + grad[PRO:TOK] * chosen[1][slot]
                )
        return carry

    lax.fori_loop(2, 4, attend, 0)
    links.start(swapped, made_q.at[1], QO, partner)
    lax.fori_loop(0, 2, attend, 0)
    PP[...] = parts[...].astype(bf16)

    def add(dst, terms):
        for i in range(2):
            for d in range(2):
                total = terms[0][i, d].astype(f32)
                for term in terms[1:]:
                    total = total + term[i, d].astype(f32)
                dst[i, d] = total.astype(dst.dtype)

    home = Reduce4(links, ring, lambda c, h: PP.at[c, pl.ds(2 * h, 2)], lambda i: land.at[i], add)
    home.begin()
    QG[...] = made_q[0]
    columns[0].hand_over(2)
    home.mid()
    for half, steps in ((1, 2), (0, 3), (0, 1), (1, 3), (1, 1)):
        columns[half].hand_over(steps)
    home.finish(lambda h: PS.at[pl.ds(2 * h, 2)])
    columns[0].finish()
    columns[1].finish()
    links.arrived(weights, W2, partner)
    links.arrived(swapped, QO, partner)
    links.drain()
    assert links.used <= ATTEND_COPIES


def attend(numbers, pkv, keys, vals, q, og, QP, OP, XT, W):
    return pl.pallas_call(
        attend_kernel,
        out_shape=(
            jax.ShapeDtypeStruct((TOK, 2048), bf16),
            jax.ShapeDtypeStruct((TOK, 2048), bf16),
            jax.ShapeDtypeStruct((2, 2, 2, TOK, HEAD), bf16),
            jax.ShapeDtypeStruct((4, 2, PRO, HEAD), f32),
            jax.ShapeDtypeStruct((2, 2, 4, 4, ROWS, 2 * DEV), bf16),
            jax.ShapeDtypeStruct((4, 4, 4, 2, ROWS, HEAD), bf16),
        ),
        in_specs=[SMEM] * 7 + [VMEM] * 3 + [HBM] * 6,
        out_specs=(VMEM, HBM, VMEM, VMEM, HBM, HBM),
        scratch_shapes=[
            pltpu.VMEM((4, 4, 2, PRO, HEAD), bf16),
            pltpu.VMEM((1024, HEAD), bf16),
            pltpu.VMEM((1024, HEAD), bf16),
            pltpu.VMEM((2, TOK, 2048), bf16),
            pltpu.VMEM((2, TOK, 2048), bf16),
            pltpu.VMEM((256, 1024), bf16),
            pltpu.VMEM((256, 1024), bf16),
            pltpu.VMEM((2, TOK, 2048), bf16),
            pltpu.VMEM((4, 4, 2, PRO, HEAD), f32),
            pltpu.VMEM((4, 4, 2, PRO, HEAD), bf16),
            pltpu.VMEM((6, 2, 2, PRO, HEAD), bf16),
            pltpu.VMEM((2, 2, 2, ROWS, 2 * DEV), bf16),
            pltpu.SemaphoreType.DMA((ATTEND_COPIES,)),
            pltpu.SemaphoreType.DMA((ATTEND_COPIES,)),
            pltpu.SemaphoreType.DMA((5,)),
        ],
        compiler_params=remote_params(2),
        name="attend",
    )(*numbers, pkv, keys, vals, q, og, QP, OP, XT, W)


SUM_COPIES = 80
I_STEP = 640


def sum_kernel(
    raw_, RG_, PS_, turns_, gain, XT, XG, W, W2,
    IG, WG,
    xg, w, w2, gg, theirs, acc, acc1, two, blocks, near, wg, raw, RG, PS, turns, send, recv, local,
):
    me = Place()
    partner = me.partner()
    ring_x, ring_y = me.ring_x(), me.ring_y()
    core, zl = me.core, me.zl
    place = (me.x, me.y)
    fetched = {}

    def fetch(name, src, dst):
        made = pltpu.make_async_copy(src, dst, local.at[sum(len(f) for f in fetched.values())])
        made.start()
        fetched.setdefault(name, []).append(made)

    for src, dst in ((raw_, raw), (RG_, RG), (PS_, PS), (turns_, turns)):
        fetch("small", src, dst)
    for z in range(2):
        fetch(0, XT.at[:, me.x, z], xg.at[z, 0, me.x])
        fetch(0, XT.at[me.y, :, z], xg.at[z, 1, me.y])
    for steps in (3, 1, 2):
        for kind in range(2):
            c = lax.rem(place[kind] + steps, 4)
            for z in range(2):
                fetch(steps, XG.at[z, kind, c], xg.at[z, kind, c])
    fetch("w", W, w)
    fetch("w", W2, w2)

    def ready(name):
        for made in fetched[name]:
            made.wait()

    greet([*ring_x[1:], *ring_y[1:], *[me.at(z=lax.rem(me.z + k, 8)) for k in range(1, 8)], partner])
    ready("small")
    links = Links(send, recv)

    for d in range(2):
        c, s = turns[d, 0], turns[d, 1]
        whose = core if d == 0 else 1 - core
        rows = pl.ds(d * DEV, DEV)
        for j in range(2):
            cot = jnp.concatenate([RG[j, d, 0].astype(f32), PS[j, whose]], 0)
            turned = (cot * c + swap_halves(cot * s)) * gain[...]
            k = raw[j, d]
            inverse = lax.rsqrt(jnp.mean(k * k, axis=1, keepdims=True) + 1e-06)
            along = jnp.mean(k * turned, axis=1, keepdims=True)
            back = inverse * turned - k * (inverse * inverse * inverse * along)
            gg[0, me.x, rows, pl.ds(j * HEAD, HEAD)] = back.astype(bf16)
            values = jnp.concatenate([RG[j, d, 1], PS[2 + j, whose].astype(bf16)], 0)
            gg[1, me.y, rows, pl.ds(j * HEAD, HEAD)] = values
    rounds = []
    for kind, ring in ((0, ring_x), (1, ring_y)):
        rounds.append(
            Gather4(
                links,
                ring,
                lambda c, kind=kind: gg.at[kind, c],
                lambda c, h, kind=kind: gg.at[kind, c, pl.ds(h * DEV, DEV)],
            )
        )
    for going in rounds:
        going.begin()
    crossed = links.take(), links.take()
    for kind in range(2):
        links.start(crossed[kind], gg.at[kind, place[kind], pl.ds(DEV, DEV)], theirs.at[kind], partner)

    def terms_of(steps):
        def body(i, carry):
            kind, z = lax.div(i, 2), lax.rem(i, 2)
            c = lax.rem(me.first_axis(kind) + steps, 4)
            left = jnp.concatenate([xg[z, kind, c, o] for o in range(4)], 0)
            swapped = 0 if steps == 0 else lax.rem(kind + core, 2)
            halves = [pl.ds(pl.multiple_of(h * DEV, DEV), DEV) for h in (swapped, 1 - swapped)]
            right = jnp.concatenate([gg[kind, c, h] for h in halves], 0)
            made = jnp.dot(left, right, preferred_element_type=f32)
            if steps != 0:
                made = made + acc[kind, z]
            if steps != 2:
                acc[kind, z] = made
            else:
                made = made.astype(bf16)
                for j in range(2):
                    for o in range(4):
                        acc1[2 * kind + j, o, z] = made[o * ROWS : (o + 1) * ROWS, j * HEAD : (j + 1) * HEAD]
            return carry

        lax.fori_loop(0, 4, body, 0)

    def input_part(i):
        rows = pl.ds(pl.multiple_of(i * I_STEP, I_STEP), I_STEP)
        total = 0.0
        mine = jnp.concatenate([gg[0, me.x, pl.ds(0, DEV)], gg[1, me.y, pl.ds(0, DEV)]], 1)
        others = jnp.concatenate([theirs[0], theirs[1]], 1)
        for left, right in ((mine, w), (others, w2)):
            both = jnp.concatenate([right[t, pl.ds(i * 4, 4)].reshape(I_STEP, HEAD) for t in range(4)], 1)
            total = total + lax.dot_general(
                left, both, (((1,), (1,)), ((), ())), preferred_element_type=f32
            )
        IG[:, rows] = total.astype(bf16)

    def input_parts(begin, end):
        def body(i, carry):
            input_part(i)
            return carry

        lax.fori_loop(begin, end, body, 0)

    second = []
    for t in range(4):
        second.append(
            Reduce4(
                links,
                ring_y if t < 2 else ring_x,
                lambda c, h, t=t: acc1.at[t, c, h],
                lambda i, t=t: two.at[t, i],
                add_block,
            )
        )

    class Wave:
        def __init__(self, n):
            self.n = n
            self.down = [links.take() for _ in range(7)]
            self.round = [links.take() for _ in range(3)]
            self.across = links.take()

        def sum_begin(self):
            for k in (4, 3, 5, 2, 6, 1, 7):
                z = lax.rem(me.z + k, 8)
                block = blocks.at[self.n, lax.rem(z, 2), lax.div(z, 2)]
                links.start(self.down[k - 1], block, near.at[self.n, k - 1], me.at(z=z))

        def sum_finish(self):
            for k in range(1, 8):
                links.arrived(self.down[k - 1], near.at[self.n, k - 1], partner)
            add_block(
                wg.at[core, self.n, me.zh],
                [blocks.at[self.n, zl, me.zh]] + [near.at[self.n, k] for k in range(7)],
            )

        def round_begin(self):
            mine = wg.at[core, self.n, me.zh]
            for k in (2, 1, 3):
                links.start(self.round[k - 1], mine, mine, me.at(z=lax.rem(me.z + 2 * k, 8)))

        def round_finish(self):
            for k in (1, 2, 3):
                links.arrived(self.round[k - 1], wg.at[core, self.n, lax.rem(me.zh + 4 - k, 4)], partner)

        def across_begin(self):
            links.start(self.across, wg.at[core, self.n], wg.at[core, self.n], partner)

        def across_finish(self):
            links.arrived(self.across, wg.at[1 - core, self.n], partner)

    waves = Wave(0), Wave(1)

    ready(0)
    terms_of(0)
    for going in rounds:
        going.forward()
    ready(3)
    terms_of(3)
    ready(1)
    terms_of(1)
    for going in rounds:
        going.finish()
    ready(2)
    terms_of(2)
    for t in (0, 2, 1, 3):
        second[t].begin()
    ready("w")
    for kind in range(2):
        links.arrived(crossed[kind], theirs.at[kind], partner)

    def settle(t):
        def add(dst, terms):
            total = terms[0][...].astype(f32)
            for term in terms[1:]:
                total = total + term[...].astype(f32)
            total = total.astype(bf16)
            for i in range(2):
                dst[2 * (t // 2) + i] = total[i * HALF : (i + 1) * HALF]

        second[t].add = add
        second[t].finish(lambda h: blocks.at[t % 2, h])

    input_parts(0, 1)
    second[0].mid()
    second[2].mid()
    second[1].mid()
    second[3].mid()
    input_parts(1, 2)
    settle(0)
    settle(2)
    waves[0].sum_begin()
    settle(1)
    settle(3)
    waves[1].sum_begin()
    input_parts(2, 4)
    waves[0].sum_finish()
    waves[0].round_begin()
    waves[1].sum_finish()
    waves[1].round_begin()
    input_parts(4, 6)
    waves[0].round_finish()
    waves[0].across_begin()
    waves[1].round_finish()
    waves[1].across_begin()
    input_parts(6, 8)
    waves[0].across_finish()
    waves[1].across_finish()
    WG[...] = wg[...]
    links.drain()
    assert links.used <= SUM_COPIES


def sum_terms(raw, RG, PS, turns, gain, XT, XG, W, W2):
    return pl.pallas_call(
        sum_kernel,
        out_shape=(
            jax.ShapeDtypeStruct((DEV, WIDTH), bf16),
            jax.ShapeDtypeStruct((2, 2, 4, HALF, HEAD), bf16),
        ),
        in_specs=[HBM] * 4 + [VMEM] + [HBM] * 4,
        out_specs=(VMEM, VMEM),
        scratch_shapes=[
            pltpu.VMEM((2, 2, 4, 4, ROWS, 2 * DEV), bf16),
            pltpu.VMEM((4, 32, ROWS, HEAD), bf16),
            pltpu.VMEM((4, 32, ROWS, HEAD), bf16),
            pltpu.VMEM((2, 4, 2 * DEV, 256), bf16),
            pltpu.VMEM((2, DEV, 256), bf16),
            pltpu.VMEM((2, 2, 4 * ROWS, 256), f32),
            pltpu.VMEM((4, 4, 2, ROWS, HEAD), bf16),
            pltpu.VMEM((4, 6, ROWS, HEAD), bf16),
            pltpu.VMEM((2, 2, 4, HALF, HEAD), bf16),
            pltpu.VMEM((2, 7, HALF, HEAD), bf16),
            pltpu.VMEM((2, 2, 4, HALF, HEAD), bf16),
            pltpu.VMEM((2, 2, DEV, HEAD), f32),
            pltpu.VMEM((2, 2, 2, TOK, HEAD), bf16),
            pltpu.VMEM((4, 2, PRO, HEAD), f32),
            pltpu.VMEM((2, 2, DEV, HEAD), f32),
            pltpu.SemaphoreType.DMA((SUM_COPIES,)),
            pltpu.SemaphoreType.DMA((SUM_COPIES,)),
            pltpu.SemaphoreType.DMA((24,)),
        ],
        compiler_params=remote_params(4),
        name="sum_terms",
    )(raw, RG, PS, turns, gain, XT, XG, W, W2)


def put_kernel(IG, WG, QG, QO, resp, prompt, qgrad, kout, vout):
    step = pl.program_id(0)
    core = lax.rem(lax.axis_index("grp"), 2)
    resp[0] = IG[:TOK]
    prompt[0] = IG[TOK:]

    @pl.when(step == core)
    def _():
        qgrad[0] = QG[...]

    @pl.when(step != core)
    def _():
        qgrad[0] = QO[...]

    @pl.when(step == 0)
    def _():
        for c in range(2):
            for j in range(2):
                lanes = pl.ds((2 * c + j) * HEAD, HEAD)
                kout[:, lanes] = WG[c, j, 0]
                vout[:, lanes] = WG[c, j, 1]


def put(IG, WG, QG, QO):
    half = WIDTH // 2
    return pl.pallas_call(
        put_kernel,
        out_shape=(
            jax.ShapeDtypeStruct((1, TOK, WIDTH), bf16),
            jax.ShapeDtypeStruct((1, PRO, WIDTH), bf16),
            jax.ShapeDtypeStruct((1, TOK, 4096), bf16),
            jax.ShapeDtypeStruct((ROWS, 512), bf16),
            jax.ShapeDtypeStruct((ROWS, 512), bf16),
        ),
        grid=(2,),
        in_specs=[
            pl.BlockSpec((DEV, half), lambda i: (0, i)),
            VMEM,
            VMEM,
            VMEM,
        ],
        out_specs=(
            pl.BlockSpec((1, TOK, half), lambda i: (0, 0, i)),
            pl.BlockSpec((1, PRO, half), lambda i: (0, 0, i)),
            pl.BlockSpec((1, TOK, 2048), lambda i: (0, 0, i)),
            VMEM,
            VMEM,
        ),
        compiler_params=LOCAL,
        name="put",
    )(IG, WG, QG, QO)


def local(
    queries, out_grad, resp_in, prompt_in, key_matrix, value_matrix, key_gain, seg_prompt, seg_start, seg_len, owner
):
    cos, sin = rotary_tables()
    gain = key_gain.reshape(1, HEAD)

    W, XP, QP, OP, SP, SS, SL = gather(
        key_matrix, value_matrix, resp_in, prompt_in, queries, out_grad, seg_prompt, seg_start, seg_len
    )
    flat = W.reshape(4, WIDTH, HEAD)
    XT, raw, keys, vals, pkv, turns = project(seg_start, SS, resp_in, prompt_in, XP, flat, cos, sin, gain)
    XT = XT.reshape(4, 4, 2, ROWS, 2 * DEV)
    numbers = (seg_prompt, seg_start, seg_len, SP, SS, SL, owner)
    QG, QO, RG, PS, XG, W2 = attend(numbers, pkv, keys, vals, queries, out_grad, QP, OP, XT, W)
    pieces = [a.reshape(4, 32, ROWS, HEAD) for a in (W, W2)]
    IG, WG = sum_terms(raw, RG, PS, turns, gain, XT, XG, *pieces)
    resp, prompt, qgrad, kout, vout = put(IG, WG.reshape(2, 2, 2, ROWS, HEAD), QG, QO)
    return qgrad, resp, prompt, kout, vout


def solution(mesh):
    in_specs = (
        P("fsdp", "grp", None),
        P("fsdp", "grp", None),
        P("fsdp", "grp", None),
        P("fsdp", "grp", None),
        P("fsdp", None),
        P("fsdp", None),
        P(),
        P("fsdp", "grp"),
        P("fsdp", "grp"),
        P("fsdp", "grp"),
        P("fsdp", None),
    )
    out_specs = (
        P("fsdp", "grp", None),
        P("fsdp", "grp", None),
        P("fsdp", "grp", None),
        P("fsdp", None),
        P("fsdp", None),
    )
    return jax.shard_map(local, mesh=mesh, in_specs=in_specs, out_specs=out_specs, check_vma=False)
```

```python
import functools
import math

import jax
import jax.numpy as jnp
import numpy as np
from jax import lax
from jax.experimental import pallas as pl
from jax.experimental.pallas import tpu as pltpu
from jax.sharding import PartitionSpec as P

MESH = pl.DeviceIdType.MESH
HBM = pl.BlockSpec(memory_space=pltpu.HBM)
SMEM = pl.BlockSpec(memory_space=pltpu.SMEM)
VMEM = pl.BlockSpec(memory_space=pltpu.VMEM)
VMEM_LIMIT = 60 * 1024 * 1024

WIDTH = 5120
HEAD = 128
ROWS = 160
HALF = 80
TOK = 128
PRO = 64
DEV = TOK + PRO
SCALE = 1.0 / math.sqrt(HEAD)
BASE = 1000000.0
bf16 = jnp.bfloat16
f32 = jnp.float32


def rotary_tables():
    frequency = np.float32(BASE) ** (-np.arange(64, dtype=np.float32) / np.float32(64))
    angles = np.arange(-128, 192, dtype=np.float32)[:, None] * frequency[None, :].astype(np.float32)
    angles = angles.astype(np.float32).astype(np.float64)
    cos, sin = np.cos(angles), np.sin(angles)
    return (
        np.concatenate([cos, cos], 1).astype(np.float32),
        np.concatenate([-sin, sin], 1).astype(np.float32),
    )


class Place:
    def __init__(self):
        g, f = lax.axis_index("grp"), lax.axis_index("fsdp")
        self.core, self.zh = lax.rem(g, 2), lax.div(g, 2)
        self.zl = lax.rem(f, 2)
        self.x = lax.rem(lax.div(f, 2), 4)
        self.y = lax.div(f, 8)
        self.z = self.zh * 2 + self.zl

    def at(self, y=None, x=None, z=None, core=None):
        y = self.y if y is None else y
        x = self.x if x is None else x
        z = self.z if z is None else z
        core = self.core if core is None else core
        return {"grp": lax.div(z, 2) * 2 + core, "fsdp": (y * 4 + x) * 2 + lax.rem(z, 2)}

    def ring_x(self):
        return self.x, self.at(x=lax.rem(self.x + 3, 4)), self.at(x=lax.rem(self.x + 1, 4))

    def ring_y(self):
        return self.y, self.at(y=lax.rem(self.y + 3, 4)), self.at(y=lax.rem(self.y + 1, 4))

    def ring_zh(self):
        return self.zh, self.at(z=lax.rem(self.z + 6, 8)), self.at(z=lax.rem(self.z + 2, 8))

    def near_z(self):
        return self.at(z=lax.rem(self.z + 7, 8)), self.at(z=lax.rem(self.z + 1, 8))

    def first_axis(self, kind):
        return self.x * (1 - kind) + self.y * kind

    def ring_of(self, kind):
        def moved(step):
            return self.at(x=lax.rem(self.x + step * (1 - kind), 4), y=lax.rem(self.y + step * kind, 4))

        return self.first_axis(kind), moved(3), moved(1)

    def partner(self):
        return self.at(core=1 - self.core)


def greet(devices):
    barrier = pltpu.get_barrier_semaphore()
    for device in devices:
        pl.semaphore_signal(barrier, inc=1, device_id=device, device_id_type=MESH)
    pl.semaphore_wait(barrier, len(devices))


class Links:
    def __init__(self, send, recv):
        self.send, self.recv, self.used, self.sent = send, recv, 0, []

    def take(self):
        self.used += 1
        return self.used - 1

    def copy(self, number, src, dst, device):
        return pltpu.make_async_remote_copy(
            src_ref=src,
            dst_ref=dst,
            send_sem=self.send.at[number],
            recv_sem=self.recv.at[number],
            device_id=device,
            device_id_type=MESH,
        )

    def start(self, number, src, dst, device):
        made = self.copy(number, src, dst, device)
        made.start()
        self.sent.append(made)

    def arrived(self, number, dst, device):
        self.copy(number, dst, dst, device).wait_recv()

    def drain(self):
        for made in self.sent:
            made.wait_send()
        self.sent = []


class Gather4:
    def __init__(self, links, ring, view, half, own=None):
        self.links, self.view, self.half = links, view, half
        self.me, self.minus, self.plus = ring
        self.own = view(self.me) if own is None else own
        self.n = [links.take() for _ in range(4)]

    def begin(self):
        self.links.start(self.n[0], self.own, self.view(self.me), self.plus)
        self.links.start(self.n[1], self.own, self.view(self.me), self.minus)

    def forward(self):
        left, right = lax.rem(self.me + 3, 4), lax.rem(self.me + 1, 4)
        self.links.arrived(self.n[0], self.view(left), self.plus)
        self.links.start(self.n[2], self.half(left, 0), self.half(left, 0), self.plus)
        self.links.arrived(self.n[1], self.view(right), self.minus)
        self.links.start(self.n[3], self.half(right, 1), self.half(right, 1), self.minus)

    def finish(self):
        across = lax.rem(self.me + 2, 4)
        self.links.arrived(self.n[2], self.half(across, 0), self.plus)
        self.links.arrived(self.n[3], self.half(across, 1), self.minus)


class Reduce4:
    def __init__(self, links, ring, part, slot, add):
        self.links, self.part, self.slot, self.add = links, part, slot, add
        self.me, self.minus, self.plus = ring
        self.n = [links.take() for _ in range(6)]

    def send_for(self, place):
        part, slot, n = self.part, self.slot, self.n
        block = lax.rem(self.me + place, 4)
        if place == 2:
            self.links.start(n[0], part(block, 0), slot(0), self.plus)
            self.links.start(n[1], part(block, 1), slot(1), self.minus)
        if place == 1:
            self.links.start(n[2], part(block, 1), slot(2), self.plus)
        if place == 3:
            self.links.start(n[3], part(block, 0), slot(3), self.minus)

    def begin(self):
        for place in (2, 1, 3):
            self.send_for(place)

    def mid(self):
        left, right = lax.rem(self.me + 3, 4), lax.rem(self.me + 1, 4)
        part, slot, n = self.part, self.slot, self.n
        self.links.arrived(n[0], slot(0), self.plus)
        self.add(slot(0), [slot(0), part(right, 0)])
        self.links.start(n[4], slot(0), slot(4), self.plus)
        self.links.arrived(n[1], slot(1), self.minus)
        self.add(slot(1), [slot(1), part(left, 1)])
        self.links.start(n[5], slot(1), slot(5), self.minus)

    def finish(self, out):
        part, slot, n = self.part, self.slot, self.n
        self.links.arrived(n[3], slot(3), self.minus)
        self.links.arrived(n[4], slot(4), self.plus)
        self.add(out(0), [part(self.me, 0), slot(3), slot(4)])
        self.links.arrived(n[2], slot(2), self.plus)
        self.links.arrived(n[5], slot(5), self.minus)
        self.add(out(1), [part(self.me, 1), slot(2), slot(5)])


def add_block(dst, terms):
    total = terms[0][...].astype(f32)
    for term in terms[1:]:
        total = total + term[...].astype(f32)
    dst[...] = total.astype(dst.dtype)


def add_blocks(dst, terms):
    def body(i, carry):
        total = terms[0][i].astype(f32)
        for term in terms[1:]:
            total = total + term[i].astype(f32)
        dst[i] = total.astype(dst.dtype)
        return carry

    lax.fori_loop(0, dst.shape[0], body, 0)


class Move4:
    def __init__(self, links, me, XT, XG, relay, zl):
        self.links, self.me, self.XT, self.XG, self.relay, self.zl = links, me, XT, XG, relay, zl
        self.place, self.minus, self.plus = me.ring_of(me.core)
        self.n = [links.take() for _ in range(9)]
        self.held = [pl.ds(0, 2), pl.ds(2, 2)]

    def from_place(self, steps):
        return lax.rem(self.place + steps, 4)

    def send(self, jobs):
        def start(kind):
            for n, steps, h, dst, device in jobs:
                c = self.from_place(steps)
                rows = pl.ds(0, 4) if h is None else self.held[h]
                src = self.XT.at[rows, c, self.zl] if kind == 0 else self.XT.at[c, rows, self.zl]
                self.links.copy(self.n[n], src, dst, device).start()

        pl.when(self.me.core == 0)(lambda: start(0))
        pl.when(self.me.core == 1)(lambda: start(1))
        for n, steps, h, dst, device in jobs:
            self.links.sent.append(self.links.copy(self.n[n], dst, dst, device))

    def begin(self):
        self.send([(0, 2, 0, self.relay.at[0], self.plus), (1, 2, 1, self.relay.at[1], self.minus)])

    def direct(self):
        mine = self.XG.at[self.me.core, self.place]
        self.send([(2, 1, None, mine, self.plus), (3, 3, None, mine, self.minus)])

    def forward(self):
        core, n = self.me.core, self.n
        self.links.arrived(n[0], self.relay.at[0], self.plus)
        self.links.start(n[4], self.relay.at[0], self.XG.at[core, self.from_place(3), self.held[0]], self.plus)
        self.links.arrived(n[1], self.relay.at[1], self.minus)
        self.links.start(n[5], self.relay.at[1], self.XG.at[core, self.from_place(1), self.held[1]], self.minus)

    def hand_over(self, steps):
        core, n, partner = self.me.core, self.n, self.me.partner()
        view = self.XG.at[core, self.from_place(steps)]
        if steps == 3:
            self.links.arrived(n[2], view, self.plus)
        elif steps == 1:
            self.links.arrived(n[3], view, self.minus)
        else:
            c = self.from_place(2)
            self.links.arrived(n[4], self.XG.at[core, c, self.held[0]], self.plus)
            self.links.arrived(n[5], self.XG.at[core, c, self.held[1]], self.minus)
        self.links.start(n[5 + steps], view, view, partner)

    def finish(self):
        other = 1 - self.me.core
        for steps in (1, 2, 3):
            c = lax.rem(self.me.first_axis(other) + steps, 4)
            self.links.arrived(self.n[5 + steps], self.XG.at[other, c], self.me.partner())


def remote_params(number, limit=None):
    return pltpu.CompilerParams(
        collective_id=number, has_side_effects=True, vmem_limit_bytes=limit or VMEM_LIMIT
    )


LOCAL = pltpu.CompilerParams(vmem_limit_bytes=VMEM_LIMIT)


GATHER_COPIES = 64


def gather_kernel(kw, vw, resp, prompt, q, og, sp, ss, sl, W, XP, QP, OP, SP, SS, SL, send, recv, local):
    me = Place()
    core, partner = me.core, me.partner()
    near_minus, near_plus = me.near_z()
    _, xm, xp = me.ring_x()
    _, ym, yp = me.ring_y()
    greet([xm, xp, ym, yp, near_minus, near_plus, partner])
    links = Links(send, recv)

    def columns(matrix, j):
        return matrix.at[:, pl.ds(pl.multiple_of((core * 2 + j) * HEAD, HEAD), HEAD)]

    own = [columns(kw, 0), columns(kw, 1), columns(vw, 0), columns(vw, 1)]
    x, y, zl = me.x, me.y, me.zl
    rows = lambda h: pl.ds(h * HALF, HALF)

    ax = Gather4(links, me.ring_x(), lambda c: W.at[0, y, c, zl], lambda c, h: W.at[0, y, c, zl, rows(h)], own[0])
    ay = Gather4(links, me.ring_y(), lambda c: W.at[0, c, :, zl], lambda c, h: W.at[0, c, :, zl, rows(h)])
    by = Gather4(links, me.ring_y(), lambda c: W.at[1, c, x, zl], lambda c, h: W.at[1, c, x, zl, rows(h)], own[1])
    bx = Gather4(links, me.ring_x(), lambda c: W.at[1, :, c, zl], lambda c, h: W.at[1, :, c, zl, rows(h)])
    cx = Gather4(links, me.ring_x(), lambda c: W.at[2, y, c], lambda c, h: W.at[2, y, c, h])
    cy = Gather4(links, me.ring_y(), lambda c: W.at[2, c], lambda c, h: W.at[2, c, :, h])
    dy = Gather4(links, me.ring_y(), lambda c: W.at[3, c, x], lambda c, h: W.at[3, c, x, h])
    dx = Gather4(links, me.ring_x(), lambda c: W.at[3, :, c], lambda c, h: W.at[3, :, c, h])

    zn = {}

    def z_view(t, place, which, h):
        if t == 0:
            return W.at[0, lax.rem(y + place, 4), :, which, rows(h)]
        if t == 1:
            return W.at[1, :, lax.rem(x + place, 4), which, rows(h)]
        return W.at[t, y, x, which, rows(h)]

    def z_begin(t, place, src=None):
        zn[t, place] = links.take(), links.take()
        for h, device in ((0, near_plus), (1, near_minus)):
            view = z_view(t, place, zl, h)
            links.start(zn[t, place][h], view if src is None else src(h), view, device)

    def z_finish(t, place):
        for h, device in ((0, near_plus), (1, near_minus)):
            links.arrived(zn[t, place][h], z_view(t, place, 1 - zl, h), device)

    ax.begin()
    by.begin()
    for t in (2, 3):
        matrix_half = lambda h, t=t: vw.at[rows(h), pl.ds(pl.multiple_of((core * 2 + t - 2) * HEAD, HEAD), HEAD)]
        z_begin(t, 0, matrix_half)

    locals_ = []

    def here(src, dst):
        made = pltpu.make_async_copy(src, dst, local.at[len(locals_)])
        made.start()
        locals_.append(made)

    for t in range(4):
        here(own[t], W.at[t, y, x, zl])
    swaps = []

    def swap(src, dst):
        number = links.take()
        links.start(number, src, dst, partner)
        swaps.append((number, dst))

    theirs = pl.ds(pl.multiple_of((1 - core) * 2048, 2048), 2048)
    swap(sp, SP)
    swap(ss, SS)
    swap(sl, SL)
    swap(resp.at[0], XP.at[pl.ds(0, TOK)])
    swap(prompt.at[0], XP.at[pl.ds(TOK, PRO)])
    swap(q.at[0, :, theirs], QP)
    swap(og.at[0, :, theirs], OP)

    ax.forward()
    by.forward()
    for made in locals_:
        made.wait()
    z_finish(2, 0)
    cx.begin()
    z_finish(3, 0)
    dy.begin()
    ax.finish()
    ay.begin()
    z_begin(0, 0)
    by.finish()
    bx.begin()
    z_begin(1, 0)
    cx.forward()
    dy.forward()
    cx.finish()
    cy.begin()
    dy.finish()
    dx.begin()
    ay.forward()
    z_begin(0, 3)
    z_begin(0, 1)
    bx.forward()
    z_begin(1, 3)
    z_begin(1, 1)
    ay.finish()
    z_begin(0, 2)
    bx.finish()
    z_begin(1, 2)
    cy.forward()
    dx.forward()
    for place in range(4):
        z_finish(0, place)
        z_finish(1, place)
    cy.finish()
    dx.finish()
    for number, landing in swaps:
        links.arrived(number, landing, partner)
    links.drain()
    assert links.used <= GATHER_COPIES


def gather(kw, vw, resp, prompt, q, og, sp, ss, sl):
    return pl.pallas_call(
        gather_kernel,
        out_shape=(
            jax.ShapeDtypeStruct((4, 4, 4, 2, ROWS, HEAD), bf16),
            jax.ShapeDtypeStruct((DEV, WIDTH), bf16),
            jax.ShapeDtypeStruct((TOK, 2048), bf16),
            jax.ShapeDtypeStruct((TOK, 2048), bf16),
            jax.ShapeDtypeStruct((1, 2), jnp.int32),
            jax.ShapeDtypeStruct((1, 2), jnp.int32),
            jax.ShapeDtypeStruct((1, 2), jnp.int32),
        ),
        in_specs=[HBM] * 9,
        out_specs=(HBM,) * 7,
        scratch_shapes=[
            pltpu.SemaphoreType.DMA((GATHER_COPIES,)),
            pltpu.SemaphoreType.DMA((GATHER_COPIES,)),
            pltpu.SemaphoreType.DMA((4,)),
        ],
        compiler_params=remote_params(1),
        name="gather",
    )(kw, vw, resp, prompt, q, og, sp, ss, sl)


K_STEP = 1024


def swap_halves(a):
    return pltpu.roll(a, 64, 1)


def tables_of(starts, cos, sin):
    start = starts[0, 1]
    late = pl.multiple_of(192 - start, 16)
    row = lax.broadcasted_iota(jnp.int32, (TOK, HEAD), 0)
    out = []
    for table in (cos, sin):
        first = table[pl.ds(192, TOK), :]
        second = table[pl.ds(late, TOK), :]
        out.append(jnp.concatenate([jnp.where(row < start, first, second), table[pl.ds(128, PRO), :]], 0))
    return out


def project_kernel(ss, SS, resp, prompt, XP, W, cos, sin, gain, XT, raw, keys, vals, pkv, turns, acc):
    step = pl.program_id(0)
    left = jnp.concatenate([resp[0], prompt[0], XP[...]], 0)
    right = jnp.concatenate([W[t] for t in range(4)], 1)
    part = jnp.dot(left, right, preferred_element_type=f32)
    XT[...] = left.T

    @pl.when(step == 0)
    def _():
        acc[...] = part

    @pl.when(step > 0)
    def _():
        acc[...] += part

    @pl.when(step == pl.num_programs(0) - 1)
    def _():
        for d in range(2):
            c, s = tables_of((ss, SS)[d], cos, sin)
            turns[d, 0], turns[d, 1] = c, s
            core = lax.rem(lax.axis_index("grp") + d, 2)
            for j in range(2):
                k = acc[pl.ds(d * DEV, DEV), pl.ds(j * HEAD, HEAD)]
                raw[j, d] = k
                square = jnp.mean(k * k, axis=1, keepdims=True)
                normed = k * lax.rsqrt(square + 1e-06) * gain[...]
                turned = (normed * c + swap_halves(normed) * s).astype(bf16)
                keys[j, d] = turned
                pkv[j, core] = turned[TOK:]
                v = acc[pl.ds(d * DEV, DEV), pl.ds((2 + j) * HEAD, HEAD)].astype(bf16)
                vals[j, d] = v
                pkv[2 + j, core] = v[TOK:]


def project(ss, SS, resp, prompt, XP, W, cos, sin, gain):
    return pl.pallas_call(
        project_kernel,
        out_shape=(
            jax.ShapeDtypeStruct((WIDTH, 2 * DEV), bf16),
            jax.ShapeDtypeStruct((2, 2, DEV, HEAD), f32),
            jax.ShapeDtypeStruct((2, 2, DEV, HEAD), bf16),
            jax.ShapeDtypeStruct((2, 2, DEV, HEAD), bf16),
            jax.ShapeDtypeStruct((4, 2, PRO, HEAD), bf16),
            jax.ShapeDtypeStruct((2, 2, DEV, HEAD), f32),
        ),
        grid=(WIDTH // K_STEP,),
        in_specs=[
            SMEM,
            SMEM,
            pl.BlockSpec((1, TOK, K_STEP), lambda i: (0, 0, i)),
            pl.BlockSpec((1, PRO, K_STEP), lambda i: (0, 0, i)),
            pl.BlockSpec((DEV, K_STEP), lambda i: (0, i)),
            pl.BlockSpec((4, K_STEP, HEAD), lambda i: (0, i, 0)),
            VMEM,
            VMEM,
            VMEM,
        ],
        out_specs=(pl.BlockSpec((K_STEP, 2 * DEV), lambda i: (i, 0)),) + (VMEM,) * 5,
        scratch_shapes=[pltpu.VMEM((2 * DEV, 512), f32)],
        compiler_params=LOCAL,
        name="project",
    )(ss, SS, resp, prompt, XP, W, cos, sin, gain)


ATTEND_COPIES = 40


def attend_kernel(
    sp, ss, sl, SP, SS, SL, owner, pkv, keys, vals, q, og, QP, OP, XT, W,
    QG, QO, RG, PS, XG, W2,
    everyone, queries, cots, rows_q, rows_g, probs, slopes, made_q, parts, PP, land, relay, send, recv, local,
):
    me = Place()
    core, partner = me.core, me.partner()
    ring = me.ring_zh()
    links = Links(send, recv)
    out = Gather4(links, ring, lambda c: everyone.at[c], lambda c, h: everyone.at[c, pl.ds(2 * h, 2)], pkv)
    columns = [Move4(links, me, XT, XG.at[z], relay.at[z], z) for z in range(2)]
    weights, swapped = links.take(), links.take()
    greet([ring[1], ring[2], columns[0].minus, columns[0].plus, partner])
    mine = pl.ds(pl.multiple_of(core * 2048, 2048), 2048)
    locals_ = []
    out.begin()
    for src, dst in (
        (pkv, everyone.at[me.zh]),
        (q.at[0, :, mine], rows_q.at[0]),
        (og.at[0, :, mine], rows_g.at[0]),
        (QP, rows_q.at[1]),
        (OP, rows_g.at[1]),
    ):
        made = pltpu.make_async_copy(src, dst, local.at[len(locals_)])
        made.start()
        locals_.append(made)
    columns[0].begin()
    columns[1].begin()
    links.start(weights, W, W2, partner)
    parts[...] = jnp.zeros_like(parts)
    out.forward()
    out.finish()
    for half in columns:
        half.forward()
    for half in columns:
        half.direct()
    for made in locals_:
        made.wait()

    def attend(i, carry):
        d, j = lax.div(i, 2), lax.rem(i, 2)

        def number(own, other, n):
            return jnp.where(d == 0, own[0, n], other[0, n])

        def slot_of(prompt):
            slot = 0
            for p in range(8):
                slot = slot + jnp.where(prompt == p, owner[0, p], 0)
            return slot

        slots = [slot_of(number(sp, SP, n)) for n in range(2)]
        start, lens = number(ss, SS, 1), [number(sl, SL, n) for n in range(2)]
        chosen = [[jnp.where(s == slot, 1.0, 0.0) for slot in range(8)] for s in slots]

        def pick(t, own):
            blocks = []
            for one in chosen:
                total = 0.0
                for slot in range(8):
                    total = total + everyone[slot // 2, t, slot % 2].astype(f32) * one[slot]
                blocks.append(total.astype(bf16))
            return jnp.concatenate(blocks + [own], 0)

        K = pick(j, keys[j, d, :TOK])
        V = pick(2 + j, vals[j, d, :TOK])

        key = lax.broadcasted_iota(jnp.int32, (2 * TOK, TOK), 0)
        row = lax.broadcasted_iota(jnp.int32, (2 * TOK, TOK), 1)
        late = row >= start
        first = jnp.where(late, start, 0)
        end = jnp.where(late, start + lens[1], lens[0])
        from_key = jnp.where(key < TOK, jnp.where(late, PRO, 0), first + TOK)
        to_key = jnp.where(key < TOK, jnp.where(late, TOK, PRO), jnp.minimum(end, row + 1) + TOK)
        bias = jnp.where((key >= from_key) & (key < to_key), 0.0, -1e30)
        bias = jnp.concatenate([bias, bias], 1)
        line = lax.broadcasted_iota(jnp.int32, (TOK, HEAD), 0)
        used = line < jnp.where(line >= start, start + lens[1], lens[0])

        def lanes(h):
            return pl.ds(pl.multiple_of(j * 1024 + h * HEAD, HEAD), HEAD)

        for h in range(8):
            block = pl.ds(h * TOK, TOK)
            queries[block, :] = rows_q[d, :, lanes(h)]
            cots[block, :] = jnp.where(used, rows_g[d, :, lanes(h)].astype(f32), 0.0).astype(bf16)
        for pair in range(4):
            block = pl.ds(pair * 2 * TOK, 2 * TOK)
            query, cot = queries[block, :], cots[block, :]
            scores = lax.dot_general(K, query, (((1,), (1,)), ((), ())), preferred_element_type=f32)
            scores = scores * SCALE + bias
            top = jnp.max(scores, axis=0, keepdims=True)
            exps = jnp.exp(scores - top)
            prob = exps * (1.0 / jnp.sum(exps, axis=0, keepdims=True))
            probs[:, block] = prob.astype(bf16)
            slope = lax.dot_general(V, cot, (((1,), (1,)), ((), ())), preferred_element_type=f32)
            slope = slope.astype(bf16).astype(f32)
            inner = jnp.sum(slope * prob, axis=0, keepdims=True)
            back = (prob * ((slope - inner) * SCALE)).astype(bf16)
            slopes[:, block] = back
            grad = lax.dot_general(
                back, K, (((0,), (0,)), ((), ())), preferred_element_type=f32
            ).astype(bf16)
            for n in range(2):
                made_q[d, :, lanes(2 * pair + n)] = grad[n * TOK : (n + 1) * TOK]
        dv = jnp.dot(probs[...], cots[...], preferred_element_type=f32)
        dk = jnp.dot(slopes[...], queries[...], preferred_element_type=f32)
        RG[j, d, 0] = dk[TOK:].astype(bf16)
        RG[j, d, 1] = dv[TOK:].astype(bf16)
        for slot in range(8):
            for t, grad in ((j, dk), (2 + j, dv)):
                parts[slot // 2, t, slot % 2] += (
                    grad[:PRO] * chosen[0][slot] + grad[PRO:TOK] * chosen[1][slot]
                )
        return carry

    lax.fori_loop(2, 4, attend, 0)
    links.start(swapped, made_q.at[1], QO, partner)
    lax.fori_loop(0, 2, attend, 0)
    PP[...] = parts[...].astype(bf16)

    def add(dst, terms):
        for i in range(2):
            for d in range(2):
                total = terms[0][i, d].astype(f32)
                for term in terms[1:]:
                    total = total + term[i, d].astype(f32)
                dst[i, d] = total.astype(dst.dtype)

    home = Reduce4(links, ring, lambda c, h: PP.at[c, pl.ds(2 * h, 2)], lambda i: land.at[i], add)
    home.begin()
    QG[...] = made_q[0]
    columns[0].hand_over(2)
    home.mid()
    for half, steps in ((1, 2), (0, 3), (0, 1), (1, 3), (1, 1)):
        columns[half].hand_over(steps)
    home.finish(lambda h: PS.at[pl.ds(2 * h, 2)])
    columns[0].finish()
    columns[1].finish()
    links.arrived(weights, W2, partner)
    links.arrived(swapped, QO, partner)
    links.drain()
    assert links.used <= ATTEND_COPIES


def attend(numbers, pkv, keys, vals, q, og, QP, OP, XT, W):
    return pl.pallas_call(
        attend_kernel,
        out_shape=(
            jax.ShapeDtypeStruct((TOK, 2048), bf16),
            jax.ShapeDtypeStruct((TOK, 2048), bf16),
            jax.ShapeDtypeStruct((2, 2, 2, TOK, HEAD), bf16),
            jax.ShapeDtypeStruct((4, 2, PRO, HEAD), f32),
            jax.ShapeDtypeStruct((2, 2, 4, 4, ROWS, 2 * DEV), bf16),
            jax.ShapeDtypeStruct((4, 4, 4, 2, ROWS, HEAD), bf16),
        ),
        in_specs=[SMEM] * 7 + [VMEM] * 3 + [HBM] * 6,
        out_specs=(VMEM, HBM, VMEM, VMEM, HBM, HBM),
        scratch_shapes=[
            pltpu.VMEM((4, 4, 2, PRO, HEAD), bf16),
            pltpu.VMEM((1024, HEAD), bf16),
            pltpu.VMEM((1024, HEAD), bf16),
            pltpu.VMEM((2, TOK, 2048), bf16),
            pltpu.VMEM((2, TOK, 2048), bf16),
            pltpu.VMEM((256, 1024), bf16),
            pltpu.VMEM((256, 1024), bf16),
            pltpu.VMEM((2, TOK, 2048), bf16),
            pltpu.VMEM((4, 4, 2, PRO, HEAD), f32),
            pltpu.VMEM((4, 4, 2, PRO, HEAD), bf16),
            pltpu.VMEM((6, 2, 2, PRO, HEAD), bf16),
            pltpu.VMEM((2, 2, 2, ROWS, 2 * DEV), bf16),
            pltpu.SemaphoreType.DMA((ATTEND_COPIES,)),
            pltpu.SemaphoreType.DMA((ATTEND_COPIES,)),
            pltpu.SemaphoreType.DMA((5,)),
        ],
        compiler_params=remote_params(2),
        name="attend",
    )(*numbers, pkv, keys, vals, q, og, QP, OP, XT, W)


SUM_COPIES = 80
I_STEP = 640


def sum_kernel(
    raw_, RG_, PS_, turns_, gain, XT, XG, W, W2,
    IG, WG,
    xg, w, w2, gg, theirs, acc, acc1, two, blocks, near, wg, raw, RG, PS, turns, send, recv, local,
):
    me = Place()
    partner = me.partner()
    ring_x, ring_y = me.ring_x(), me.ring_y()
    core, zl = me.core, me.zl
    place = (me.x, me.y)
    fetched = {}

    def fetch(name, src, dst):
        made = pltpu.make_async_copy(src, dst, local.at[sum(len(f) for f in fetched.values())])
        made.start()
        fetched.setdefault(name, []).append(made)

    for src, dst in ((raw_, raw), (RG_, RG), (PS_, PS), (turns_, turns)):
        fetch("small", src, dst)
    for z in range(2):
        fetch(0, XT.at[:, me.x, z], xg.at[z, 0, me.x])
        fetch(0, XT.at[me.y, :, z], xg.at[z, 1, me.y])
    for steps in (3, 1, 2):
        for kind in range(2):
            c = lax.rem(place[kind] + steps, 4)
            for z in range(2):
                fetch(steps, XG.at[z, kind, c], xg.at[z, kind, c])
    fetch("w", W, w)
    fetch("w", W2, w2)

    def ready(name):
        for made in fetched[name]:
            made.wait()

    greet([*ring_x[1:], *ring_y[1:], *[me.at(z=lax.rem(me.z + k, 8)) for k in range(1, 8)], partner])
    ready("small")
    links = Links(send, recv)

    for d in range(2):
        c, s = turns[d, 0], turns[d, 1]
        whose = core if d == 0 else 1 - core
        rows = pl.ds(d * DEV, DEV)
        for j in range(2):
            cot = jnp.concatenate([RG[j, d, 0].astype(f32), PS[j, whose]], 0)
            turned = (cot * c + swap_halves(cot * s)) * gain[...]
            k = raw[j, d]
            inverse = lax.rsqrt(jnp.mean(k * k, axis=1, keepdims=True) + 1e-06)
            along = jnp.mean(k * turned, axis=1, keepdims=True)
            back = inverse * turned - k * (inverse * inverse * inverse * along)
            gg[0, me.x, rows, pl.ds(j * HEAD, HEAD)] = back.astype(bf16)
            values = jnp.concatenate([RG[j, d, 1], PS[2 + j, whose].astype(bf16)], 0)
            gg[1, me.y, rows, pl.ds(j * HEAD, HEAD)] = values
    rounds = []
    for kind, ring in ((0, ring_x), (1, ring_y)):
        rounds.append(
            Gather4(
                links,
                ring,
                lambda c, kind=kind: gg.at[kind, c],
                lambda c, h, kind=kind: gg.at[kind, c, pl.ds(h * DEV, DEV)],
            )
        )
    for going in rounds:
        going.begin()
    crossed = links.take(), links.take()
    for kind in range(2):
        links.start(crossed[kind], gg.at[kind, place[kind], pl.ds(DEV, DEV)], theirs.at[kind], partner)

    def terms_of(steps):
        def body(i, carry):
            kind, z = lax.div(i, 2), lax.rem(i, 2)
            c = lax.rem(me.first_axis(kind) + steps, 4)
            left = jnp.concatenate([xg[z, kind, c, o] for o in range(4)], 0)
            swapped = 0 if steps == 0 else lax.rem(kind + core, 2)
            halves = [pl.ds(pl.multiple_of(h * DEV, DEV), DEV) for h in (swapped, 1 - swapped)]
            right = jnp.concatenate([gg[kind, c, h] for h in halves], 0)
            made = jnp.dot(left, right, preferred_element_type=f32)
            if steps != 0:
                made = made + acc[kind, z]
            if steps != 2:
                acc[kind, z] = made
            else:
                made = made.astype(bf16)
                for j in range(2):
                    for o in range(4):
                        acc1[2 * kind + j, o, z] = made[o * ROWS : (o + 1) * ROWS, j * HEAD : (j + 1) * HEAD]
            return carry

        lax.fori_loop(0, 4, body, 0)

    def input_part(i):
        rows = pl.ds(pl.multiple_of(i * I_STEP, I_STEP), I_STEP)
        total = 0.0
        mine = jnp.concatenate([gg[0, me.x, pl.ds(0, DEV)], gg[1, me.y, pl.ds(0, DEV)]], 1)
        others = jnp.concatenate([theirs[0], theirs[1]], 1)
        for left, right in ((mine, w), (others, w2)):
            both = jnp.concatenate([right[t, pl.ds(i * 4, 4)].reshape(I_STEP, HEAD) for t in range(4)], 1)
            total = total + lax.dot_general(
                left, both, (((1,), (1,)), ((), ())), preferred_element_type=f32
            )
        IG[:, rows] = total.astype(bf16)

    def input_parts(begin, end):
        def body(i, carry):
            input_part(i)
            return carry

        lax.fori_loop(begin, end, body, 0)

    second = []
    for t in range(4):
        second.append(
            Reduce4(
                links,
                ring_y if t < 2 else ring_x,
                lambda c, h, t=t: acc1.at[t, c, h],
                lambda i, t=t: two.at[t, i],
                add_block,
            )
        )

    class Wave:
        def __init__(self, n):
            self.n = n
            self.down = [links.take() for _ in range(7)]
            self.round = [links.take() for _ in range(3)]
            self.across = links.take()

        def sum_begin(self):
            for k in (4, 3, 5, 2, 6, 1, 7):
                z = lax.rem(me.z + k, 8)
                block = blocks.at[self.n, lax.rem(z, 2), lax.div(z, 2)]
                links.start(self.down[k - 1], block, near.at[self.n, k - 1], me.at(z=z))

        def sum_finish(self):
            for k in range(1, 8):
                links.arrived(self.down[k - 1], near.at[self.n, k - 1], partner)
            add_block(
                wg.at[core, self.n, me.zh],
                [blocks.at[self.n, zl, me.zh]] + [near.at[self.n, k] for k in range(7)],
            )

        def round_begin(self):
            mine = wg.at[core, self.n, me.zh]
            for k in (2, 1, 3):
                links.start(self.round[k - 1], mine, mine, me.at(z=lax.rem(me.z + 2 * k, 8)))

        def round_finish(self):
            for k in (1, 2, 3):
                links.arrived(self.round[k - 1], wg.at[core, self.n, lax.rem(me.zh + 4 - k, 4)], partner)

        def across_begin(self):
            links.start(self.across, wg.at[core, self.n], wg.at[core, self.n], partner)

        def across_finish(self):
            links.arrived(self.across, wg.at[1 - core, self.n], partner)

    waves = Wave(0), Wave(1)

    ready(0)
    terms_of(0)
    for going in rounds:
        going.forward()
    ready("w")
    for kind in range(2):
        links.arrived(crossed[kind], theirs.at[kind], partner)
    input_parts(0, 2)
    ready(3)
    terms_of(3)
    ready(1)
    terms_of(1)
    for going in rounds:
        going.finish()
    ready(2)
    terms_of(2)
    for t in (0, 2, 1, 3):
        second[t].begin()

    def settle(t):
        def add(dst, terms):
            total = terms[0][...].astype(f32)
            for term in terms[1:]:
                total = total + term[...].astype(f32)
            total = total.astype(bf16)
            for i in range(2):
                dst[2 * (t // 2) + i] = total[i * HALF : (i + 1) * HALF]

        second[t].add = add
        second[t].finish(lambda h: blocks.at[t % 2, h])

    input_parts(2, 3)
    second[0].mid()
    second[2].mid()
    second[1].mid()
    second[3].mid()
    input_parts(3, 4)
    settle(0)
    settle(2)
    waves[0].sum_begin()
    settle(1)
    settle(3)
    waves[1].sum_begin()
    input_parts(4, 6)
    waves[0].sum_finish()
    waves[0].round_begin()
    waves[1].sum_finish()
    waves[1].round_begin()
    input_parts(6, 8)
    waves[0].round_finish()
    waves[0].across_begin()
    waves[1].round_finish()
    waves[1].across_begin()
    waves[0].across_finish()
    waves[1].across_finish()
    WG[...] = wg[...]
    links.drain()
    assert links.used <= SUM_COPIES


def sum_terms(raw, RG, PS, turns, gain, XT, XG, W, W2):
    return pl.pallas_call(
        sum_kernel,
        out_shape=(
            jax.ShapeDtypeStruct((DEV, WIDTH), bf16),
            jax.ShapeDtypeStruct((2, 2, 4, HALF, HEAD), bf16),
        ),
        in_specs=[HBM] * 4 + [VMEM] + [HBM] * 4,
        out_specs=(VMEM, VMEM),
        scratch_shapes=[
            pltpu.VMEM((2, 2, 4, 4, ROWS, 2 * DEV), bf16),
            pltpu.VMEM((4, 32, ROWS, HEAD), bf16),
            pltpu.VMEM((4, 32, ROWS, HEAD), bf16),
            pltpu.VMEM((2, 4, 2 * DEV, 256), bf16),
            pltpu.VMEM((2, DEV, 256), bf16),
            pltpu.VMEM((2, 2, 4 * ROWS, 256), f32),
            pltpu.VMEM((4, 4, 2, ROWS, HEAD), bf16),
            pltpu.VMEM((4, 6, ROWS, HEAD), bf16),
            pltpu.VMEM((2, 2, 4, HALF, HEAD), bf16),
            pltpu.VMEM((2, 7, HALF, HEAD), bf16),
            pltpu.VMEM((2, 2, 4, HALF, HEAD), bf16),
            pltpu.VMEM((2, 2, DEV, HEAD), f32),
            pltpu.VMEM((2, 2, 2, TOK, HEAD), bf16),
            pltpu.VMEM((4, 2, PRO, HEAD), f32),
            pltpu.VMEM((2, 2, DEV, HEAD), f32),
            pltpu.SemaphoreType.DMA((SUM_COPIES,)),
            pltpu.SemaphoreType.DMA((SUM_COPIES,)),
            pltpu.SemaphoreType.DMA((24,)),
        ],
        compiler_params=remote_params(4),
        name="sum_terms",
    )(raw, RG, PS, turns, gain, XT, XG, W, W2)


def put_kernel(IG, WG, QG, QO, resp, prompt, qgrad, kout, vout):
    step = pl.program_id(0)
    core = lax.rem(lax.axis_index("grp"), 2)
    resp[0] = IG[:TOK]
    prompt[0] = IG[TOK:]

    @pl.when(step // 2 == core)
    def _():
        qgrad[0] = QG[...]

    @pl.when(step // 2 != core)
    def _():
        qgrad[0] = QO[...]

    @pl.when(step == 0)
    def _():
        for c in range(2):
            for j in range(2):
                lanes = pl.ds((2 * c + j) * HEAD, HEAD)
                kout[:, lanes] = WG[c, j, 0]
                vout[:, lanes] = WG[c, j, 1]


def put(IG, WG, QG, QO):
    part = WIDTH // 4
    return pl.pallas_call(
        put_kernel,
        out_shape=(
            jax.ShapeDtypeStruct((1, TOK, WIDTH), bf16),
            jax.ShapeDtypeStruct((1, PRO, WIDTH), bf16),
            jax.ShapeDtypeStruct((1, TOK, 4096), bf16),
            jax.ShapeDtypeStruct((ROWS, 512), bf16),
            jax.ShapeDtypeStruct((ROWS, 512), bf16),
        ),
        grid=(4,),
        in_specs=[
            pl.BlockSpec((DEV, part), lambda i: (0, i)),
            VMEM,
            pl.BlockSpec((TOK, 1024), lambda i: (0, lax.rem(i, 2))),
            pl.BlockSpec((TOK, 1024), lambda i: (0, lax.rem(i, 2))),
        ],
        out_specs=(
            pl.BlockSpec((1, TOK, part), lambda i: (0, 0, i)),
            pl.BlockSpec((1, PRO, part), lambda i: (0, 0, i)),
            pl.BlockSpec((1, TOK, 1024), lambda i: (0, 0, i)),
            VMEM,
            VMEM,
        ),
        compiler_params=LOCAL,
        name="put",
    )(IG, WG, QG, QO)


def local(
    queries, out_grad, resp_in, prompt_in, key_matrix, value_matrix, key_gain, seg_prompt, seg_start, seg_len, owner
):
    cos, sin = rotary_tables()
    gain = key_gain.reshape(1, HEAD)

    W, XP, QP, OP, SP, SS, SL = gather(
        key_matrix, value_matrix, resp_in, prompt_in, queries, out_grad, seg_prompt, seg_start, seg_len
    )
    flat = W.reshape(4, WIDTH, HEAD)
    XT, raw, keys, vals, pkv, turns = project(seg_start, SS, resp_in, prompt_in, XP, flat, cos, sin, gain)
    XT = XT.reshape(4, 4, 2, ROWS, 2 * DEV)
    numbers = (seg_prompt, seg_start, seg_len, SP, SS, SL, owner)
    QG, QO, RG, PS, XG, W2 = attend(numbers, pkv, keys, vals, queries, out_grad, QP, OP, XT, W)
    pieces = [a.reshape(4, 32, ROWS, HEAD) for a in (W, W2)]
    IG, WG = sum_terms(raw, RG, PS, turns, gain, XT, XG, *pieces)
    resp, prompt, qgrad, kout, vout = put(IG, WG.reshape(2, 2, 2, ROWS, HEAD), QG, QO)
    return qgrad, resp, prompt, kout, vout


def solution(mesh):
    in_specs = (
        P("fsdp", "grp", None),
        P("fsdp", "grp", None),
        P("fsdp", "grp", None),
        P("fsdp", "grp", None),
        P("fsdp", None),
        P("fsdp", None),
        P(),
        P("fsdp", "grp"),
        P("fsdp", "grp"),
        P("fsdp", "grp"),
        P("fsdp", None),
    )
    out_specs = (
        P("fsdp", "grp", None),
        P("fsdp", "grp", None),
        P("fsdp", "grp", None),
        P("fsdp", None),
        P("fsdp", None),
    )
    return jax.shard_map(local, mesh=mesh, in_specs=in_specs, out_specs=out_specs, check_vma=False)
```
